32 devices in a mesh: shard: 4 (over z), replica: 2 (over x), ctx: 4 (over y, core).
Axes of the slice: x: 2, y: 2, z: 4, core: 2. Of those that a mesh axis runs over, the one named last changes fastest.
Arguments:
- tokens: bfloat16 [64, 512, 1088], P(('shard', 'replica'), 'ctx'), may hold values from -6 to 6
- cotangent: bfloat16 [64, 512, 1088], P(('shard', 'replica'), 'ctx'), may hold values from -6 to 6
- block_order: int32 [4], replicated, may hold values from 0 to 3, each once
- ln1_gain: bfloat16 [1088], P('shard'), may hold values from 0.5 to 1.5
- ln1_bias: bfloat16 [1088], P('shard'), may hold values from -3 to 3
- qkv_weight: bfloat16 [1088, 3264], P('shard'), may hold values from -0.1875 to 0.1875
- q_bias: bfloat16 [1088], P('shard'), may hold values from -3 to 3
- v_bias: bfloat16 [1088], P('shard'), may hold values from -3 to 3
- out_weight: bfloat16 [1088, 1088], P('shard'), may hold values from -0.75 to 0.75
- out_bias: bfloat16 [1088], P('shard'), may hold values from -3 to 3
- ln2_gain: bfloat16 [1088], P('shard'), may hold values from 0.5 to 1.5
- ln2_bias: bfloat16 [1088], P('shard'), may hold values from -3 to 3
- fc_weight: bfloat16 [1088, 4352], P('shard'), may hold values from -0.1875 to 0.1875
- fc_bias: bfloat16 [4352], P('shard'), may hold values from -3 to 3
- proj_weight: bfloat16 [4352, 1088], P('shard'), may hold values from -0.09375 to 0.09375
- proj_bias: bfloat16 [1088], P('shard'), may hold values from -3 to 3
Outputs:
- layer_out: bfloat16 [64, 512, 1088], P(('shard', 'replica'), 'ctx')
- input_grad: float32 [64, 512, 1088], P(('shard', 'replica'), 'ctx')
- ln1_gain_grad: float32 [1088], P('shard')
- ln1_bias_grad: float32 [1088], P('shard')
- qkv_weight_grad: float32 [1088, 3264], P('shard')
- q_bias_grad: float32 [1088], P('shard')
- v_bias_grad: float32 [1088], P('shard')
- out_weight_grad: float32 [1088, 1088], P('shard')
- out_bias_grad: float32 [1088], P('shard')
- ln2_gain_grad: float32 [1088], P('shard')
- ln2_bias_grad: float32 [1088], P('shard')
- fc_weight_grad: float32 [1088, 4352], P('shard')
- fc_bias_grad: float32 [4352], P('shard')
- proj_weight_grad: float32 [4352, 1088], P('shard')
- proj_bias_grad: float32 [1088], P('shard')
The draws below stay inside these ranges and needn't reach their ends.
Inputs may be any that keep to these rules, and one draw needn't show every extreme that they name: A permutation: the index c of ctx holds positions block_order[c] * 128 to block_order[c] * 128 + 127 of each of its sequences.
All inputs are finite; a program needn't handle non-finite values.
Results may differ from the reference program's by a relative error of at most 0.018.
Values may be sent and summed in bfloat16 or wider, within the bound.
No kernel may reach another device: no remote copies, remote signals or barrier semaphores. Data moves between devices by JAX's collectives and lax.ppermute only.
A program may use at most 384 MiB of HBM per device.

```python
import math
import jax
import jax.numpy as jnp
from jax import lax

D = 1088
HEADS = 17
HEAD_DIM = 64
FF = 4352
LOCAL_LEN = 128
SEQLEN = 512
SEQS = 64
N_CTX = 4


def levels(stream_key, dims, cuts, low, largest):
    factor_of = 1.0
    for position, parts in cuts:
        draws = jax.random.uniform(jax.random.fold_in(jax.random.fold_in(stream_key, 6), position), (parts,), jnp.float32, low / len(cuts), largest / len(cuts))
        factor_of = factor_of * jnp.repeat(jnp.exp(draws), dims[position] // parts).reshape((-1,) + (1,) * (len(dims) - 1 - position))
    return factor_of


def normal_values(rng, dims, width, limit, split=(), kind=jnp.bfloat16):
    entries = jax.random.normal(rng, dims, jnp.float32) * width
    if len(split) > 0:
        entries = levels(rng, dims, split, -0.22, 0.18) * entries
    return jnp.clip(entries, min=-limit, max=limit).astype(kind)


def setup_inputs(seed: int = 0) -> dict:
    seeds = jax.random.split(jax.random.key(seed), 17)
    return {
        "tokens": normal_values(seeds[0], (SEQS, SEQLEN, D), 1.0, 6.0, ((0, 8), (1, 4))),
        "cotangent": normal_values(seeds[1], (SEQS, SEQLEN, D), 1.0, 6.0, ((0, 8), (1, 4))),
        "block_order": jax.random.permutation(seeds[2], N_CTX).astype(jnp.int32),
        "ln1_gain": jnp.clip(1.0 + 0.1 * jax.random.normal(seeds[3], (D,), jnp.float32), 0.5, 1.5).astype(jnp.bfloat16),
        "ln1_bias": normal_values(seeds[4], (D,), 0.3, 3.0, ((0, 4),)),
        "qkv_weight": normal_values(seeds[5], (D, 3 * D), D ** -0.5, 0.1875, ((0, 4),)),
        "q_bias": normal_values(seeds[6], (D,), 0.5, 3.0, ((0, 4),)),
        "v_bias": normal_values(seeds[7], (D,), 0.5, 3.0, ((0, 4),)),
        "out_weight": normal_values(seeds[8], (D, D), (D // 16) ** -0.5, 0.75, ((0, 4),)),
        "out_bias": normal_values(seeds[9], (D,), 0.5, 3.0, ((0, 4),)),
        "ln2_gain": jnp.clip(1.0 + 0.1 * jax.random.normal(seeds[10], (D,), jnp.float32), 0.5, 1.5).astype(jnp.bfloat16),
        "ln2_bias": normal_values(seeds[11], (D,), 0.3, 3.0, ((0, 4),)),
        "fc_weight": normal_values(seeds[12], (D, FF), D ** -0.5, 0.1875, ((0, 4),)),
        "fc_bias": normal_values(seeds[13], (FF,), 0.5, 3.0, ((0, 4),)),
        "proj_weight": normal_values(seeds[14], (FF, D), FF ** -0.5, 0.09375, ((0, 4),)),
        "proj_bias": normal_values(seeds[15], (D,), 0.5, 3.0, ((0, 4),)),
    }


@jax.custom_vjp
def low(v):
    return lax.optimization_barrier(v.astype(jnp.bfloat16)).astype(jnp.float32)

@jax.custom_vjp
def low_back(v):
    return v

def low_keep(v):
    return (low(v), None)

def low_pass(kept, grad):
    return (grad,)

def back_keep(v):
    return (v, None)

def back_low(kept, grad):
    return (low(grad),)
low.defvjp(low_keep, low_pass)
low_back.defvjp(back_keep, back_low)
epsilon = 1e-05
highest = lax.Precision.HIGHEST

def layer_norm(values, gain_vec, shift_vec):
    centred = values - lax.optimization_barrier(jnp.mean(values, axis=-1, keepdims=True))
    inverse = lax.rsqrt(lax.optimization_barrier(jnp.mean(centred * centred, axis=-1, keepdims=True)) + epsilon)
    return centred * inverse * gain_vec + shift_vec

def project(values, matrix):
    return jnp.einsum('std,de->ste', values, matrix, precision=highest)

def attend(triple, allowed):
    queries, key_rows, value_rows = triple
    raw_scores = low_back(jnp.einsum('sqhe,skhe->shqk', queries, key_rows, precision=highest))
    scores = jnp.where(allowed, raw_scores * HEAD_DIM ** (-0.5), -1e+30)
    attn_probs = low(jax.nn.softmax(scores, axis=-1))
    mixed_out = jnp.einsum('shqk,skhe->sqhe', attn_probs, value_rows, precision=highest)
    return low_back(low(mixed_out))

def forward(inputs, params, allowed):
    ln1_gain, ln1_bias, qkv_weight, q_bias, v_bias, out_weight, out_bias, ln2_gain, ln2_bias, fc_weight, fc_bias, proj_weight, proj_bias = params
    model_width = inputs.shape[-1]
    sequences = inputs.shape[0]
    length = inputs.shape[1]
    normed_one = low(layer_norm(inputs, ln1_gain, ln1_bias))
    joined = project(normed_one, qkv_weight)
    queries = low_back(low(joined[..., :model_width] + q_bias))
    key_rows = low_back(low(joined[..., model_width:2 * model_width]))
    value_rows = low_back(low(joined[..., 2 * model_width:] + v_bias))
    group_size = math.gcd(sequences, max(1, 4096 // length))

    def heads_view(tensor):
        return tensor.reshape(sequences // group_size, group_size, length, HEADS, HEAD_DIM)
    mixed_out = lax.map(jax.checkpoint(lambda triple: attend(triple, allowed)), (heads_view(queries), heads_view(key_rows), heads_view(value_rows)))
    mixed_out = mixed_out.reshape(sequences, length, model_width)
    branch = low_back(project(mixed_out, out_weight) + out_bias)
    middle = inputs + branch
    normed_two = low(layer_norm(middle, ln2_gain, ln2_bias))
    hidden = low_back(project(normed_two, fc_weight) + fc_bias)
    activated = low(jax.nn.gelu(hidden, approximate=True))
    return middle + low_back(project(activated, proj_weight) + proj_bias)

def reference(tokens, cotangent, block_order, ln1_gain, ln1_bias, qkv_weight, q_bias, v_bias, out_weight, out_bias, ln2_gain, ln2_bias, fc_weight, fc_bias, proj_weight, proj_bias):
    places = jnp.arange(SEQLEN, dtype=jnp.int32)
    positions = block_order[places // LOCAL_LEN] * LOCAL_LEN + places % LOCAL_LEN
    allowed = positions[None, :] <= positions[:, None]
    params = tuple((entry_array.astype(jnp.float32) for entry_array in (ln1_gain, ln1_bias, qkv_weight, q_bias, v_bias, out_weight, out_bias, ln2_gain, ln2_bias, fc_weight, fc_bias, proj_weight, proj_bias)))
    result, pullback = jax.vjp(lambda inputs, *weights: forward(inputs, weights, allowed), tokens.astype(jnp.float32), *params)
    gradients = pullback(cotangent.astype(jnp.float32))
    return (result.astype(jnp.bfloat16), gradients[0], gradients[1], gradients[2], gradients[3], gradients[4], gradients[5], gradients[6], gradients[7], gradients[8], gradients[9], gradients[10], gradients[11], gradients[12], gradients[13])
```

```python
import functools

import jax
import jax.numpy as jnp
from jax import lax
from jax.experimental import pallas as pl
from jax.experimental.pallas import tpu as pltpu
from jax.sharding import PartitionSpec as P

HEAD_DIM = 64
EPSILON = 1e-05
LANES = 128
UNITS = 8
VMEM_LIMIT = 48 * 1024 * 1024

BF16 = jnp.bfloat16
F32 = jnp.float32


def dot_nn(left, right):
    return lax.dot_general(left, right, (((1,), (0,)), ((), ())), preferred_element_type=F32)


def dot_nt(left, right):
    return lax.dot_general(left, right, (((1,), (1,)), ((), ())), preferred_element_type=F32)


def dot_tn(left, right):
    return lax.dot_general(left, right, (((0,), (0,)), ((), ())), preferred_element_type=F32)


def head_lanes(shape, which):
    lane = lax.broadcasted_iota(jnp.int32, shape, 1)
    return (lane < HEAD_DIM) if which == 0 else (lane >= HEAD_DIM)


def only_valid(values, width):
    if width % LANES == 0:
        return values
    lane = lax.broadcasted_iota(jnp.int32, values.shape, 1) + pl.program_id(1) * LANES
    return jnp.where(lane < width, values, jnp.zeros_like(values))


def causal(rows, columns):
    key_at = lax.broadcasted_iota(jnp.int32, (rows, columns), 0)
    query_at = lax.broadcasted_iota(jnp.int32, (rows, columns), 1)
    return key_at <= query_at


def attention_forward_kernel(tile, width, q_ref, k_ref, v_ref, o_ref, lse_ref):
    length = q_ref.shape[2]
    keys = only_valid(k_ref[0, 0], width)
    values_t = v_ref[0, 0].astype(F32).T.astype(BF16)
    diagonal = causal(tile, tile)
    for start in range(0, length, tile):
        queries = q_ref[0, 0, start : start + tile, :] * jnp.asarray(HEAD_DIM**-0.5, BF16)
        pieces = []
        for which in range(2):
            masked_q = jnp.where(head_lanes(queries.shape, which), queries, jnp.zeros_like(queries))
            scores = dot_nt(keys[: start + tile], masked_q)
            blocks = []
            if start > 0:
                blocks.append(scores[:start])
            blocks.append(jnp.where(diagonal, scores[start:], -1e30))
            top = functools.reduce(
                jnp.maximum, [jnp.max(block, axis=0, keepdims=True) for block in blocks]
            )
            weights = [jnp.exp(block - top) for block in blocks]
            total = sum(jnp.sum(weight, axis=0, keepdims=True) for weight in weights)
            low = jnp.concatenate([weight.astype(BF16) for weight in weights], axis=0)
            rows = values_t[which * HEAD_DIM : (which + 1) * HEAD_DIM, : start + tile]
            pieces.append(dot_nn(rows, low) * (1.0 / total))
            lse_ref[0, 0, which : which + 1, start : start + tile] = top + jnp.log(total)
        mixed_t = jnp.concatenate(pieces, axis=0)
        o_ref[0, start : start + tile, :] = mixed_t.T.astype(BF16)


def attention_backward_kernel(
    tile, width, q_ref, k_ref, v_ref, o_ref, do_ref, lse_ref, out_ref, dk_acc, dv_acc
):
    length = q_ref.shape[2]
    keys = only_valid(k_ref[0, 0], width)
    values = only_valid(v_ref[0, 0], width)
    keys_t = keys.astype(F32).T.astype(BF16)
    diagonal = causal(tile, tile)
    for start in range(0, length, tile):
        stop = start + tile
        queries = q_ref[0, 0, start:stop, :] * jnp.asarray(HEAD_DIM**-0.5, BF16)
        grads = do_ref[0, start:stop, :]
        product_t = (grads.astype(F32) * o_ref[0, start:stop, :].astype(F32)).T
        lanes = head_lanes(queries.shape, 0)
        key_lanes = head_lanes((stop, LANES), 0)
        dq_parts, dk_parts, dv_parts = [], [], []
        for which in range(2):
            mine = head_lanes(queries.shape, which)
            masked_q = jnp.where(mine, queries, jnp.zeros_like(queries))
            masked_g = jnp.where(mine, grads, jnp.zeros_like(grads))
            delta = jnp.sum(
                product_t[which * HEAD_DIM : (which + 1) * HEAD_DIM], axis=0, keepdims=True
            )
            lse = lse_ref[0, 0, which : which + 1, start:stop]
            scores = dot_nt(keys[:stop], masked_q)
            grad_weights = dot_nt(values[:stop], masked_g)
            weights = jnp.exp(scores - lse)
            if start > 0:
                weights = jnp.concatenate(
                    [weights[:start], jnp.where(diagonal, weights[start:], 0.0)], axis=0
                )
            else:
                weights = jnp.where(diagonal, weights, 0.0)
            low_scores = (weights * (grad_weights - delta)).astype(BF16)
            dv_parts.append(dot_nn(weights.astype(BF16), grads))
            dk_parts.append(dot_nn(low_scores, queries))
            dq_parts.append(
                dot_nn(keys_t[which * HEAD_DIM : (which + 1) * HEAD_DIM, :stop], low_scores)
            )
        dq_t = jnp.concatenate(dq_parts, axis=0) * (HEAD_DIM**-0.5)
        out_ref[0, 0, start:stop, :] = dq_t.T.astype(BF16)
        dk = jnp.where(key_lanes, dk_parts[0], dk_parts[1])
        dv = jnp.where(key_lanes, dv_parts[0], dv_parts[1])
        if start > 0:
            dk_acc[:start] += dk[:start]
            dv_acc[:start] += dv[:start]
        dk_acc[start:stop] = dk[start:]
        dv_acc[start:stop] = dv[start:]
    out_ref[1, 0] = dk_acc[...].astype(BF16)
    out_ref[2, 0] = dv_acc[...].astype(BF16)


def attention_tile(length):
    return 256 if length % 256 == 0 else 128


def attention_forward(joined):
    _, seqs, length, width = joined.shape
    pairs = pl.cdiv(width, LANES)
    spec = lambda which: pl.BlockSpec((1, 1, length, LANES), lambda s, h: (which, s, 0, h))
    return pl.pallas_call(
        functools.partial(attention_forward_kernel, attention_tile(length), width),
        grid=(seqs, pairs),
        in_specs=[spec(0), spec(1), spec(2)],
        out_specs=[
            pl.BlockSpec((1, length, LANES), lambda s, h: (s, 0, h)),
            pl.BlockSpec((1, 1, 8, length), lambda s, h: (s, h, 0, 0)),
        ],
        out_shape=[
            jax.ShapeDtypeStruct((seqs, length, width), BF16),
            jax.ShapeDtypeStruct((seqs, pairs, 8, length), F32),
        ],
        compiler_params=pltpu.CompilerParams(vmem_limit_bytes=VMEM_LIMIT),
        cost_estimate=pl.CostEstimate(
            flops=seqs * pairs * 8 * length * length * LANES,
            bytes_accessed=8 * seqs * length * width,
            transcendentals=seqs * pairs * 2 * length * length,
        ),
    )(joined, joined, joined)


def attention_backward(joined, mixed, grad_mixed, lse):
    _, seqs, length, width = joined.shape
    pairs = pl.cdiv(width, LANES)
    spec = lambda which: pl.BlockSpec((1, 1, length, LANES), lambda s, h: (which, s, 0, h))
    rows = pl.BlockSpec((1, length, LANES), lambda s, h: (s, 0, h))
    return pl.pallas_call(
        functools.partial(attention_backward_kernel, attention_tile(length), width),
        grid=(seqs, pairs),
        in_specs=[
            spec(0),
            spec(1),
            spec(2),
            rows,
            rows,
            pl.BlockSpec((1, 1, 8, length), lambda s, h: (s, h, 0, 0)),
        ],
        out_specs=pl.BlockSpec((3, 1, length, LANES), lambda s, h: (0, s, 0, h)),
        out_shape=jax.ShapeDtypeStruct((3, seqs, length, width), BF16),
        scratch_shapes=[pltpu.VMEM((length, LANES), F32), pltpu.VMEM((length, LANES), F32)],
        compiler_params=pltpu.CompilerParams(vmem_limit_bytes=VMEM_LIMIT),
        cost_estimate=pl.CostEstimate(
            flops=seqs * pairs * 20 * length * length * LANES,
            bytes_accessed=16 * seqs * length * width,
            transcendentals=seqs * pairs * 2 * length * length,
        ),
    )(joined, joined, joined, mixed, grad_mixed, lse)


def standardize(values):
    centred = values - jnp.mean(values, axis=-1, keepdims=True)
    inverse = lax.rsqrt(jnp.mean(centred * centred, axis=-1, keepdims=True) + EPSILON)
    return centred * inverse, inverse


def normalize_back(grad_out, standard, inverse, gain_vec):
    scaled = grad_out * gain_vec
    grad_in = inverse * (
        scaled
        - jnp.mean(scaled, axis=-1, keepdims=True)
        - standard * jnp.mean(scaled * standard, axis=-1, keepdims=True)
    )
    return grad_in, jnp.sum(grad_out * standard, axis=0), jnp.sum(grad_out, axis=0)


def swap_pairs(count, offset):
    return [(index, index ^ offset) for index in range(count)]


def to_sequences(values, block_order, count):
    seqs, local, width = values.shape
    own = lax.axis_index("ctx")
    share = seqs // count
    out = jnp.zeros((share, count, local, width), values.dtype)
    for offset in range(count):
        other = own ^ offset
        piece = lax.dynamic_slice_in_dim(values, other * share, share, axis=0)
        if offset:
            piece = lax.ppermute(piece, "ctx", swap_pairs(count, offset))
        place = lax.dynamic_index_in_dim(block_order, other, keepdims=False)
        out = lax.dynamic_update_slice(out, piece[:, None], (0, place, 0, 0))
    return out


def to_blocks(values, block_order, count):
    share, _, local, width = values.shape
    own = lax.axis_index("ctx")
    out = jnp.zeros((share * count, local, width), values.dtype)
    for offset in range(count):
        other = own ^ offset
        place = lax.dynamic_index_in_dim(block_order, other, keepdims=False)
        piece = lax.dynamic_slice(values, (0, place, 0, 0), (share, 1, local, width))[:, 0]
        if offset:
            piece = lax.ppermute(piece, "ctx", swap_pairs(count, offset))
        out = lax.dynamic_update_slice(out, piece, (other * share, 0, 0))
    return out


def per_device(
    tokens,
    cotangent,
    block_order,
    ln1_gain,
    ln1_bias,
    qkv_weight,
    q_bias,
    v_bias,
    out_weight,
    out_bias,
    ln2_gain,
    ln2_bias,
    fc_weight,
    fc_bias,
    proj_weight,
    proj_bias,
):
    seq_count, local_len, width = tokens.shape
    owned_rows = ln1_gain.shape[0]
    shards = width // owned_rows
    half = owned_rows // 2
    wide = fc_weight.shape[1] // width
    count = lax.axis_size("ctx")
    rows = seq_count * local_len
    spread = ("replica", "ctx")
    others = ()
    if UNITS % (lax.axis_size("replica") * count):
        spread, others = ("ctx",), ("replica",)
    parts = 1
    for axis in spread:
        parts *= lax.axis_size(axis)
    units = UNITS // parts
    everyone = ("shard",) + spread
    part = lax.axis_index(spread)

    def take_units(blocks):
        flat = blocks.reshape(UNITS * half, width)
        return lax.dynamic_slice_in_dim(flat, part * units * half, units * half, axis=0)

    def gather(chunk):
        full = lax.all_gather(chunk, everyone, axis=0, tiled=False)
        return full.reshape(shards, parts, chunk.shape[0], width)

    def to_matrices(gathered):
        blocks = gathered.reshape(shards, 4, owned_rows, width)
        return blocks.transpose(1, 0, 2, 3).reshape(4, width, width)

    vectors = jnp.concatenate(
        [ln1_gain, ln1_bias, q_bias, v_bias, out_bias, ln2_gain, ln2_bias, proj_bias, fc_bias]
    )
    vector_rows = vectors.shape[0] // width
    vector_pad = -vector_rows % 8
    vector_tile = jnp.pad(vectors.reshape(vector_rows, width), ((0, vector_pad), (0, 0)))
    blocks_a = jnp.concatenate(
        [qkv_weight.reshape(owned_rows, 3, width).transpose(1, 0, 2), out_weight[None]], axis=0
    )
    blocks_b = fc_weight.reshape(owned_rows, wide, width).transpose(1, 0, 2)
    chunk_a = jnp.concatenate([take_units(blocks_a), vector_tile], axis=0)
    gathered_a = gather(chunk_a)
    gathered_b = gather(take_units(blocks_b))
    gathered_c = gather(take_units(proj_weight.reshape(4, owned_rows, width)))
    used = units * half
    matrices_a = to_matrices(gathered_a[:, :, :used])
    w_qkv, w_out = matrices_a[:3], matrices_a[3]
    w_fc = to_matrices(gathered_b)
    w_proj = gathered_c.reshape(wide, width, width)
    vector_part = gathered_a[:, 0, used : used + vector_rows].reshape(shards, vector_rows * width)
    vector_part = vector_part.astype(F32)
    small = vector_part[:, : 8 * owned_rows].reshape(shards, 8, owned_rows)
    small = small.transpose(1, 0, 2).reshape(8, width)
    g_one, b_one, bias_q, bias_v, bias_out, g_two, b_two, bias_proj = [small[i] for i in range(8)]
    bias_fc = vector_part[:, 8 * owned_rows :].reshape(wide, 1, width)

    low_inputs = to_sequences(tokens, block_order, count).reshape(rows, width)
    low_grad_out = to_sequences(cotangent, block_order, count).reshape(rows, width)
    share = seq_count // count
    full_len = count * local_len

    inputs = low_inputs.astype(F32)
    standard_one, inverse_one = standardize(inputs)
    low_one = (standard_one * g_one + b_one).astype(BF16)
    joined = jnp.einsum("td,cdx->ctx", low_one, w_qkv, preferred_element_type=F32)
    bias_qkv = jnp.stack([bias_q, jnp.zeros_like(bias_q), bias_v])[:, None]
    joined = (joined + bias_qkv).astype(BF16).reshape(3, share, full_len, width)
    mixed, lse = attention_forward(joined)
    attended = mixed.reshape(rows, width)
    middle = inputs + (dot_nn(attended, w_out) + bias_out)
    standard_two, inverse_two = standardize(middle)
    low_two = (standard_two * g_two + b_two).astype(BF16)
    hidden = jnp.einsum("td,cdx->ctx", low_two, w_fc, preferred_element_type=F32) + bias_fc
    activated, gelu_pull = jax.vjp(lambda pre_act: jax.nn.gelu(pre_act, approximate=True), hidden)
    low_act = activated.astype(BF16)
    outputs = middle + (
        jnp.einsum("ctx,cxd->td", low_act, w_proj, preferred_element_type=F32) + bias_proj
    )
    layer_out = to_blocks(
        outputs.astype(BF16).reshape(share, count, local_len, width), block_order, count
    )

    def reduce_units(grads):
        owned = lax.psum_scatter(grads, everyone, scatter_dimension=0, tiled=False)
        if others:
            owned = lax.psum(owned, others)
        return lax.all_gather(owned, spread, axis=0, tiled=False)

    def from_matrices(grads):
        blocks = grads.reshape(4, shards, owned_rows, width).transpose(1, 0, 2, 3)
        return blocks.reshape(shards * parts, units * half, width)

    grad_out = low_grad_out.astype(F32)
    grad_proj = jnp.einsum("ctx,td->cxd", low_act, low_grad_out, preferred_element_type=F32)
    owned_proj = reduce_units(grad_proj.astype(BF16).reshape(shards * parts, units * half, width))
    grad_proj_bias = jnp.sum(grad_out, axis=0)
    grad_act = jnp.einsum("td,cxd->ctx", low_grad_out, w_proj, preferred_element_type=F32)
    grad_hidden = gelu_pull(grad_act)[0].astype(BF16)
    grad_fc = jnp.einsum("td,ctx->cdx", low_two, grad_hidden, preferred_element_type=F32)
    owned_fc = reduce_units(from_matrices(grad_fc.astype(BF16)))
    grad_fc_bias = jnp.sum(grad_hidden.astype(F32), axis=1)
    grad_two = jnp.einsum("ctx,cdx->td", grad_hidden, w_fc, preferred_element_type=F32)
    grad_norm_two, grad_g_two, grad_b_two = normalize_back(
        grad_two, standard_two, inverse_two, g_two
    )
    grad_middle = grad_out + grad_norm_two
    low_grad_middle = grad_middle.astype(BF16)
    grad_out_weight = dot_tn(attended, low_grad_middle)
    grad_out_bias = jnp.sum(low_grad_middle.astype(F32), axis=0)
    grad_attended = dot_nt(low_grad_middle, w_out).astype(BF16)
    grad_joined = attention_backward(
        joined, mixed, grad_attended.reshape(share, full_len, width), lse
    ).reshape(3, rows, width)
    grad_qkv = jnp.einsum("td,ctx->cdx", low_one, grad_joined, preferred_element_type=F32)
    grad_q_bias = jnp.sum(grad_joined[0].astype(F32), axis=0)
    grad_v_bias = jnp.sum(grad_joined[2].astype(F32), axis=0)
    grad_one = jnp.einsum("ctx,cdx->td", grad_joined, w_qkv, preferred_element_type=F32)
    grad_norm_one, grad_g_one, grad_b_one = normalize_back(
        grad_one, standard_one, inverse_one, g_one
    )
    input_grad = to_blocks(
        (grad_middle + grad_norm_one).astype(BF16).reshape(share, count, local_len, width),
        block_order,
        count,
    ).astype(F32)

    small_grads = jnp.stack(
        [
            grad_g_one,
            grad_b_one,
            grad_q_bias,
            grad_v_bias,
            grad_out_bias,
            grad_g_two,
            grad_b_two,
            grad_proj_bias,
        ]
    )
    vector_grads = jnp.concatenate(
        [
            small_grads.reshape(8, shards, owned_rows)
            .transpose(1, 0, 2)
            .reshape(shards, 8 * owned_rows),
            grad_fc_bias.reshape(shards, owned_rows * wide),
        ],
        axis=1,
    ).astype(BF16)
    vector_tile = vector_grads.reshape(shards, parts, 1, -1)
    piece = vector_tile.shape[-1]
    vector_tile = jnp.pad(vector_tile, ((0, 0), (0, 0), (0, 7), (0, width - piece)))
    grads_a = jnp.concatenate([grad_qkv.astype(BF16), grad_out_weight.astype(BF16)[None]], axis=0)
    grads_a = jnp.concatenate(
        [from_matrices(grads_a), vector_tile.reshape(shards * parts, 8, width)], axis=1
    )
    owned_a = reduce_units(grads_a)
    owned_vectors = owned_a[:, used, :piece].reshape(-1).astype(F32)
    vec = [owned_vectors[i * owned_rows : (i + 1) * owned_rows] for i in range(8)]
    fc_bias_grad = owned_vectors[8 * owned_rows :]
    owned_blocks = owned_a[:, :used].reshape(4, owned_rows, width)
    qkv_grad = owned_blocks[:3].transpose(1, 0, 2).reshape(owned_rows, 3 * width).astype(F32)
    fc_grad = (
        owned_fc.reshape(wide, owned_rows, width)
        .transpose(1, 0, 2)
        .reshape(owned_rows, wide * width)
        .astype(F32)
    )
    return (
        layer_out,
        input_grad,
        vec[0],
        vec[1],
        qkv_grad,
        vec[2],
        vec[3],
        owned_blocks[3].astype(F32),
        vec[4],
        vec[5],
        vec[6],
        fc_grad,
        fc_bias_grad,
        owned_proj.reshape(wide * owned_rows, width).astype(F32),
        vec[7],
    )


def solution(mesh):
    vector, matrix = P("shard"), P("shard", None)
    rows = P(("shard", "replica"), "ctx", None)
    weights = (
        vector,
        vector,
        matrix,
        vector,
        vector,
        matrix,
        vector,
        vector,
        vector,
        matrix,
        vector,
        matrix,
        vector,
    )
    return jax.shard_map(
        per_device,
        mesh=mesh,
        in_specs=(rows, rows, P()) + weights,
        out_specs=(rows, rows) + weights,
        check_vma=False,
    )
```

```python
import functools

import jax
import jax.numpy as jnp
from jax import lax
from jax.experimental import pallas as pl
from jax.experimental.layout import Layout, with_layout_constraint
from jax.experimental.pallas import tpu as pltpu
from jax.sharding import PartitionSpec as P

HEAD_DIM = 64
EPSILON = 1e-05
LANES = 128
VMEM_LIMIT = 48 * 1024 * 1024

BF16 = jnp.bfloat16
F32 = jnp.float32


def dot_nn(left, right):
    return lax.dot_general(left, right, (((1,), (0,)), ((), ())), preferred_element_type=F32)


def dot_nt(left, right):
    return lax.dot_general(left, right, (((1,), (1,)), ((), ())), preferred_element_type=F32)


def dot_tn(left, right):
    return lax.dot_general(left, right, (((0,), (0,)), ((), ())), preferred_element_type=F32)


def head_lanes(shape, which):
    lane = lax.broadcasted_iota(jnp.int32, shape, 1)
    return (lane < HEAD_DIM) if which == 0 else (lane >= HEAD_DIM)


def only_valid(values, width):
    if width % LANES == 0:
        return values
    lane = lax.broadcasted_iota(jnp.int32, values.shape, 1) + pl.program_id(1) * LANES
    return jnp.where(lane < width, values, jnp.zeros_like(values))


def sorted_rows(ref, lead, order_ref, first, last):
    return jnp.concatenate([ref[lead + (order_ref[i], 0)] for i in range(first, last)], axis=0)


def store_rows(ref, lead, order_ref, first, rows):
    local = ref.shape[-2]
    for i in range(rows.shape[0] // local):
        ref[lead + (order_ref[first + i], 0)] = rows[i * local : (i + 1) * local]


def causal(rows, columns):
    key_at = lax.broadcasted_iota(jnp.int32, (rows, columns), 0)
    query_at = lax.broadcasted_iota(jnp.int32, (rows, columns), 1)
    return key_at <= query_at


def attention_forward_kernel(blocks, width, order_ref, q_ref, k_ref, v_ref, o_ref, lse_ref):
    count, local = k_ref.shape[1], k_ref.shape[3]
    tile = blocks * local
    keys = only_valid(sorted_rows(k_ref, (0,), order_ref, 0, count), width)
    values_t = sorted_rows(v_ref, (0,), order_ref, 0, count).astype(F32).T.astype(BF16)
    diagonal = causal(tile, tile)
    for first in range(0, count, blocks):
        start, stop = first * local, (first + blocks) * local
        queries = sorted_rows(q_ref, (0,), order_ref, first, first + blocks)
        queries = queries * jnp.asarray(HEAD_DIM**-0.5, BF16)
        pieces = []
        for which in range(2):
            masked_q = jnp.where(head_lanes(queries.shape, which), queries, jnp.zeros_like(queries))
            scores = dot_nt(keys[:stop], masked_q)
            tiles = []
            if start > 0:
                tiles.append(scores[:start])
            tiles.append(jnp.where(diagonal, scores[start:], -1e30))
            top = functools.reduce(
                jnp.maximum, [jnp.max(block, axis=0, keepdims=True) for block in tiles]
            )
            weights = [jnp.exp(block - top) for block in tiles]
            total = sum(jnp.sum(weight, axis=0, keepdims=True) for weight in weights)
            low = jnp.concatenate([weight.astype(BF16) for weight in weights], axis=0)
            rows = values_t[which * HEAD_DIM : (which + 1) * HEAD_DIM, :stop]
            pieces.append(dot_nn(rows, low) * (1.0 / total))
            lse_ref[0, 0, which : which + 1, start:stop] = top + jnp.log(total)
        mixed_t = jnp.concatenate(pieces, axis=0)
        store_rows(o_ref, (), order_ref, first, mixed_t.T.astype(BF16))


def attention_backward_kernel(
    blocks,
    width,
    order_ref,
    q_ref,
    k_ref,
    v_ref,
    o_ref,
    do_ref,
    lse_ref,
    out_ref,
    dk_acc,
    dv_acc,
):
    count, local = k_ref.shape[1], k_ref.shape[3]
    tile = blocks * local
    keys = only_valid(sorted_rows(k_ref, (0,), order_ref, 0, count), width)
    values = only_valid(sorted_rows(v_ref, (0,), order_ref, 0, count), width)
    keys_t = keys.astype(F32).T.astype(BF16)
    diagonal = causal(tile, tile)
    for first in range(0, count, blocks):
        start, stop = first * local, (first + blocks) * local
        queries = sorted_rows(q_ref, (0,), order_ref, first, first + blocks)
        queries = queries * jnp.asarray(HEAD_DIM**-0.5, BF16)
        grads = sorted_rows(do_ref, (), order_ref, first, first + blocks)
        mixed = sorted_rows(o_ref, (), order_ref, first, first + blocks)
        product_t = (grads.astype(F32) * mixed.astype(F32)).T
        key_lanes = head_lanes((stop, LANES), 0)
        dq_parts, dk_parts, dv_parts = [], [], []
        for which in range(2):
            mine = head_lanes(queries.shape, which)
            masked_q = jnp.where(mine, queries, jnp.zeros_like(queries))
            masked_g = jnp.where(mine, grads, jnp.zeros_like(grads))
            delta = jnp.sum(
                product_t[which * HEAD_DIM : (which + 1) * HEAD_DIM], axis=0, keepdims=True
            )
            lse = lse_ref[0, 0, which : which + 1, start:stop]
            scores = dot_nt(keys[:stop], masked_q)
            grad_weights = dot_nt(values[:stop], masked_g)
            weights = jnp.exp(scores - lse)
            if start > 0:
                weights = jnp.concatenate(
                    [weights[:start], jnp.where(diagonal, weights[start:], 0.0)], axis=0
                )
            else:
                weights = jnp.where(diagonal, weights, 0.0)
            low_scores = (weights * (grad_weights - delta)).astype(BF16)
            dv_parts.append(dot_nn(weights.astype(BF16), grads))
            dk_parts.append(dot_nn(low_scores, queries))
            dq_parts.append(
                dot_nn(keys_t[which * HEAD_DIM : (which + 1) * HEAD_DIM, :stop], low_scores)
            )
        dq_t = jnp.concatenate(dq_parts, axis=0) * (HEAD_DIM**-0.5)
        store_rows(out_ref, (0,), order_ref, first, dq_t.T.astype(BF16))
        dk = jnp.where(key_lanes, dk_parts[0], dk_parts[1])
        dv = jnp.where(key_lanes, dv_parts[0], dv_parts[1])
        if start > 0:
            dk_acc[:start] += dk[:start]
            dv_acc[:start] += dv[:start]
        dk_acc[start:stop] = dk[start:]
        dv_acc[start:stop] = dv[start:]
    store_rows(out_ref, (1,), order_ref, 0, dk_acc[...].astype(BF16))
    store_rows(out_ref, (2,), order_ref, 0, dv_acc[...].astype(BF16))


def query_blocks(count):
    return 2 if count % 2 == 0 else 1


def attention_forward(joined, order):
    _, count, seqs, local, width = joined.shape
    length = count * local
    pairs = pl.cdiv(width, LANES)
    spec = lambda which: pl.BlockSpec(
        (1, count, 1, local, LANES), lambda s, h, order: (which, 0, s, 0, h)
    )
    return pl.pallas_call(
        functools.partial(attention_forward_kernel, query_blocks(count), width),
        grid_spec=pltpu.PrefetchScalarGridSpec(
            num_scalar_prefetch=1,
            grid=(seqs, pairs),
            in_specs=[spec(0), spec(1), spec(2)],
            out_specs=[
                pl.BlockSpec((count, 1, local, LANES), lambda s, h, order: (0, s, 0, h)),
                pl.BlockSpec((1, 1, 8, length), lambda s, h, order: (s, h, 0, 0)),
            ],
        ),
        out_shape=[
            jax.ShapeDtypeStruct((count, seqs, local, width), BF16),
            jax.ShapeDtypeStruct((seqs, pairs, 8, length), F32),
        ],
        compiler_params=pltpu.CompilerParams(vmem_limit_bytes=VMEM_LIMIT),
        cost_estimate=pl.CostEstimate(
            flops=seqs * pairs * 16 * length * length * LANES,
            bytes_accessed=8 * seqs * length * width,
            transcendentals=seqs * pairs * 2 * length * length,
        ),
    )(order, joined, joined, joined)


def attention_backward(joined, mixed, grad_mixed, lse, order):
    _, count, seqs, local, width = joined.shape
    length = count * local
    pairs = pl.cdiv(width, LANES)
    spec = lambda which: pl.BlockSpec(
        (1, count, 1, local, LANES), lambda s, h, order: (which, 0, s, 0, h)
    )
    rows = pl.BlockSpec((count, 1, local, LANES), lambda s, h, order: (0, s, 0, h))
    return pl.pallas_call(
        functools.partial(attention_backward_kernel, query_blocks(count), width),
        grid_spec=pltpu.PrefetchScalarGridSpec(
            num_scalar_prefetch=1,
            grid=(seqs, pairs),
            in_specs=[
                spec(0),
                spec(1),
                spec(2),
                rows,
                rows,
                pl.BlockSpec((1, 1, 8, length), lambda s, h, order: (s, h, 0, 0)),
            ],
            out_specs=pl.BlockSpec(
                (3, count, 1, local, LANES), lambda s, h, order: (0, 0, s, 0, h)
            ),
            scratch_shapes=[pltpu.VMEM((length, LANES), F32), pltpu.VMEM((length, LANES), F32)],
        ),
        out_shape=jax.ShapeDtypeStruct(joined.shape, BF16),
        compiler_params=pltpu.CompilerParams(vmem_limit_bytes=VMEM_LIMIT),
        cost_estimate=pl.CostEstimate(
            flops=seqs * pairs * 20 * length * length * LANES,
            bytes_accessed=16 * seqs * length * width,
            transcendentals=seqs * pairs * 2 * length * length,
        ),
    )(order, joined, joined, joined, mixed, grad_mixed, lse)


def standardize(values):
    centred = values - jnp.mean(values, axis=-1, keepdims=True)
    inverse = lax.rsqrt(jnp.mean(centred * centred, axis=-1, keepdims=True) + EPSILON)
    return centred * inverse, inverse


def normalize_back(grad_out, standard, inverse, gain_vec):
    scaled = grad_out * gain_vec
    grad_in = inverse * (
        scaled
        - jnp.mean(scaled, axis=-1, keepdims=True)
        - standard * jnp.mean(scaled * standard, axis=-1, keepdims=True)
    )
    return grad_in, jnp.sum(grad_out * standard, axis=0), jnp.sum(grad_out, axis=0)


def row_major(values):
    return with_layout_constraint(values, Layout(major_to_minor=tuple(range(values.ndim))))


def swap(values, axis, offset):
    count = lax.axis_size(axis)
    return lax.ppermute(values, axis, [(index, index ^ offset) for index in range(count)])


def pick(bit, on_zero, on_one):
    return jnp.where(bit == 0, on_zero, on_one)


def to_sequences(values, count):
    seqs, local, width = values.shape
    own = lax.axis_index("ctx")
    parts = values.reshape(count, seqs // count, local, width)
    pieces = []
    for offset in range(count):
        piece = lax.dynamic_index_in_dim(parts, own ^ offset, keepdims=False)
        pieces.append(swap(piece, "ctx", offset) if offset else piece)
    return row_major(jnp.stack(pieces))


def to_blocks(values, kind):
    count, share, local, width = values.shape
    own = lax.axis_index("ctx")
    out = row_major(jnp.zeros((count, share, local, width), kind))
    for offset in range(count):
        piece = swap(values[offset], "ctx", offset) if offset else values[0]
        out = lax.dynamic_update_index_in_dim(out, piece.astype(kind), own ^ offset, 0)
    return row_major(out).reshape(count * share, local, width)


class Windows:
    def __init__(self, owned_rows):
        tiles = owned_rows // 16
        self.start = tiles // 2 * 16
        self.size = owned_rows - self.start
        ctx = lax.axis_index("ctx")
        self.core = ctx % 2
        self.y = ctx // 2
        self.x = lax.axis_index("replica")

    def rows(self, values):
        return pick(
            self.core, values[..., : self.size, :], values[..., self.start :, :]
        )

    def other_rows(self, values):
        return pick(
            self.core, values[..., self.start :, :], values[..., : self.size, :]
        )

    def block(self, blocks):
        return pick(
            self.x,
            pick(self.y, blocks[0], blocks[1]),
            pick(self.y, blocks[2], blocks[3]),
        )


def assemble_kernel(groups, start, size, here_ref, *refs):
    arrays, out_ref, sem = refs[:-2], refs[-2], refs[-1]
    x, y, core = here_ref[0], here_ref[1], here_ref[2]
    for turn in range(2):
        copies = []
        row = pl.multiple_of((core ^ turn) * start, 16)
        for (places, first), ref in zip(groups, arrays[turn * len(groups) :]):
            for i, (dx, dy) in enumerate(places):
                for s in range(ref.shape[1]):
                    copies.append(
                        pltpu.make_async_copy(
                            ref.at[i, s, pl.ds(0, size), :],
                            out_ref.at[
                                2 * (x ^ dx) + (y ^ dy), first + s, pl.ds(row, size), :
                            ],
                            sem.at[len(copies)],
                        )
                    )
        for copy in copies:
            copy.start()
        for copy in copies:
            copy.wait()


def assemble(win, groups, own, other, owned_rows, shards):
    width = own[0].shape[-1]
    here = jnp.stack([win.x, win.y, win.core]).astype(jnp.int32)
    most = sum(len(places) * array.shape[1] for (places, _), array in zip(groups, own))
    return pl.pallas_call(
        functools.partial(assemble_kernel, groups, win.start, win.size),
        in_specs=[pl.BlockSpec(memory_space=pltpu.SMEM)]
        + [pl.BlockSpec(memory_space=pl.ANY)] * (2 * len(groups)),
        out_specs=pl.BlockSpec(memory_space=pl.ANY),
        out_shape=jax.ShapeDtypeStruct((4, shards, owned_rows, width), BF16),
        scratch_shapes=[pltpu.SemaphoreType.DMA((most,))],
        cost_estimate=pl.CostEstimate(
            flops=0, bytes_accessed=16 * shards * owned_rows * width, transcendentals=0
        ),
    )(here, *own, *other)


def spread_weights(win, mine, owned_rows):
    shards = mine.shape[0]
    if shards % 2:
        first = jnp.stack([mine, swap(mine, "replica", 1)])
        own = [first, swap(first, "ctx", 2)]
        groups = ((((0, 0), (1, 0)), 0), (((0, 1), (1, 1)), 0))
    else:
        half = shards // 2
        low, high = mine[:half], mine[half:]
        first = jnp.stack([low, swap(low, "replica", 1)])
        second = jnp.stack([high, swap(high, "ctx", 2)])
        own = [first, second, swap(first, "ctx", 2), swap(second, "replica", 1)]
        groups = (
            (((0, 0), (1, 0)), 0),
            (((0, 0), (0, 1)), half),
            (((0, 1), (1, 1)), 0),
            (((1, 0), (1, 1)), half),
        )
    other = [swap(array, "ctx", 1) for array in own]
    return assemble(win, groups, own, other, owned_rows, shards)


def add_pair(kept, received):
    return (kept.astype(F32) + received.astype(F32)).astype(BF16)


def reduce_blocks(win, grads):
    shards = grads.shape[1]
    half = shards // 2
    both = add_pair(win.rows(grads), swap(win.other_rows(grads), "ctx", 1))
    x_kept = pick(win.x, both[:2, :half], both[2:, :half])
    x_sent = pick(win.x, both[2:, :half], both[:2, :half])
    y_kept = pick(win.y, both[0::2, half:], both[1::2, half:])
    y_sent = pick(win.y, both[1::2, half:], both[0::2, half:])
    low = add_pair(x_kept, swap(x_sent, "replica", 1))
    high = add_pair(y_kept, swap(y_sent, "ctx", 2))
    low_sum = add_pair(
        pick(win.y, low[0], low[1]), swap(pick(win.y, low[1], low[0]), "ctx", 2)
    )
    high_sum = add_pair(
        pick(win.x, high[0], high[1]), swap(pick(win.x, high[1], high[0]), "replica", 1)
    )
    return jnp.concatenate([low_sum, high_sum], axis=0)


def reduce_vectors(values):
    values = add_pair(values, swap(values, "ctx", 1))
    values = add_pair(values, swap(values, "replica", 1))
    return add_pair(values, swap(values, "ctx", 2))


def per_device(
    tokens,
    cotangent,
    block_order,
    ln1_gain,
    ln1_bias,
    qkv_weight,
    q_bias,
    v_bias,
    out_weight,
    out_bias,
    ln2_gain,
    ln2_bias,
    fc_weight,
    fc_bias,
    proj_weight,
    proj_bias,
):
    seq_count, local_len, width = tokens.shape
    owned_rows = ln1_gain.shape[0]
    shards = width // owned_rows
    wide = fc_weight.shape[1] // width
    count = lax.axis_size("ctx")
    rows = seq_count * local_len
    pairwise = lax.axis_size("replica") == 2 and count == 4 and shards % 2 == 0
    win = Windows(owned_rows)

    vectors = jnp.concatenate(
        [ln1_gain, ln1_bias, q_bias, v_bias, out_bias, ln2_gain, ln2_bias, proj_bias, fc_bias]
    )
    vector_rows = vectors.shape[0] // width
    vector_tile = jnp.pad(vectors.reshape(vector_rows, width), ((0, -vector_rows % 16), (0, 0)))
    column = lambda values, i: values[:, i * width : (i + 1) * width]
    blocks_a = [column(qkv_weight, i) for i in range(3)] + [out_weight]
    blocks_b = [column(fc_weight, i) for i in range(wide)]
    blocks_c = [proj_weight[i * owned_rows : (i + 1) * owned_rows] for i in range(wide)]

    def gather_z(values):
        return lax.all_gather(values, "shard", axis=0, tiled=False)

    if pairwise:
        mine = [win.rows(win.block(blocks)) for blocks in (blocks_a, blocks_b, blocks_c)]
        part_a = gather_z(jnp.concatenate([mine[0], vector_tile], axis=0))
        part_b, part_c = gather_z(mine[1]), gather_z(mine[2])
        vector_part = part_a[:, win.size : win.size + vector_rows]
        full_a = spread_weights(win, part_a[:, : win.size], owned_rows)
        full_b = spread_weights(win, part_b, owned_rows)
        full_c = spread_weights(win, part_c, owned_rows)
    else:
        vector_part = gather_z(vector_tile)[:, :vector_rows]
        full_a, full_b, full_c = [
            gather_z(jnp.stack(blocks)).transpose(1, 0, 2, 3)
            for blocks in (blocks_a, blocks_b, blocks_c)
        ]
    matrices_a = full_a.reshape(4, width, width)
    w_qkv, w_out = matrices_a[:3], matrices_a[3]
    w_fc = full_b.reshape(wide, width, width)
    w_proj = full_c.transpose(1, 0, 2, 3).reshape(wide, width, width)
    vector_part = vector_part.reshape(shards, vector_rows * width).astype(F32)
    small = vector_part[:, : 8 * owned_rows].reshape(shards, 8, owned_rows)
    small = small.transpose(1, 0, 2).reshape(8, width)
    g_one, b_one, bias_q, bias_v, bias_out, g_two, b_two, bias_proj = [small[i] for i in range(8)]
    bias_fc = vector_part[:, 8 * owned_rows :].reshape(wide, 1, width)

    low_inputs = to_sequences(tokens, count).reshape(rows, width)
    low_grad_out = to_sequences(cotangent, count).reshape(rows, width)
    share = seq_count // count
    blocked = (count, share, local_len, width)
    index = jnp.arange(count, dtype=jnp.int32)
    held_by = jnp.sum(jnp.where(block_order[None, :] == index[:, None], index[None, :], 0), axis=1)
    order = (held_by ^ lax.axis_index("ctx")).astype(jnp.int32)

    inputs = low_inputs.astype(F32)
    standard_one, inverse_one = standardize(inputs)
    low_one = (standard_one * g_one + b_one).astype(BF16)
    joined = jnp.einsum("td,cdx->ctx", low_one, w_qkv, preferred_element_type=F32)
    bias_qkv = jnp.stack([bias_q, jnp.zeros_like(bias_q), bias_v])[:, None]
    joined = (joined + bias_qkv).astype(BF16).reshape((3,) + blocked)
    mixed, lse = attention_forward(joined, order)
    attended = mixed.reshape(rows, width)
    middle = inputs + (dot_nn(attended, w_out) + bias_out)
    standard_two, inverse_two = standardize(middle)
    low_two = (standard_two * g_two + b_two).astype(BF16)
    hidden = jnp.einsum("td,cdx->ctx", low_two, w_fc, preferred_element_type=F32) + bias_fc
    activated, gelu_pull = jax.vjp(lambda pre_act: jax.nn.gelu(pre_act, approximate=True), hidden)
    low_act = activated.astype(BF16)
    outputs = middle + (
        jnp.einsum("ctx,cxd->td", low_act, w_proj, preferred_element_type=F32) + bias_proj
    )
    layer_out = to_blocks(row_major(outputs.astype(BF16).reshape(blocked)), BF16)

    def reduce_units(grads, extra=None):
        if pairwise:
            sums = reduce_blocks(win, grads)
            if extra is not None:
                sums = jnp.concatenate([sums, reduce_vectors(extra)], axis=1)
            sums = lax.psum_scatter(sums, "shard", scatter_dimension=0, tiled=False)
            full = spread_weights(win, sums[None, : win.size], owned_rows)[:, 0]
            return full, sums[win.size :]
        rest = ("replica", "ctx")
        full = lax.psum_scatter(grads, "shard", scatter_dimension=1, tiled=False)
        full = lax.psum(full, rest)
        if extra is not None:
            extra = lax.psum_scatter(extra, "shard", scatter_dimension=0, tiled=False)
            extra = lax.psum(extra, rest)
        return full, extra

    def by_shard(grads):
        return grads.astype(BF16).reshape(4, shards, owned_rows, width)

    grad_out = low_grad_out.astype(F32)
    grad_proj = jnp.einsum("ctx,td->cxd", low_act, low_grad_out, preferred_element_type=F32)
    owned_proj, _ = reduce_units(by_shard(grad_proj).transpose(1, 0, 2, 3))
    grad_proj_bias = jnp.sum(grad_out, axis=0)
    grad_act = jnp.einsum("td,cxd->ctx", low_grad_out, w_proj, preferred_element_type=F32)
    grad_hidden = gelu_pull(grad_act)[0].astype(BF16)
    grad_fc = jnp.einsum("td,ctx->cdx", low_two, grad_hidden, preferred_element_type=F32)
    owned_fc, _ = reduce_units(by_shard(grad_fc))
    grad_fc_bias = jnp.sum(grad_hidden.astype(F32), axis=1)
    grad_two = jnp.einsum("ctx,cdx->td", grad_hidden, w_fc, preferred_element_type=F32)
    grad_norm_two, grad_g_two, grad_b_two = normalize_back(
        grad_two, standard_two, inverse_two, g_two
    )
    grad_middle = grad_out + grad_norm_two
    low_grad_middle = grad_middle.astype(BF16)
    grad_out_weight = dot_tn(attended, low_grad_middle)
    grad_out_bias = jnp.sum(low_grad_middle.astype(F32), axis=0)
    grad_attended = dot_nt(low_grad_middle, w_out).astype(BF16)
    grad_joined = attention_backward(
        joined, mixed, grad_attended.reshape(blocked), lse, order
    ).reshape(3, rows, width)
    grad_qkv = jnp.einsum("td,ctx->cdx", low_one, grad_joined, preferred_element_type=F32)
    grads_a = jnp.concatenate([grad_qkv.astype(BF16), grad_out_weight.astype(BF16)[None]], axis=0)
    grad_q_bias = jnp.sum(grad_joined[0].astype(F32), axis=0)
    grad_v_bias = jnp.sum(grad_joined[2].astype(F32), axis=0)
    grad_one = jnp.einsum("ctx,cdx->td", grad_joined, w_qkv, preferred_element_type=F32)
    grad_norm_one, grad_g_one, grad_b_one = normalize_back(
        grad_one, standard_one, inverse_one, g_one
    )
    input_grad = to_blocks(
        row_major((grad_middle + grad_norm_one).astype(BF16).reshape(blocked)), F32
    )

    small_grads = jnp.stack(
        [
            grad_g_one,
            grad_b_one,
            grad_q_bias,
            grad_v_bias,
            grad_out_bias,
            grad_g_two,
            grad_b_two,
            grad_proj_bias,
        ]
    )
    vector_grads = jnp.concatenate(
        [
            small_grads.reshape(8, shards, owned_rows)
            .transpose(1, 0, 2)
            .reshape(shards, 8 * owned_rows),
            grad_fc_bias.reshape(shards, owned_rows * wide),
        ],
        axis=1,
    ).astype(BF16)
    vector_grads = jnp.pad(
        vector_grads.reshape(shards, vector_rows, width),
        ((0, 0), (0, -vector_rows % 16), (0, 0)),
    )
    owned_a, owned_vectors = reduce_units(by_shard(grads_a), vector_grads)
    owned_vectors = owned_vectors[:vector_rows].reshape(-1).astype(F32)
    vec = [owned_vectors[i * owned_rows : (i + 1) * owned_rows] for i in range(8)]
    qkv_grad = jnp.concatenate([owned_a[i] for i in range(3)], axis=1).astype(F32)
    fc_grad = jnp.concatenate([owned_fc[i] for i in range(wide)], axis=1).astype(F32)
    return (
        layer_out,
        input_grad,
        vec[0],
        vec[1],
        qkv_grad,
        vec[2],
        vec[3],
        owned_a[3].astype(F32),
        vec[4],
        vec[5],
        vec[6],
        fc_grad,
        owned_vectors[8 * owned_rows :],
        owned_proj.reshape(wide * owned_rows, width).astype(F32),
        vec[7],
    )


def solution(mesh):
    vector, matrix = P("shard"), P("shard", None)
    rows = P(("shard", "replica"), "ctx", None)
    weights = (
        vector,
        vector,
        matrix,
        vector,
        vector,
        matrix,
        vector,
        vector,
        vector,
        matrix,
        vector,
        matrix,
        vector,
    )
    return jax.shard_map(
        per_device,
        mesh=mesh,
        in_specs=(rows, rows, P()) + weights,
        out_specs=(rows, rows) + weights,
        check_vma=False,
    )
```

```python
import functools

import jax
import jax.numpy as jnp
from jax import lax
from jax.experimental import pallas as pl
from jax.experimental.layout import Layout, with_layout_constraint
from jax.experimental.pallas import tpu as pltpu
from jax.sharding import PartitionSpec as P

HEAD_DIM = 64
EPSILON = 1e-05
LANES = 128
VMEM_LIMIT = 56 * 1024 * 1024

BF16 = jnp.bfloat16
F32 = jnp.float32


def dot_nn(left, right):
    return lax.dot_general(left, right, (((1,), (0,)), ((), ())), preferred_element_type=F32)


def dot_nt(left, right):
    return lax.dot_general(left, right, (((1,), (1,)), ((), ())), preferred_element_type=F32)


def dot_tn(left, right):
    return lax.dot_general(left, right, (((0,), (0,)), ((), ())), preferred_element_type=F32)


def head_lanes(shape, which):
    lane = lax.broadcasted_iota(jnp.int32, shape, 1)
    return (lane < HEAD_DIM) if which == 0 else (lane >= HEAD_DIM)


def only_valid(values, width):
    if width % LANES == 0:
        return values
    lane = lax.broadcasted_iota(jnp.int32, values.shape, 1) + pl.program_id(1) * LANES
    return jnp.where(lane < width, values, jnp.zeros_like(values))


def sorted_rows(ref, lead, order_ref, first, last):
    return jnp.concatenate([ref[lead + (order_ref[i], 0)] for i in range(first, last)], axis=0)


def store_rows(ref, lead, order_ref, first, rows):
    local = ref.shape[-2]
    for i in range(rows.shape[0] // local):
        ref[lead + (order_ref[first + i], 0)] = rows[i * local : (i + 1) * local]


def causal(rows, columns):
    key_at = lax.broadcasted_iota(jnp.int32, (rows, columns), 0)
    query_at = lax.broadcasted_iota(jnp.int32, (rows, columns), 1)
    return key_at <= query_at


def attention_forward_kernel(blocks, width, order_ref, q_ref, k_ref, v_ref, o_ref, lse_ref):
    count, local = k_ref.shape[1], k_ref.shape[3]
    tile = blocks * local
    keys = only_valid(sorted_rows(k_ref, (0,), order_ref, 0, count), width)
    values_t = sorted_rows(v_ref, (0,), order_ref, 0, count).astype(F32).T.astype(BF16)
    diagonal = causal(tile, tile)
    for first in range(0, count, blocks):
        start, stop = first * local, (first + blocks) * local
        queries = sorted_rows(q_ref, (0,), order_ref, first, first + blocks)
        queries = queries * jnp.asarray(HEAD_DIM**-0.5, BF16)
        pieces = []
        for which in range(2):
            masked_q = jnp.where(head_lanes(queries.shape, which), queries, jnp.zeros_like(queries))
            scores = dot_nt(keys[:stop], masked_q)
            tiles = []
            if start > 0:
                tiles.append(scores[:start])
            tiles.append(jnp.where(diagonal, scores[start:], -1e30))
            top = functools.reduce(
                jnp.maximum, [jnp.max(block, axis=0, keepdims=True) for block in tiles]
            )
            weights = [jnp.exp(block - top) for block in tiles]
            total = sum(jnp.sum(weight, axis=0, keepdims=True) for weight in weights)
            low = jnp.concatenate([weight.astype(BF16) for weight in weights], axis=0)
            rows = values_t[which * HEAD_DIM : (which + 1) * HEAD_DIM, :stop]
            pieces.append(dot_nn(rows, low) * (1.0 / total))
            lse_ref[0, 0, which : which + 1, start:stop] = top + jnp.log(total)
        mixed_t = jnp.concatenate(pieces, axis=0)
        store_rows(o_ref, (), order_ref, first, mixed_t.T.astype(BF16))


def attention_backward_kernel(
    blocks,
    width,
    order_ref,
    q_ref,
    k_ref,
    v_ref,
    o_ref,
    do_ref,
    lse_ref,
    *refs,
):
    out_ref, dk_acc, dv_acc = refs[-3:]
    count, local = k_ref.shape[1], k_ref.shape[3]
    tile = blocks * local
    keys = only_valid(sorted_rows(k_ref, (0,), order_ref, 0, count), width)
    values = only_valid(sorted_rows(v_ref, (0,), order_ref, 0, count), width)
    keys_t = keys.astype(F32).T.astype(BF16)
    diagonal = causal(tile, tile)
    for first in range(0, count, blocks):
        start, stop = first * local, (first + blocks) * local
        queries = sorted_rows(q_ref, (0,), order_ref, first, first + blocks)
        queries = queries * jnp.asarray(HEAD_DIM**-0.5, BF16)
        grads = sorted_rows(do_ref, (), order_ref, first, first + blocks)
        mixed = sorted_rows(o_ref, (), order_ref, first, first + blocks)
        product_t = (grads.astype(F32) * mixed.astype(F32)).T
        key_lanes = head_lanes((stop, LANES), 0)
        dq_parts, dk_parts, dv_parts = [], [], []
        for which in range(2):
            mine = head_lanes(queries.shape, which)
            masked_q = jnp.where(mine, queries, jnp.zeros_like(queries))
            masked_g = jnp.where(mine, grads, jnp.zeros_like(grads))
            delta = jnp.sum(
                product_t[which * HEAD_DIM : (which + 1) * HEAD_DIM], axis=0, keepdims=True
            )
            lse = lse_ref[0, 0, which : which + 1, start:stop]
            scores = dot_nt(keys[:stop], masked_q)
            grad_weights = dot_nt(values[:stop], masked_g)
            weights = jnp.exp(scores - lse)
            if start > 0:
                weights = jnp.concatenate(
                    [weights[:start], jnp.where(diagonal, weights[start:], 0.0)], axis=0
                )
            else:
                weights = jnp.where(diagonal, weights, 0.0)
            low_scores = (weights * (grad_weights - delta)).astype(BF16)
            dv_parts.append(dot_nn(weights.astype(BF16), grads))
            dk_parts.append(dot_nn(low_scores, queries))
            dq_parts.append(
                dot_nn(keys_t[which * HEAD_DIM : (which + 1) * HEAD_DIM, :stop], low_scores)
            )
        dq_t = jnp.concatenate(dq_parts, axis=0) * (HEAD_DIM**-0.5)
        store_rows(out_ref, (0,), order_ref, first, dq_t.T.astype(BF16))
        dk = jnp.where(key_lanes, dk_parts[0], dk_parts[1])
        dv = jnp.where(key_lanes, dv_parts[0], dv_parts[1])
        if start > 0:
            dk_acc[:start] += dk[:start]
            dv_acc[:start] += dv[:start]
        dk_acc[start:stop] = dk[start:]
        dv_acc[start:stop] = dv[start:]
    store_rows(out_ref, (1,), order_ref, 0, dk_acc[...].astype(BF16))
    store_rows(out_ref, (2,), order_ref, 0, dv_acc[...].astype(BF16))


def query_blocks(count):
    return 2 if count % 2 == 0 else 1


def attention_forward(joined, order):
    _, count, seqs, local, width = joined.shape
    length = count * local
    pairs = pl.cdiv(width, LANES)
    spec = lambda which: pl.BlockSpec(
        (1, count, 1, local, LANES), lambda s, h, order: (which, 0, s, 0, h)
    )
    return pl.pallas_call(
        functools.partial(attention_forward_kernel, query_blocks(count), width),
        grid_spec=pltpu.PrefetchScalarGridSpec(
            num_scalar_prefetch=1,
            grid=(seqs, pairs),
            in_specs=[spec(0), spec(1), spec(2)],
            out_specs=[
                pl.BlockSpec((count, 1, local, LANES), lambda s, h, order: (0, s, 0, h)),
                pl.BlockSpec((1, 1, 8, length), lambda s, h, order: (s, h, 0, 0)),
            ],
        ),
        out_shape=[
            jax.ShapeDtypeStruct((count, seqs, local, width), BF16),
            jax.ShapeDtypeStruct((seqs, pairs, 8, length), F32),
        ],
        compiler_params=pltpu.CompilerParams(vmem_limit_bytes=VMEM_LIMIT),
        cost_estimate=pl.CostEstimate(
            flops=seqs * pairs * 16 * length * length * LANES,
            bytes_accessed=8 * seqs * length * width,
            transcendentals=seqs * pairs * 2 * length * length,
        ),
    )(order, joined, joined, joined)


def attention_backward(joined, mixed, grad_mixed, lse, order, ties=()):
    _, count, seqs, local, width = joined.shape
    length = count * local
    pairs = pl.cdiv(width, LANES)
    spec = lambda which: pl.BlockSpec(
        (1, count, 1, local, LANES), lambda s, h, order: (which, 0, s, 0, h)
    )
    rows = pl.BlockSpec((count, 1, local, LANES), lambda s, h, order: (0, s, 0, h))
    return pl.pallas_call(
        functools.partial(attention_backward_kernel, query_blocks(count), width),
        grid_spec=pltpu.PrefetchScalarGridSpec(
            num_scalar_prefetch=1,
            grid=(seqs, pairs),
            in_specs=[
                spec(0),
                spec(1),
                spec(2),
                rows,
                rows,
                pl.BlockSpec((1, 1, 8, length), lambda s, h, order: (s, h, 0, 0)),
            ]
            + [pl.BlockSpec(memory_space=pl.ANY)] * len(ties),
            out_specs=pl.BlockSpec(
                (3, count, 1, local, LANES), lambda s, h, order: (0, 0, s, 0, h)
            ),
            scratch_shapes=[pltpu.VMEM((length, LANES), F32), pltpu.VMEM((length, LANES), F32)],
        ),
        out_shape=jax.ShapeDtypeStruct(joined.shape, BF16),
        compiler_params=pltpu.CompilerParams(vmem_limit_bytes=VMEM_LIMIT),
        cost_estimate=pl.CostEstimate(
            flops=seqs * pairs * 20 * length * length * LANES,
            bytes_accessed=16 * seqs * length * width,
            transcendentals=seqs * pairs * 2 * length * length,
        ),
    )(order, joined, joined, joined, mixed, grad_mixed, lse, *ties)


def standardize(values):
    centred = values - jnp.mean(values, axis=-1, keepdims=True)
    inverse = lax.rsqrt(jnp.mean(centred * centred, axis=-1, keepdims=True) + EPSILON)
    return centred * inverse, inverse


def normalize_back(grad_out, standard, inverse, gain):
    scaled = grad_out * gain
    return inverse * (
        scaled
        - jnp.mean(scaled, axis=-1, keepdims=True)
        - standard * jnp.mean(scaled * standard, axis=-1, keepdims=True)
    )


def add_row(sums_ref, row, values):
    sums_ref[row : row + 1, :] += jnp.sum(values, axis=0, keepdims=True)


def clear_first(sums_ref):
    @pl.when(pl.program_id(0) == 0)
    def _():
        sums_ref[...] = jnp.zeros_like(sums_ref)


G_ONE, B_ONE, BIAS_Q, BIAS_V, BIAS_OUT, G_TWO, B_TWO, BIAS_PROJ = range(8)


def row(small_ref, index):
    return small_ref[index : index + 1, :]


def qkv_kernel(x_ref, w_ref, small_ref, joined_ref, low_ref):
    standard, _ = standardize(x_ref[...].astype(F32))
    low = (standard * row(small_ref, G_ONE) + row(small_ref, B_ONE)).astype(BF16)
    low_ref[...] = low
    for which, bias in enumerate((BIAS_Q, None, BIAS_V)):
        out = dot_nn(low, w_ref[which])
        if bias is not None:
            out = out + row(small_ref, bias)
        joined_ref[which] = out.astype(BF16)


def attended_kernel(x_ref, o_ref, w_ref, small_ref, middle_ref, low_ref):
    middle = x_ref[...].astype(F32) + dot_nn(o_ref[...], w_ref[0]) + row(small_ref, BIAS_OUT)
    middle_ref[...] = middle
    standard, _ = standardize(middle)
    low_ref[...] = (standard * row(small_ref, G_TWO) + row(small_ref, B_TWO)).astype(BF16)


def hidden_kernel(low_ref, w_ref, bias_ref, act_ref, slope_ref):
    low = low_ref[...]
    scale = 0.7978845608028654
    for which in range(w_ref.shape[0]):
        hidden = dot_nn(low, w_ref[which]) + bias_ref[which]
        square = hidden * hidden
        bent = jnp.tanh(scale * hidden * (1.0 + 0.044715 * square))
        half = 0.5 * (1.0 + bent)
        act_ref[which] = (hidden * half).astype(BF16)
        slope = half + 0.5 * hidden * (1.0 - bent * bent) * (
            scale * (1.0 + 3.0 * 0.044715 * square)
        )
        slope_ref[which] = slope.astype(BF16)


def output_kernel(middle_ref, act_ref, w_ref, small_ref, out_ref):
    total = middle_ref[...] + row(small_ref, BIAS_PROJ)
    for which in range(w_ref.shape[0]):
        total += dot_nn(act_ref[which], w_ref[which])
    out_ref[...] = total.astype(BF16)


def hidden_back_kernel(grad_ref, slope_ref, w_ref, *refs):
    out_ref, sums_ref = refs[-2:]
    clear_first(sums_ref)
    grad = grad_ref[...]
    for which in range(w_ref.shape[0]):
        back = dot_nt(grad, w_ref[which]) * slope_ref[which].astype(F32)
        low = back.astype(BF16)
        out_ref[which] = low
        add_row(sums_ref, which, low.astype(F32))


def middle_back_kernel(hidden_ref, grad_ref, middle_ref, w_ref, out_w_ref, small_ref, *refs):
    grad_middle_ref, low_ref, mixed_ref, sums_ref = refs[-4:]
    clear_first(sums_ref)
    grad_two = dot_nt(hidden_ref[0], w_ref[0])
    for which in range(1, w_ref.shape[0]):
        grad_two += dot_nt(hidden_ref[which], w_ref[which])
    standard, inverse = standardize(middle_ref[...])
    grad_out = grad_ref[...].astype(F32)
    grad_middle = grad_out + normalize_back(grad_two, standard, inverse, row(small_ref, G_TWO))
    low = grad_middle.astype(BF16)
    grad_middle_ref[...] = grad_middle
    low_ref[...] = low
    mixed_ref[...] = dot_nt(low, out_w_ref[0]).astype(BF16)
    add_row(sums_ref, G_TWO, grad_two * standard)
    add_row(sums_ref, B_TWO, grad_two)
    add_row(sums_ref, BIAS_OUT, low.astype(F32))
    add_row(sums_ref, BIAS_PROJ, grad_out)


def input_back_kernel(joined_ref, grad_middle_ref, x_ref, w_ref, small_ref, *refs):
    out_ref, sums_ref = refs[-2:]
    clear_first(sums_ref)
    grad_one = dot_nt(joined_ref[0], w_ref[0])
    for which in range(1, 3):
        grad_one += dot_nt(joined_ref[which], w_ref[which])
    standard, inverse = standardize(x_ref[...].astype(F32))
    back = normalize_back(grad_one, standard, inverse, row(small_ref, G_ONE))
    out_ref[...] = (grad_middle_ref[...] + back).astype(BF16)
    add_row(sums_ref, G_ONE, grad_one * standard)
    add_row(sums_ref, B_ONE, grad_one)
    add_row(sums_ref, BIAS_Q, joined_ref[0].astype(F32))
    add_row(sums_ref, BIAS_V, joined_ref[2].astype(F32))


def by_rows(kernel, by_row, fixed, outs, sums=None, ties=(), tile=256):
    rows, width = by_row[0].shape[-2:]
    tile = tile if rows % tile == 0 else rows
    whole = lambda shape, index: pl.BlockSpec(
        shape, lambda i: index, pipeline_mode=pl.Buffered(buffer_count=1)
    )
    tiled = lambda lead: pl.BlockSpec(
        tuple(lead) + (tile, width), lambda i: (0,) * len(lead) + (i, 0)
    )
    in_specs = [tiled(array.shape[:-2]) for array in by_row]
    operands = list(by_row)
    products = 0
    for entry in fixed:
        array, first, blocks = entry if isinstance(entry, tuple) else (entry, 0, entry.shape[0])
        shape = (blocks,) + array.shape[1:]
        in_specs.append(whole(shape, (first // blocks,) + (0,) * (array.ndim - 1)))
        operands.append(array)
        if array.dtype == BF16:
            products += blocks
    in_specs += [pl.BlockSpec(memory_space=pl.ANY)] * len(ties)
    operands += list(ties)
    out_specs = [tiled(lead) for lead, _ in outs]
    out_shape = [jax.ShapeDtypeStruct(tuple(lead) + (rows, width), kind) for lead, kind in outs]
    if sums:
        out_specs.append(pl.BlockSpec((sums, width), lambda i: (0, 0)))
        out_shape.append(jax.ShapeDtypeStruct((sums, width), F32))
    moved = sum(array.size * array.dtype.itemsize for array in operands)
    moved += sum(leaf.size * leaf.dtype.itemsize for leaf in out_shape)
    return pl.pallas_call(
        kernel,
        grid=(rows // tile,),
        in_specs=in_specs,
        out_specs=out_specs,
        out_shape=out_shape,
        compiler_params=pltpu.CompilerParams(vmem_limit_bytes=VMEM_LIMIT),
        cost_estimate=pl.CostEstimate(
            flops=3 * rows * width * width * products, bytes_accessed=moved, transcendentals=0
        ),
    )(*operands)


def row_major(values):
    return with_layout_constraint(values, Layout(major_to_minor=tuple(range(values.ndim))))


def swap(values, axis, offset):
    count = lax.axis_size(axis)
    return lax.ppermute(values, axis, [(index, index ^ offset) for index in range(count)])


def after(values, *earlier):
    return lax.optimization_barrier((values, *earlier))


def pick(bit, on_zero, on_one):
    return jnp.where(bit == 0, on_zero, on_one)


def to_sequences(values, count):
    seqs, local, width = values.shape
    own = lax.axis_index("ctx")
    parts = values.reshape(count, seqs // count, local, width)
    pieces = []
    for offset in range(count):
        piece = row_major(lax.dynamic_index_in_dim(parts, own ^ offset, keepdims=False))
        pieces.append(row_major(swap(piece, "ctx", offset)) if offset else piece)
    return row_major(jnp.stack(pieces))


def to_blocks(values, kind):
    count, share, local, width = values.shape
    own = lax.axis_index("ctx")
    out = row_major(jnp.zeros((count, share, local, width), kind))
    for offset in range(count):
        piece = row_major(values[offset])
        if offset:
            piece = row_major(swap(piece, "ctx", offset))
        out = lax.dynamic_update_index_in_dim(out, piece.astype(kind), own ^ offset, 0)
    return row_major(out).reshape(count * share, local, width)


class Windows:
    def __init__(self, owned_rows):
        tiles = owned_rows // 16
        self.start = tiles // 2 * 16
        self.size = owned_rows - self.start
        ctx = lax.axis_index("ctx")
        self.core = ctx % 2
        self.y = ctx // 2
        self.x = lax.axis_index("replica")

    def rows(self, values):
        return pick(
            self.core, values[..., : self.size, :], values[..., self.start :, :]
        )

    def other_rows(self, values):
        return pick(
            self.core, values[..., self.start :, :], values[..., : self.size, :]
        )

    def block(self, blocks):
        return pick(
            self.x,
            pick(self.y, blocks[0], blocks[1]),
            pick(self.y, blocks[2], blocks[3]),
        )


def assemble_kernel(groups, start, size, transposed, here_ref, *refs):
    arrays, out_ref = refs[:-1], refs[-1]
    x, y, core = here_ref[0], here_ref[1], here_ref[2]
    for turn in range(2):
        row = pl.multiple_of((core ^ turn) * start, 16)
        for (places, first), ref in zip(groups, arrays[turn * len(groups) :]):
            for i, (dx, dy) in enumerate(places):
                block = 2 * (x ^ dx) + (y ^ dy)
                for s in range(ref.shape[1]):
                    place = (first + s, block) if transposed else (block, first + s)
                    out_ref[place + (pl.ds(row, size), slice(None))] = ref[
                        i, s, :size, :
                    ].astype(out_ref.dtype)


def assemble(win, groups, own, other, owned_rows, shards, transposed, kind):
    width = own[0].shape[-1]
    here = jnp.stack([win.x, win.y, win.core]).astype(jnp.int32)
    shape = (shards, 4, owned_rows, width) if transposed else (4, shards, owned_rows, width)
    return pl.pallas_call(
        functools.partial(assemble_kernel, groups, win.start, win.size, transposed),
        in_specs=[pl.BlockSpec(memory_space=pltpu.SMEM)]
        + [pl.BlockSpec(memory_space=pltpu.VMEM)] * (2 * len(groups)),
        out_specs=pl.BlockSpec(memory_space=pltpu.VMEM),
        out_shape=jax.ShapeDtypeStruct(shape, kind),
        compiler_params=pltpu.CompilerParams(vmem_limit_bytes=VMEM_LIMIT),
        cost_estimate=pl.CostEstimate(
            flops=0, bytes_accessed=16 * shards * owned_rows * width, transcendentals=0
        ),
    )(here, *own, *other)


def spread_weights(win, mine, owned_rows, transposed=False, kind=BF16):
    shards = mine.shape[0]
    if shards == 1:
        first = jnp.stack([mine, swap(mine, "replica", 1)])
        own = [first, swap(first, "ctx", 2)]
        groups = ((((0, 0), (1, 0)), 0), (((0, 1), (1, 1)), 0))
    else:
        split = max(shards // 4, 1)
        low, high = mine[:split], mine[split:]
        low_there, high_there = after(swap(low, "replica", 1), swap(high, "ctx", 2))
        first = jnp.stack([low, low_there])
        second = jnp.stack([high, high_there])
        own = [first, second, swap(first, "ctx", 2), swap(second, "replica", 1)]
        groups = (
            (((0, 0), (1, 0)), 0),
            (((0, 0), (0, 1)), split),
            (((0, 1), (1, 1)), 0),
            (((1, 0), (1, 1)), split),
        )
    other = [swap(array, "ctx", 1) for array in own]
    return assemble(win, groups, own, other, owned_rows, shards, transposed, kind), own[-2:]


def add_pair(kept, received):
    return (kept.astype(F32) + received.astype(F32)).astype(BF16)


def corner(values):
    return values[(0,) * (values.ndim - 2)][:16, :LANES]


def reduce_blocks(win, grads):
    shards = grads.shape[1]
    split = shards - max(shards // 4, 1)
    received = swap(win.other_rows(grads), "ctx", 1)
    both = add_pair(win.rows(grads), received)
    x_kept = pick(win.x, both[:2, :split], both[2:, :split])
    x_sent = pick(win.x, both[2:, :split], both[:2, :split])
    y_kept = pick(win.y, both[0::2, split:], both[1::2, split:])
    y_sent = pick(win.y, both[1::2, split:], both[0::2, split:])
    x_received, y_received = after(swap(x_sent, "replica", 1), swap(y_sent, "ctx", 2))
    low = add_pair(x_kept, x_received)
    high = add_pair(y_kept, y_received)
    low_received = swap(pick(win.y, low[1], low[0]), "ctx", 2)
    high_received = swap(pick(win.x, high[1], high[0]), "replica", 1)
    low_sum = add_pair(pick(win.y, low[0], low[1]), low_received)
    high_sum = add_pair(pick(win.x, high[0], high[1]), high_received)
    marks = (
        [corner(received)],
        [corner(x_received), corner(y_received)],
        [corner(low_received), corner(high_received)],
    )
    return jnp.concatenate([low_sum, high_sum], axis=0), marks


def reduce_vectors(values):
    values = add_pair(values, swap(values, "ctx", 1))
    values = add_pair(values, swap(values, "replica", 1))
    return add_pair(values, swap(values, "ctx", 2))


def per_device(
    tokens,
    cotangent,
    block_order,
    ln1_gain,
    ln1_bias,
    qkv_weight,
    q_bias,
    v_bias,
    out_weight,
    out_bias,
    ln2_gain,
    ln2_bias,
    fc_weight,
    fc_bias,
    proj_weight,
    proj_bias,
):
    seq_count, local_len, width = tokens.shape
    owned_rows = ln1_gain.shape[0]
    shards = width // owned_rows
    wide = fc_weight.shape[1] // width
    count = lax.axis_size("ctx")
    rows = seq_count * local_len
    pairwise = lax.axis_size("replica") == 2 and count == 4 and shards % 2 == 0
    win = Windows(owned_rows)

    vectors = jnp.concatenate(
        [ln1_gain, ln1_bias, q_bias, v_bias, out_bias, ln2_gain, ln2_bias, proj_bias, fc_bias]
    )
    vector_rows = vectors.shape[0] // width
    vector_tile = jnp.pad(vectors.reshape(vector_rows, width), ((0, -vector_rows % 16), (0, 0)))
    column = lambda values, i: values[:, i * width : (i + 1) * width]
    blocks_a = [column(qkv_weight, i) for i in range(3)] + [out_weight]
    blocks_b = [column(fc_weight, i) for i in range(wide)]
    blocks_c = [proj_weight[i * owned_rows : (i + 1) * owned_rows] for i in range(wide)]

    def gather_z(values):
        return lax.all_gather(values, "shard", axis=0, tiled=False)

    low_inputs = to_sequences(tokens, count).reshape(rows, width)

    if pairwise:
        mine = [win.rows(win.block(blocks)) for blocks in (blocks_a, blocks_b, blocks_c)]
        part_a = gather_z(jnp.concatenate([mine[0], vector_tile], axis=0))
        mine_b, part_a = after(mine[1], part_a)
        part_b = gather_z(mine_b)
        mine_c, part_b = after(mine[2], part_b)
        part_c = gather_z(mine_c)
        part_a, low_inputs = after(part_a, low_inputs)
        vector_part = part_a[:, win.size : win.size + vector_rows]
        full_a, steps = spread_weights(win, part_a[:, : win.size], owned_rows)
        part_b, *_ = after(part_b, *steps)
        full_b, steps = spread_weights(win, part_b, owned_rows)
        part_c, *_ = after(part_c, *steps)
        full_c, steps = spread_weights(win, part_c, owned_rows, transposed=True)
        cotangent, *_ = after(cotangent, *steps)
    else:
        vector_part = gather_z(vector_tile)[:, :vector_rows]
        full_a, full_b, full_c = [
            gather_z(jnp.stack(blocks)) for blocks in (blocks_a, blocks_b, blocks_c)
        ]
        full_a, full_b = full_a.transpose(1, 0, 2, 3), full_b.transpose(1, 0, 2, 3)
    w_a = full_a.reshape(4, width, width)
    w_fc = full_b.reshape(wide, width, width)
    w_proj = full_c.reshape(wide, width, width)
    vector_part = vector_part.reshape(shards, vector_rows * width).astype(F32)
    small = vector_part[:, : 8 * owned_rows].reshape(shards, 8, owned_rows)
    small = small.transpose(1, 0, 2).reshape(8, width)
    bias_fc = vector_part[:, 8 * owned_rows :].reshape(wide, 1, width)

    low_grad_out = to_sequences(cotangent, count).reshape(rows, width)
    share = seq_count // count
    blocked = (count, share, local_len, width)
    index = jnp.arange(count, dtype=jnp.int32)
    held_by = jnp.sum(jnp.where(block_order[None, :] == index[:, None], index[None, :], 0), axis=1)
    order = (held_by ^ lax.axis_index("ctx")).astype(jnp.int32)

    joined, low_one = by_rows(
        qkv_kernel, [low_inputs], [(w_a, 0, 3), small], [((3,), BF16), ((), BF16)]
    )
    joined = joined.reshape((3,) + blocked)
    mixed, lse = attention_forward(joined, order)
    attended = mixed.reshape(rows, width)
    middle, low_two = by_rows(
        attended_kernel, [low_inputs, attended], [(w_a, 3, 1), small], [((), F32), ((), BF16)]
    )
    low_act, slope = by_rows(
        hidden_kernel, [low_two], [w_fc, bias_fc], [((wide,), BF16), ((wide,), BF16)]
    )
    (outputs,) = by_rows(output_kernel, [middle, low_act], [w_proj, small], [((), BF16)])
    layer_out = to_blocks(outputs.reshape(blocked), BF16)

    def reduce_units(grads, extra=None):
        if pairwise:
            sums, marks = reduce_blocks(win, grads)
            if extra is not None:
                sums = jnp.concatenate([sums, reduce_vectors(extra)], axis=1)
            sums = lax.psum_scatter(sums, "shard", scatter_dimension=0, tiled=False)
            full = spread_weights(win, sums[None, : win.size], owned_rows, kind=F32)[0][:, 0]
            return full, sums[win.size :], marks
        rest = ("replica", "ctx")
        full = lax.psum_scatter(grads, "shard", scatter_dimension=1, tiled=False)
        full = lax.psum(full, rest)
        if extra is not None:
            extra = lax.psum_scatter(extra, "shard", scatter_dimension=0, tiled=False)
            extra = lax.psum(extra, rest)
        return full.astype(F32), extra, ((), (), ())

    def by_shard(grads):
        return grads.astype(BF16).reshape(4, shards, owned_rows, width)

    grad_proj = jnp.einsum("ctx,td->cxd", low_act, low_grad_out, preferred_element_type=F32)
    grad_proj = grad_proj.astype(BF16)
    owned_proj, _, proj_marks = reduce_units(by_shard(grad_proj).transpose(1, 0, 2, 3))
    grad_hidden, sums_hidden = by_rows(
        hidden_back_kernel,
        [low_grad_out, slope],
        [w_proj],
        [((wide,), BF16)],
        sums=8,
        ties=[corner(grad_proj)],
    )
    grad_fc = jnp.einsum("td,ctx->cdx", low_two, grad_hidden, preferred_element_type=F32)
    grad_fc = grad_fc.astype(BF16)
    owned_fc, _, fc_marks = reduce_units(by_shard(grad_fc))
    grad_middle, low_grad_middle, grad_mixed, sums_middle = by_rows(
        middle_back_kernel,
        [grad_hidden, low_grad_out, middle],
        [w_fc, (w_a, 3, 1), small],
        [((), F32), ((), BF16), ((), BF16)],
        sums=8,
        ties=[corner(grad_fc), *proj_marks[0]],
    )
    grad_out_weight = dot_tn(attended, low_grad_middle).astype(BF16)
    grad_joined = attention_backward(
        joined,
        mixed,
        grad_mixed.reshape(blocked),
        lse,
        order,
        ties=[*proj_marks[1], *fc_marks[0]],
    ).reshape(3, rows, width)
    grad_qkv = jnp.einsum("td,ctx->cdx", low_one, grad_joined, preferred_element_type=F32)
    grad_qkv = grad_qkv.astype(BF16)
    grads_a = jnp.concatenate([grad_qkv, grad_out_weight[None]], axis=0)
    grad_inputs, sums_input = by_rows(
        input_back_kernel,
        [grad_joined, grad_middle, low_inputs],
        [(w_a, 0, 3), small],
        [((), BF16)],
        sums=8,
        ties=[corner(grad_qkv), *proj_marks[2], *fc_marks[1]],
    )
    input_grad = to_blocks(grad_inputs.reshape(blocked), F32)

    small_grads = sums_middle + sums_input
    grad_fc_bias = sums_hidden[:wide]
    vector_grads = jnp.concatenate(
        [
            small_grads.reshape(8, shards, owned_rows)
            .transpose(1, 0, 2)
            .reshape(shards, 8 * owned_rows),
            grad_fc_bias.reshape(shards, owned_rows * wide),
        ],
        axis=1,
    ).astype(BF16)
    vector_grads = jnp.pad(
        vector_grads.reshape(shards, vector_rows, width),
        ((0, 0), (0, -vector_rows % 16), (0, 0)),
    )
    owned_a, owned_vectors, _ = reduce_units(by_shard(grads_a), vector_grads)
    owned_vectors = owned_vectors[:vector_rows].reshape(-1).astype(F32)
    vec = [owned_vectors[i * owned_rows : (i + 1) * owned_rows] for i in range(8)]
    qkv_grad = jnp.concatenate([owned_a[i] for i in range(3)], axis=1)
    fc_grad = jnp.concatenate([owned_fc[i] for i in range(wide)], axis=1)
    return (
        layer_out,
        input_grad,
        vec[0],
        vec[1],
        qkv_grad,
        vec[2],
        vec[3],
        owned_a[3],
        vec[4],
        vec[5],
        vec[6],
        fc_grad,
        owned_vectors[8 * owned_rows :],
        owned_proj.reshape(wide * owned_rows, width),
        vec[7],
    )


def solution(mesh):
    vector, matrix = P("shard"), P("shard", None)
    rows = P(("shard", "replica"), "ctx", None)
    weights = (
        vector,
        vector,
        matrix,
        vector,
        vector,
        matrix,
        vector,
        vector,
        vector,
        matrix,
        vector,
        matrix,
        vector,
    )
    return jax.shard_map(
        per_device,
        mesh=mesh,
        in_specs=(rows, rows, P()) + weights,
        out_specs=(rows, rows) + weights,
        check_vma=False,
    )
```

```python
import functools

import jax
import jax.numpy as jnp
from jax import lax
from jax.experimental import pallas as pl
from jax.experimental.layout import Layout, with_layout_constraint
from jax.experimental.pallas import tpu as pltpu
from jax.sharding import PartitionSpec as P

HEAD_DIM = 64
EPSILON = 1e-05
LANES = 128
VMEM_LIMIT = 56 * 1024 * 1024
COST_SCALE = 8

BF16 = jnp.bfloat16
F32 = jnp.float32


def dot_nn(left, right):
    return lax.dot_general(left, right, (((1,), (0,)), ((), ())), preferred_element_type=F32)


def dot_nt(left, right):
    return lax.dot_general(left, right, (((1,), (1,)), ((), ())), preferred_element_type=F32)


def dot_tn(left, right):
    return lax.dot_general(left, right, (((0,), (0,)), ((), ())), preferred_element_type=F32)


def head_lanes(shape, which):
    lane = lax.broadcasted_iota(jnp.int32, shape, 1)
    return (lane < HEAD_DIM) if which == 0 else (lane >= HEAD_DIM)


def only_valid(values, width):
    if width % LANES == 0:
        return values
    lane = lax.broadcasted_iota(jnp.int32, values.shape, 1) + pl.program_id(1) * LANES
    return jnp.where(lane < width, values, jnp.zeros_like(values))


def sorted_rows(ref, lead, order_ref, first, last):
    return jnp.concatenate([ref[lead + (order_ref[i], 0)] for i in range(first, last)], axis=0)


def store_rows(ref, lead, order_ref, first, rows):
    local = ref.shape[-2]
    for i in range(rows.shape[0] // local):
        ref[lead + (order_ref[first + i], 0)] = rows[i * local : (i + 1) * local]


def causal(rows, columns):
    key_at = lax.broadcasted_iota(jnp.int32, (rows, columns), 0)
    query_at = lax.broadcasted_iota(jnp.int32, (rows, columns), 1)
    return key_at <= query_at


def attention_forward_kernel(blocks, width, order_ref, q_ref, k_ref, v_ref, o_ref, lse_ref):
    count, local = k_ref.shape[1], k_ref.shape[3]
    tile = blocks * local
    keys = only_valid(sorted_rows(k_ref, (0,), order_ref, 0, count), width)
    values_t = sorted_rows(v_ref, (0,), order_ref, 0, count).astype(F32).T.astype(BF16)
    diagonal = causal(tile, tile)
    for first in range(0, count, blocks):
        start, stop = first * local, (first + blocks) * local
        queries = sorted_rows(q_ref, (0,), order_ref, first, first + blocks)
        queries = queries * jnp.asarray(HEAD_DIM**-0.5, BF16)
        pieces = []
        for which in range(2):
            masked_q = jnp.where(head_lanes(queries.shape, which), queries, jnp.zeros_like(queries))
            scores = dot_nt(keys[:stop], masked_q)
            tiles = []
            if start > 0:
                tiles.append(scores[:start])
            tiles.append(jnp.where(diagonal, scores[start:], -1e30))
            top = functools.reduce(
                jnp.maximum, [jnp.max(block, axis=0, keepdims=True) for block in tiles]
            )
            weights = [jnp.exp(block - top) for block in tiles]
            total = sum(jnp.sum(weight, axis=0, keepdims=True) for weight in weights)
            low = jnp.concatenate([weight.astype(BF16) for weight in weights], axis=0)
            rows = values_t[which * HEAD_DIM : (which + 1) * HEAD_DIM, :stop]
            pieces.append(dot_nn(rows, low) * (1.0 / total))
            lse_ref[0, 0, which : which + 1, start:stop] = top + jnp.log(total)
        mixed_t = jnp.concatenate(pieces, axis=0)
        store_rows(o_ref, (), order_ref, first, mixed_t.T.astype(BF16))


def attention_backward_kernel(
    blocks,
    width,
    order_ref,
    q_ref,
    k_ref,
    v_ref,
    o_ref,
    do_ref,
    lse_ref,
    *refs,
):
    out_ref, dk_acc, dv_acc = refs[-3:]
    count, local = k_ref.shape[1], k_ref.shape[3]
    tile = blocks * local
    keys = only_valid(sorted_rows(k_ref, (0,), order_ref, 0, count), width)
    values = only_valid(sorted_rows(v_ref, (0,), order_ref, 0, count), width)
    keys_t = keys.astype(F32).T.astype(BF16)
    diagonal = causal(tile, tile)
    for first in range(0, count, blocks):
        start, stop = first * local, (first + blocks) * local
        queries = sorted_rows(q_ref, (0,), order_ref, first, first + blocks)
        queries = queries * jnp.asarray(HEAD_DIM**-0.5, BF16)
        grads = sorted_rows(do_ref, (), order_ref, first, first + blocks)
        mixed = sorted_rows(o_ref, (), order_ref, first, first + blocks)
        product_t = (grads.astype(F32) * mixed.astype(F32)).T
        key_lanes = head_lanes((stop, LANES), 0)
        dq_parts, dk_parts, dv_parts = [], [], []
        for which in range(2):
            mine = head_lanes(queries.shape, which)
            masked_q = jnp.where(mine, queries, jnp.zeros_like(queries))
            masked_g = jnp.where(mine, grads, jnp.zeros_like(grads))
            delta = jnp.sum(
                product_t[which * HEAD_DIM : (which + 1) * HEAD_DIM], axis=0, keepdims=True
            )
            lse = lse_ref[0, 0, which : which + 1, start:stop]
            scores = dot_nt(keys[:stop], masked_q)
            grad_weights = dot_nt(values[:stop], masked_g)
            weights = jnp.exp(scores - lse)
            if start > 0:
                weights = jnp.concatenate(
                    [weights[:start], jnp.where(diagonal, weights[start:], 0.0)], axis=0
                )
            else:
                weights = jnp.where(diagonal, weights, 0.0)
            low_scores = (weights * (grad_weights - delta)).astype(BF16)
            dv_parts.append(dot_nn(weights.astype(BF16), grads))
            dk_parts.append(dot_nn(low_scores, queries))
            dq_parts.append(
                dot_nn(keys_t[which * HEAD_DIM : (which + 1) * HEAD_DIM, :stop], low_scores)
            )
        dq_t = jnp.concatenate(dq_parts, axis=0) * (HEAD_DIM**-0.5)
        store_rows(out_ref, (0,), order_ref, first, dq_t.T.astype(BF16))
        dk = jnp.where(key_lanes, dk_parts[0], dk_parts[1])
        dv = jnp.where(key_lanes, dv_parts[0], dv_parts[1])
        if start > 0:
            dk_acc[:start] += dk[:start]
            dv_acc[:start] += dv[:start]
        dk_acc[start:stop] = dk[start:]
        dv_acc[start:stop] = dv[start:]
    store_rows(out_ref, (1,), order_ref, 0, dk_acc[...].astype(BF16))
    store_rows(out_ref, (2,), order_ref, 0, dv_acc[...].astype(BF16))


def query_blocks(count):
    return 2 if count % 2 == 0 else 1


def attention_forward(joined, order):
    _, count, seqs, local, width = joined.shape
    length = count * local
    pairs = pl.cdiv(width, LANES)
    spec = lambda which: pl.BlockSpec(
        (1, count, 1, local, LANES), lambda s, h, order: (which, 0, s, 0, h)
    )
    return pl.pallas_call(
        functools.partial(attention_forward_kernel, query_blocks(count), width),
        grid_spec=pltpu.PrefetchScalarGridSpec(
            num_scalar_prefetch=1,
            grid=(seqs, pairs),
            in_specs=[spec(0), spec(1), spec(2)],
            out_specs=[
                pl.BlockSpec((count, 1, local, LANES), lambda s, h, order: (0, s, 0, h)),
                pl.BlockSpec((1, 1, 8, length), lambda s, h, order: (s, h, 0, 0)),
            ],
        ),
        out_shape=[
            jax.ShapeDtypeStruct((count, seqs, local, width), BF16),
            jax.ShapeDtypeStruct((seqs, pairs, 8, length), F32),
        ],
        compiler_params=pltpu.CompilerParams(vmem_limit_bytes=VMEM_LIMIT),
        cost_estimate=pl.CostEstimate(
            flops=seqs * pairs * 16 * length * length * LANES // COST_SCALE,
            bytes_accessed=8 * seqs * length * width // COST_SCALE,
            transcendentals=0,
        ),
    )(order, joined, joined, joined)


def attention_backward(joined, mixed, grad_mixed, lse, order, ties=()):
    _, count, seqs, local, width = joined.shape
    length = count * local
    pairs = pl.cdiv(width, LANES)
    spec = lambda which: pl.BlockSpec(
        (1, count, 1, local, LANES), lambda s, h, order: (which, 0, s, 0, h)
    )
    rows = pl.BlockSpec((count, 1, local, LANES), lambda s, h, order: (0, s, 0, h))
    return pl.pallas_call(
        functools.partial(attention_backward_kernel, query_blocks(count), width),
        grid_spec=pltpu.PrefetchScalarGridSpec(
            num_scalar_prefetch=1,
            grid=(seqs, pairs),
            in_specs=[
                spec(0),
                spec(1),
                spec(2),
                rows,
                rows,
                pl.BlockSpec((1, 1, 8, length), lambda s, h, order: (s, h, 0, 0)),
            ]
            + [pl.BlockSpec(memory_space=pl.ANY)] * len(ties),
            out_specs=pl.BlockSpec(
                (3, count, 1, local, LANES), lambda s, h, order: (0, 0, s, 0, h)
            ),
            scratch_shapes=[pltpu.VMEM((length, LANES), F32), pltpu.VMEM((length, LANES), F32)],
        ),
        out_shape=jax.ShapeDtypeStruct(joined.shape, BF16),
        compiler_params=pltpu.CompilerParams(vmem_limit_bytes=VMEM_LIMIT),
        cost_estimate=pl.CostEstimate(
            flops=seqs * pairs * 20 * length * length * LANES // COST_SCALE,
            bytes_accessed=16 * seqs * length * width // COST_SCALE,
            transcendentals=0,
        ),
    )(order, joined, joined, joined, mixed, grad_mixed, lse, *ties)


def standardize(values):
    centred = values - jnp.mean(values, axis=-1, keepdims=True)
    inverse = lax.rsqrt(jnp.mean(centred * centred, axis=-1, keepdims=True) + EPSILON)
    return centred * inverse, inverse


def normalize_back(grad_out, standard, inverse, gain):
    scaled = grad_out * gain
    return inverse * (
        scaled
        - jnp.mean(scaled, axis=-1, keepdims=True)
        - standard * jnp.mean(scaled * standard, axis=-1, keepdims=True)
    )


def add_row(sums_ref, row, values):
    sums_ref[row : row + 1, :] += jnp.sum(values, axis=0, keepdims=True)


def clear_first(sums_ref):
    @pl.when(pl.program_id(0) == 0)
    def _():
        sums_ref[...] = jnp.zeros_like(sums_ref)


G_ONE, B_ONE, BIAS_Q, BIAS_V, BIAS_OUT, G_TWO, B_TWO, BIAS_PROJ = range(8)


def row(small_ref, index):
    return small_ref[index : index + 1, :]


def qkv_kernel(x_ref, w_ref, small_ref, joined_ref, low_ref):
    standard, _ = standardize(x_ref[...].astype(F32))
    low = (standard * row(small_ref, G_ONE) + row(small_ref, B_ONE)).astype(BF16)
    low_ref[...] = low
    for which, bias in enumerate((BIAS_Q, None, BIAS_V)):
        out = dot_nn(low, w_ref[which])
        if bias is not None:
            out = out + row(small_ref, bias)
        joined_ref[which] = out.astype(BF16)


def attended_kernel(x_ref, o_ref, w_ref, small_ref, *refs):
    middle_ref, low_ref = refs[-2:]
    middle = x_ref[...].astype(F32) + dot_nn(o_ref[...], w_ref[0]) + row(small_ref, BIAS_OUT)
    middle_ref[...] = middle
    standard, _ = standardize(middle)
    low_ref[...] = (standard * row(small_ref, G_TWO) + row(small_ref, B_TWO)).astype(BF16)


def hidden_kernel(low_ref, w_ref, bias_ref, act_ref, slope_ref):
    low = low_ref[...]
    scale = 0.7978845608028654
    for which in range(w_ref.shape[0]):
        hidden = dot_nn(low, w_ref[which]) + bias_ref[which]
        square = hidden * hidden
        bent = jnp.tanh(scale * hidden * (1.0 + 0.044715 * square))
        half = 0.5 * (1.0 + bent)
        act_ref[which] = (hidden * half).astype(BF16)
        slope = half + 0.5 * hidden * (1.0 - bent * bent) * (
            scale * (1.0 + 3.0 * 0.044715 * square)
        )
        slope_ref[which] = slope.astype(BF16)


def output_kernel(middle_ref, act_ref, w_ref, small_ref, *refs):
    out_ref = refs[-1]
    total = middle_ref[...] + row(small_ref, BIAS_PROJ)
    for which in range(w_ref.shape[0]):
        total += dot_nn(act_ref[which], w_ref[which])
    out_ref[...] = total.astype(BF16)


def hidden_back_kernel(grad_ref, slope_ref, w_ref, *refs):
    out_ref, sums_ref = refs[-2:]
    clear_first(sums_ref)
    grad = grad_ref[...]
    for which in range(w_ref.shape[0]):
        back = dot_nt(grad, w_ref[which]) * slope_ref[which].astype(F32)
        low = back.astype(BF16)
        out_ref[which] = low
        add_row(sums_ref, which, low.astype(F32))


def middle_back_kernel(hidden_ref, grad_ref, middle_ref, w_ref, out_w_ref, small_ref, *refs):
    grad_middle_ref, low_ref, mixed_ref, sums_ref = refs[-4:]
    clear_first(sums_ref)
    grad_two = dot_nt(hidden_ref[0], w_ref[0])
    for which in range(1, w_ref.shape[0]):
        grad_two += dot_nt(hidden_ref[which], w_ref[which])
    standard, inverse = standardize(middle_ref[...])
    grad_out = grad_ref[...].astype(F32)
    grad_middle = grad_out + normalize_back(grad_two, standard, inverse, row(small_ref, G_TWO))
    low = grad_middle.astype(BF16)
    grad_middle_ref[...] = grad_middle
    low_ref[...] = low
    mixed_ref[...] = dot_nt(low, out_w_ref[0]).astype(BF16)
    add_row(sums_ref, G_TWO, grad_two * standard)
    add_row(sums_ref, B_TWO, grad_two)
    add_row(sums_ref, BIAS_OUT, low.astype(F32))
    add_row(sums_ref, BIAS_PROJ, grad_out)


def input_back_kernel(joined_ref, grad_middle_ref, x_ref, w_ref, small_ref, *refs):
    out_ref, sums_ref = refs[-2:]
    clear_first(sums_ref)
    grad_one = dot_nt(joined_ref[0], w_ref[0])
    for which in range(1, 3):
        grad_one += dot_nt(joined_ref[which], w_ref[which])
    standard, inverse = standardize(x_ref[...].astype(F32))
    back = normalize_back(grad_one, standard, inverse, row(small_ref, G_ONE))
    out_ref[...] = (grad_middle_ref[...] + back).astype(BF16)
    add_row(sums_ref, G_ONE, grad_one * standard)
    add_row(sums_ref, B_ONE, grad_one)
    add_row(sums_ref, BIAS_Q, joined_ref[0].astype(F32))
    add_row(sums_ref, BIAS_V, joined_ref[2].astype(F32))


def by_rows(kernel, by_row, fixed, outs, sums=None, ties=(), tile=256):
    rows, width = by_row[0].shape[-2:]
    tile = tile if rows % tile == 0 else rows
    whole = lambda shape, index: pl.BlockSpec(
        shape, lambda i: index, pipeline_mode=pl.Buffered(buffer_count=1)
    )
    tiled = lambda lead: pl.BlockSpec(
        tuple(lead) + (tile, width), lambda i: (0,) * len(lead) + (i, 0)
    )
    in_specs = [tiled(array.shape[:-2]) for array in by_row]
    operands = list(by_row)
    products = 0
    for entry in fixed:
        array, first, blocks = entry if isinstance(entry, tuple) else (entry, 0, entry.shape[0])
        shape = (blocks,) + array.shape[1:]
        in_specs.append(whole(shape, (first // blocks,) + (0,) * (array.ndim - 1)))
        operands.append(array)
        if array.dtype == BF16:
            products += blocks
    in_specs += [pl.BlockSpec(memory_space=pl.ANY)] * len(ties)
    operands += list(ties)
    out_specs = [tiled(lead) for lead, _ in outs]
    out_shape = [jax.ShapeDtypeStruct(tuple(lead) + (rows, width), kind) for lead, kind in outs]
    if sums:
        out_specs.append(pl.BlockSpec((sums, width), lambda i: (0, 0)))
        out_shape.append(jax.ShapeDtypeStruct((sums, width), F32))
    moved = sum(array.size * array.dtype.itemsize for array in operands)
    moved += sum(leaf.size * leaf.dtype.itemsize for leaf in out_shape)
    return pl.pallas_call(
        kernel,
        grid=(rows // tile,),
        in_specs=in_specs,
        out_specs=out_specs,
        out_shape=out_shape,
        compiler_params=pltpu.CompilerParams(vmem_limit_bytes=VMEM_LIMIT),
        cost_estimate=pl.CostEstimate(
            flops=3 * rows * width * width * products // COST_SCALE,
            bytes_accessed=moved // COST_SCALE,
            transcendentals=0,
        ),
    )(*operands)


def row_major(values):
    return with_layout_constraint(values, Layout(major_to_minor=tuple(range(values.ndim))))


def swap(values, axis, offset):
    count = lax.axis_size(axis)
    return lax.ppermute(values, axis, [(index, index ^ offset) for index in range(count)])


def after(values, *earlier):
    return lax.optimization_barrier((values, *earlier))


def held(values, *earlier):
    wrong = jnp.zeros((), jnp.bool_)
    for array in earlier:
        entry = array[(0,) * array.ndim]
        wrong = wrong | (entry != entry)
    return jnp.where(wrong, jnp.zeros_like(values), values)


def pick(bit, on_zero, on_one):
    return jnp.where(bit == 0, on_zero, on_one)


def to_sequences(values, count, *earlier):
    seqs, local, width = values.shape
    own = lax.axis_index("ctx")
    parts = values.reshape(count, seqs // count, local, width)
    pieces = []
    for offset in range(count):
        piece = lax.dynamic_index_in_dim(parts, own ^ offset, keepdims=False)
        if earlier:
            piece = held(piece, *earlier)
        pieces.append(swap(piece, "ctx", offset) if offset else piece)
    return row_major(jnp.stack(pieces))


def to_blocks(values, kind, *earlier):
    count, share, local, width = values.shape
    own = lax.axis_index("ctx")
    out = row_major(jnp.zeros((count, share, local, width), kind))
    for offset in range(count):
        piece = values[offset]
        if earlier:
            piece = held(piece, *earlier)
        piece = row_major(piece)
        if offset:
            piece = row_major(swap(piece, "ctx", offset))
        out = lax.dynamic_update_index_in_dim(out, piece.astype(kind), own ^ offset, 0)
    return row_major(out).reshape(count * share, local, width)


class Windows:
    def __init__(self, owned_rows):
        tiles = owned_rows // 16
        self.start = tiles // 2 * 16
        self.size = owned_rows - self.start
        ctx = lax.axis_index("ctx")
        self.core = ctx % 2
        self.y = ctx // 2
        self.x = lax.axis_index("replica")

    def rows(self, values):
        return pick(
            self.core, values[..., : self.size, :], values[..., self.start :, :]
        )

    def other_rows(self, values):
        return pick(
            self.core, values[..., self.start :, :], values[..., : self.size, :]
        )

    def block(self, blocks):
        return pick(
            self.x,
            pick(self.y, blocks[0], blocks[1]),
            pick(self.y, blocks[2], blocks[3]),
        )


def assemble_kernel(groups, start, size, transposed, here_ref, *refs):
    arrays, out_ref = refs[:-1], refs[-1]
    x, y, core = here_ref[0], here_ref[1], here_ref[2]
    for turn in range(2):
        row = pl.multiple_of((core ^ turn) * start, 16)
        for (places, first), ref in zip(groups, arrays[turn * len(groups) :]):
            for i, (dx, dy) in enumerate(places):
                block = 2 * (x ^ dx) + (y ^ dy)
                for s in range(ref.shape[1]):
                    place = (first + s, block) if transposed else (block, first + s)
                    out_ref[place + (pl.ds(row, size), slice(None))] = ref[
                        i, s, :size, :
                    ].astype(out_ref.dtype)


def assemble(win, groups, own, other, owned_rows, shards, transposed, kind):
    width = own[0].shape[-1]
    here = jnp.stack([win.x, win.y, win.core]).astype(jnp.int32)
    shape = (shards, 4, owned_rows, width) if transposed else (4, shards, owned_rows, width)
    return pl.pallas_call(
        functools.partial(assemble_kernel, groups, win.start, win.size, transposed),
        in_specs=[pl.BlockSpec(memory_space=pltpu.SMEM)]
        + [pl.BlockSpec(memory_space=pltpu.VMEM)] * (2 * len(groups)),
        out_specs=pl.BlockSpec(memory_space=pltpu.VMEM),
        out_shape=jax.ShapeDtypeStruct(shape, kind),
        compiler_params=pltpu.CompilerParams(vmem_limit_bytes=VMEM_LIMIT),
        cost_estimate=pl.CostEstimate(
            flops=0, bytes_accessed=16 * shards * owned_rows * width, transcendentals=0
        ),
    )(here, *own, *other)


def spread_chips(mine, hold=()):
    shards = mine.shape[0]
    if shards == 1:
        first = jnp.stack([mine, swap(mine, "replica", 1)])
        return [first, swap(first, "ctx", 2)]
    split = shards // 2
    low, high = mine[:split], mine[split:]
    low_there, high_there = after(swap(low, "replica", 1), swap(high, "ctx", 2))
    first = held(jnp.stack([low, low_there]), *hold)
    second = held(jnp.stack([high, high_there]), *hold)
    return [first, second, swap(first, "ctx", 2), swap(second, "replica", 1)]


def chip_groups(shards):
    if shards == 1:
        return ((((0, 0), (1, 0)), 0), (((0, 1), (1, 1)), 0))
    return (
        (((0, 0), (1, 0)), 0),
        (((0, 0), (0, 1)), shards // 2),
        (((0, 1), (1, 1)), 0),
        (((1, 0), (1, 1)), shards // 2),
    )


def spread_cores(own):
    return [swap(array, "ctx", 1) for array in own]


def place(win, own, other, owned_rows, shards, transposed=False, kind=BF16):
    return assemble(win, chip_groups(shards), own, other, owned_rows, shards, transposed, kind)


def add_pair(kept, received):
    return (kept.astype(F32) + received.astype(F32)).astype(BF16)


def corner(values):
    return values[(0,) * (values.ndim - 2)][:16, :LANES]


def reduce_first(win, grads, transposed):
    shards = grads.shape[0 if transposed else 1]
    split = shards // 2

    def part(values, blocks, which):
        return values[which, blocks] if transposed else values[blocks, which]

    lower, upper = slice(None, split), slice(split, None)
    entry = lambda values, i: values[:, i] if transposed else values[i]
    received = swap(win.other_rows(grads), "ctx", 1)
    both = add_pair(win.rows(grads), received)
    by_x = [part(both, slice(2 * i, 2 * i + 2), lower) for i in range(2)]
    by_y = [part(both, slice(i, None, 2), upper) for i in range(2)]
    x_sent = row_major(pick(win.x, by_x[1], by_x[0]))
    y_sent = row_major(pick(win.y, by_y[1], by_y[0]))
    x_received, y_received = after(
        row_major(swap(x_sent, "replica", 1)), row_major(swap(y_sent, "ctx", 2))
    )
    low = row_major(add_pair(pick(win.x, *by_x), x_received))
    high = row_major(add_pair(pick(win.y, *by_y), y_received))
    low, high = [entry(low, i) for i in range(2)], [entry(high, i) for i in range(2)]
    return (low, high), [corner(x_sent), corner(y_sent)]


def reduce_second(win, halves, *earlier):
    low, high = halves
    low_sent, high_sent = pick(win.y, low[1], low[0]), pick(win.x, high[1], high[0])
    if earlier:
        low_sent, high_sent = held(low_sent, *earlier), held(high_sent, *earlier)
    low_received, high_received = after(
        swap(low_sent, "ctx", 2), swap(high_sent, "replica", 1)
    )
    low_sum = add_pair(pick(win.y, *low), low_received)
    high_sum = add_pair(pick(win.x, *high), high_received)
    sums = jnp.concatenate([low_sum, high_sum], axis=0)
    return sums, [corner(low_sent), corner(high_sent)], [corner(sums)]


def reduce_vectors(values):
    values = add_pair(values, swap(values, "ctx", 1))
    values = add_pair(values, swap(values, "replica", 1))
    values = add_pair(values, swap(values, "ctx", 2))
    step = 1
    while step < lax.axis_size("shard"):
        values = add_pair(values, swap(values, "shard", step))
        step *= 2
    return values


def per_device(
    tokens,
    cotangent,
    block_order,
    ln1_gain,
    ln1_bias,
    qkv_weight,
    q_bias,
    v_bias,
    out_weight,
    out_bias,
    ln2_gain,
    ln2_bias,
    fc_weight,
    fc_bias,
    proj_weight,
    proj_bias,
):
    seq_count, local_len, width = tokens.shape
    owned_rows = ln1_gain.shape[0]
    shards = width // owned_rows
    wide = fc_weight.shape[1] // width
    count = lax.axis_size("ctx")
    rows = seq_count * local_len
    pairwise = lax.axis_size("replica") == 2 and count == 4 and shards == 4
    win = Windows(owned_rows)

    vectors = jnp.concatenate(
        [ln1_gain, ln1_bias, q_bias, v_bias, out_bias, ln2_gain, ln2_bias, proj_bias, fc_bias]
    )
    vector_rows = vectors.shape[0] // width
    vector_tile = jnp.pad(vectors.reshape(vector_rows, width), ((0, -vector_rows % 16), (0, 0)))
    column = lambda values, i: values[:, i * width : (i + 1) * width]
    blocks_a = [column(qkv_weight, i) for i in range(3)] + [out_weight]
    blocks_b = [column(fc_weight, i) for i in range(wide)]
    blocks_c = [proj_weight[i * owned_rows : (i + 1) * owned_rows] for i in range(wide)]

    def gather_z(values):
        return lax.all_gather(values, "shard", axis=0, tiled=False)

    low_inputs = to_sequences(tokens, count).reshape(rows, width)

    if pairwise:
        mine = [win.rows(win.block(blocks)) for blocks in (blocks_a, blocks_b, blocks_c)]
        part_a = gather_z(mine[0])
        mine_b, part_a = after(jnp.concatenate([mine[1], vector_tile], axis=0), part_a)
        part_b = gather_z(mine_b)
        mine_c, part_b = after(mine[2], part_b)
        part_c = gather_z(mine_c)
        part_a, low_inputs = after(part_a, low_inputs)
        own_a = spread_chips(part_a)
        other_a = spread_cores(own_a)
        full_a = place(win, own_a, other_a, owned_rows, shards)
        vector_part = part_b[:, win.size : win.size + vector_rows]
        own_b = spread_chips(held(part_b[:, : win.size], *own_a[-2:]), hold=other_a)
    else:
        vector_part = gather_z(vector_tile)[:, :vector_rows]
        full_a, full_b, full_c = [
            gather_z(jnp.stack(blocks)) for blocks in (blocks_a, blocks_b, blocks_c)
        ]
        full_a, full_b = full_a.transpose(1, 0, 2, 3), full_b.transpose(1, 0, 2, 3)
    w_a = full_a.reshape(4, width, width)
    vector_part = vector_part.reshape(shards, vector_rows * width).astype(F32)
    small = vector_part[:, : 8 * owned_rows].reshape(shards, 8, owned_rows)
    small = small.transpose(1, 0, 2).reshape(8, width)
    bias_fc = vector_part[:, 8 * owned_rows :].reshape(wide, 1, width)

    share = seq_count // count
    blocked = (count, share, local_len, width)
    index = jnp.arange(count, dtype=jnp.int32)
    held_by = jnp.sum(jnp.where(block_order[None, :] == index[:, None], index[None, :], 0), axis=1)
    order = (held_by ^ lax.axis_index("ctx")).astype(jnp.int32)

    joined, low_one = by_rows(
        qkv_kernel, [low_inputs], [(w_a, 0, 3), small], [((3,), BF16), ((), BF16)]
    )
    joined = joined.reshape((3,) + blocked)
    if pairwise:
        other_b = spread_cores(own_b)
        full_b = place(win, own_b, other_b, owned_rows, shards)
        own_c = spread_chips(held(part_c, joined, *own_b[-2:]), hold=other_b)
        steps = [corner(array[1]) for array in own_c[:2]]
    else:
        steps = []
    mixed, lse = attention_forward(joined, order)
    attended = mixed.reshape(rows, width)
    middle, low_two = by_rows(
        attended_kernel,
        [low_inputs, attended],
        [(w_a, 3, 1), small],
        [((), F32), ((), BF16)],
        ties=steps,
    )
    w_fc = full_b.reshape(wide, width, width)
    low_act, slope = by_rows(
        hidden_kernel, [low_two], [w_fc, bias_fc], [((wide,), BF16), ((wide,), BF16)]
    )
    if pairwise:
        full_c = place(win, own_c, spread_cores(own_c), owned_rows, shards, transposed=True)
    w_proj = full_c.reshape(wide, width, width)
    low_grad_out = to_sequences(cotangent, count, *(own_b[-2:] if pairwise else ()))
    if pairwise:
        low_grad_out = held(low_grad_out, *own_c[-2:])
    low_grad_out = low_grad_out.reshape(rows, width)

    def finish_units(sums, *earlier):
        sums = lax.psum_scatter(sums, "shard", scatter_dimension=0, tiled=False)
        own = spread_chips(held(sums[None], *earlier))
        return place(win, own, spread_cores(own), owned_rows, 1, kind=F32)[:, 0]

    def reduce_whole(grads, transposed=False):
        if transposed:
            grads = grads.transpose(1, 0, 2, 3)
        full = lax.psum_scatter(grads, "shard", scatter_dimension=1, tiled=False)
        return lax.psum(full, ("replica", "ctx")).astype(F32)

    def start_units(grads, transposed=False):
        if not pairwise:
            return grads, ((), (), ())
        halves, first = reduce_first(win, grads, transposed)
        sums, second, last = reduce_second(win, halves)
        return sums, (first, second, last)

    def by_shard(grads):
        return grads.astype(BF16).reshape(4, shards, owned_rows, width)

    grad_proj = jnp.einsum("ctx,td->cxd", low_act, low_grad_out, preferred_element_type=F32)
    grad_proj = grad_proj.astype(BF16)
    partial_proj, proj_marks = start_units(by_shard(grad_proj), transposed=True)
    (outputs,) = by_rows(
        output_kernel,
        [middle, low_act],
        [w_proj, small],
        [((), BF16)],
        ties=[corner(grad_proj)],
    )
    grad_hidden, sums_hidden = by_rows(
        hidden_back_kernel,
        [low_grad_out, slope],
        [w_proj],
        [((wide,), BF16)],
        sums=8,
        ties=[corner(outputs), *proj_marks[0]],
    )
    grad_fc = jnp.einsum("td,ctx->cdx", low_two, grad_hidden, preferred_element_type=F32)
    grad_fc = grad_fc.astype(BF16)
    partial_fc, fc_marks = start_units(by_shard(grad_fc))
    grad_middle, low_grad_middle, grad_mixed, sums_middle = by_rows(
        middle_back_kernel,
        [grad_hidden, low_grad_out, middle],
        [w_fc, (w_a, 3, 1), small],
        [((), F32), ((), BF16), ((), BF16)],
        sums=8,
        ties=[corner(grad_fc), *proj_marks[1]],
    )
    layer_out = to_blocks(
        outputs.reshape(blocked), BF16, low_grad_middle, *proj_marks[2], *fc_marks[0]
    )
    grad_out_weight = dot_tn(attended, low_grad_middle).astype(BF16)
    grad_joined = attention_backward(
        joined,
        mixed,
        grad_mixed.reshape(blocked),
        lse,
        order,
        ties=[corner(grad_out_weight), *proj_marks[2], *fc_marks[0]],
    ).reshape(3, rows, width)
    grad_qkv = jnp.einsum("td,ctx->cdx", low_one, grad_joined, preferred_element_type=F32)
    grad_qkv = grad_qkv.astype(BF16)
    grads_a = jnp.concatenate([grad_qkv, grad_out_weight[None]], axis=0)
    partial_a, mark = by_shard(grads_a), ()
    if pairwise:
        halves, mark = reduce_first(win, partial_a, False)
    grad_inputs, sums_input = by_rows(
        input_back_kernel,
        [grad_joined, grad_middle, low_inputs],
        [(w_a, 0, 3), small],
        [((), BF16)],
        sums=8,
        ties=[corner(grad_qkv), *mark, *fc_marks[2]],
    )
    if pairwise:
        partial_a, _, _ = reduce_second(win, halves, grad_inputs)
    earlier = (partial_a,) if pairwise else ()
    input_grad = to_blocks(grad_inputs.reshape(blocked), F32, *earlier)

    small_grads = sums_middle + sums_input
    grad_fc_bias = sums_hidden[:wide]
    vector_grads = jnp.concatenate(
        [
            small_grads.reshape(8, shards, owned_rows)
            .transpose(1, 0, 2)
            .reshape(shards, 8 * owned_rows),
            grad_fc_bias.reshape(shards, owned_rows * wide),
        ],
        axis=1,
    ).astype(BF16)
    vector_grads = jnp.pad(
        vector_grads.reshape(shards, vector_rows, width),
        ((0, 0), (0, -vector_rows % 16), (0, 0)),
    )
    if pairwise:
        owned_proj = finish_units(partial_proj, grad_joined)
        owned_a = finish_units(partial_a)
        owned_fc = finish_units(partial_fc, partial_a)
        owned_vectors = lax.dynamic_index_in_dim(
            reduce_vectors(held(vector_grads, partial_a)),
            lax.axis_index("shard"),
            keepdims=False,
        )
    else:
        owned_proj = reduce_whole(partial_proj, transposed=True)
        owned_a, owned_fc = reduce_whole(partial_a), reduce_whole(partial_fc)
        owned_vectors = lax.psum_scatter(
            vector_grads, "shard", scatter_dimension=0, tiled=False
        )
        owned_vectors = lax.psum(owned_vectors, ("replica", "ctx"))
    owned_vectors = owned_vectors[:vector_rows].reshape(-1).astype(F32)
    vec = [owned_vectors[i * owned_rows : (i + 1) * owned_rows] for i in range(8)]
    qkv_grad = jnp.concatenate([owned_a[i] for i in range(3)], axis=1)
    fc_grad = jnp.concatenate([owned_fc[i] for i in range(wide)], axis=1)
    return (
        layer_out,
        input_grad,
        vec[0],
        vec[1],
        qkv_grad,
        vec[2],
        vec[3],
        owned_a[3],
        vec[4],
        vec[5],
        vec[6],
        fc_grad,
        owned_vectors[8 * owned_rows :],
        owned_proj.reshape(wide * owned_rows, width),
        vec[7],
    )


def solution(mesh):
    vector, matrix = P("shard"), P("shard", None)
    rows = P(("shard", "replica"), "ctx", None)
    weights = (
        vector,
        vector,
        matrix,
        vector,
        vector,
        matrix,
        vector,
        vector,
        vector,
        matrix,
        vector,
        matrix,
        vector,
    )
    return jax.shard_map(
        per_device,
        mesh=mesh,
        in_specs=(rows, rows, P()) + weights,
        out_specs=(rows, rows) + weights,
        check_vma=False,
    )
```

```python
import functools

import jax
import jax.numpy as jnp
from jax import lax
from jax.experimental import pallas as pl
from jax.experimental.layout import Layout, with_layout_constraint
from jax.experimental.pallas import tpu as pltpu
from jax.sharding import PartitionSpec as P

HEAD_DIM = 64
EPSILON = 1e-05
LANES = 128
VMEM_LIMIT = 56 * 1024 * 1024
COST_SCALE = 8

BF16 = jnp.bfloat16
F32 = jnp.float32


def dot_nn(left, right):
    return lax.dot_general(left, right, (((1,), (0,)), ((), ())), preferred_element_type=F32)


def dot_nt(left, right):
    return lax.dot_general(left, right, (((1,), (1,)), ((), ())), preferred_element_type=F32)


def dot_tn(left, right):
    return lax.dot_general(left, right, (((0,), (0,)), ((), ())), preferred_element_type=F32)


def head_lanes(shape, which):
    lane = lax.broadcasted_iota(jnp.int32, shape, 1)
    return (lane < HEAD_DIM) if which == 0 else (lane >= HEAD_DIM)


def only_valid(values, width):
    if width % LANES == 0:
        return values
    lane = lax.broadcasted_iota(jnp.int32, values.shape, 1) + pl.program_id(1) * LANES
    return jnp.where(lane < width, values, jnp.zeros_like(values))


def sorted_rows(ref, lead, order_ref, first, last):
    return jnp.concatenate([ref[lead + (order_ref[i], 0)] for i in range(first, last)], axis=0)


def store_rows(ref, lead, order_ref, first, rows):
    local = ref.shape[-2]
    for i in range(rows.shape[0] // local):
        ref[lead + (order_ref[first + i], 0)] = rows[i * local : (i + 1) * local]


def causal(rows, columns):
    key_at = lax.broadcasted_iota(jnp.int32, (rows, columns), 0)
    query_at = lax.broadcasted_iota(jnp.int32, (rows, columns), 1)
    return key_at <= query_at


def attention_forward_kernel(blocks, width, order_ref, q_ref, k_ref, v_ref, *refs):
    o_ref, lse_ref = refs[-2:]
    count, local = k_ref.shape[1], k_ref.shape[3]
    tile = blocks * local
    keys = only_valid(sorted_rows(k_ref, (0,), order_ref, 0, count), width)
    values_t = sorted_rows(v_ref, (0,), order_ref, 0, count).astype(F32).T.astype(BF16)
    diagonal = causal(tile, tile)
    for first in range(0, count, blocks):
        start, stop = first * local, (first + blocks) * local
        queries = sorted_rows(q_ref, (0,), order_ref, first, first + blocks)
        queries = queries * jnp.asarray(HEAD_DIM**-0.5, BF16)
        pieces = []
        for which in range(2):
            masked_q = jnp.where(head_lanes(queries.shape, which), queries, jnp.zeros_like(queries))
            scores = dot_nt(keys[:stop], masked_q)
            tiles = []
            if start > 0:
                tiles.append(scores[:start])
            tiles.append(jnp.where(diagonal, scores[start:], -1e30))
            top = functools.reduce(
                jnp.maximum, [jnp.max(block, axis=0, keepdims=True) for block in tiles]
            )
            weights = [jnp.exp(block - top) for block in tiles]
            total = sum(jnp.sum(weight, axis=0, keepdims=True) for weight in weights)
            low = jnp.concatenate([weight.astype(BF16) for weight in weights], axis=0)
            rows = values_t[which * HEAD_DIM : (which + 1) * HEAD_DIM, :stop]
            pieces.append(dot_nn(rows, low) * (1.0 / total))
            lse_ref[0, 0, which : which + 1, start:stop] = top + jnp.log(total)
        mixed_t = jnp.concatenate(pieces, axis=0)
        store_rows(o_ref, (), order_ref, first, mixed_t.T.astype(BF16))


def attention_backward_kernel(
    blocks,
    width,
    order_ref,
    q_ref,
    k_ref,
    v_ref,
    o_ref,
    do_ref,
    lse_ref,
    *refs,
):
    out_ref, dk_acc, dv_acc = refs[-3:]
    count, local = k_ref.shape[1], k_ref.shape[3]
    tile = blocks * local
    keys = only_valid(sorted_rows(k_ref, (0,), order_ref, 0, count), width)
    values = only_valid(sorted_rows(v_ref, (0,), order_ref, 0, count), width)
    keys_t = keys.astype(F32).T.astype(BF16)
    diagonal = causal(tile, tile)
    for first in range(0, count, blocks):
        start, stop = first * local, (first + blocks) * local
        queries = sorted_rows(q_ref, (0,), order_ref, first, first + blocks)
        queries = queries * jnp.asarray(HEAD_DIM**-0.5, BF16)
        grads = sorted_rows(do_ref, (), order_ref, first, first + blocks)
        mixed = sorted_rows(o_ref, (), order_ref, first, first + blocks)
        product_t = (grads.astype(F32) * mixed.astype(F32)).T
        key_lanes = head_lanes((stop, LANES), 0)
        dq_parts, dk_parts, dv_parts = [], [], []
        for which in range(2):
            mine = head_lanes(queries.shape, which)
            masked_q = jnp.where(mine, queries, jnp.zeros_like(queries))
            masked_g = jnp.where(mine, grads, jnp.zeros_like(grads))
            delta = jnp.sum(
                product_t[which * HEAD_DIM : (which + 1) * HEAD_DIM], axis=0, keepdims=True
            )
            lse = lse_ref[0, 0, which : which + 1, start:stop]
            scores = dot_nt(keys[:stop], masked_q)
            grad_weights = dot_nt(values[:stop], masked_g)
            weights = jnp.exp(scores - lse)
            if start > 0:
                weights = jnp.concatenate(
                    [weights[:start], jnp.where(diagonal, weights[start:], 0.0)], axis=0
                )
            else:
                weights = jnp.where(diagonal, weights, 0.0)
            low_scores = (weights * (grad_weights - delta)).astype(BF16)
            dv_parts.append(dot_nn(weights.astype(BF16), grads))
            dk_parts.append(dot_nn(low_scores, queries))
            dq_parts.append(
                dot_nn(keys_t[which * HEAD_DIM : (which + 1) * HEAD_DIM, :stop], low_scores)
            )
        dq_t = jnp.concatenate(dq_parts, axis=0) * (HEAD_DIM**-0.5)
        store_rows(out_ref, (0,), order_ref, first, dq_t.T.astype(BF16))
        dk = jnp.where(key_lanes, dk_parts[0], dk_parts[1])
        dv = jnp.where(key_lanes, dv_parts[0], dv_parts[1])
        if start > 0:
            dk_acc[:start] += dk[:start]
            dv_acc[:start] += dv[:start]
        dk_acc[start:stop] = dk[start:]
        dv_acc[start:stop] = dv[start:]
    store_rows(out_ref, (1,), order_ref, 0, dk_acc[...].astype(BF16))
    store_rows(out_ref, (2,), order_ref, 0, dv_acc[...].astype(BF16))


def query_blocks(count):
    return 2 if count % 2 == 0 else 1


def attention_forward(joined, order, ties=()):
    _, count, seqs, local, width = joined.shape
    length = count * local
    pairs = pl.cdiv(width, LANES)
    spec = lambda which: pl.BlockSpec(
        (1, count, 1, local, LANES), lambda s, h, order: (which, 0, s, 0, h)
    )
    return pl.pallas_call(
        functools.partial(attention_forward_kernel, query_blocks(count), width),
        grid_spec=pltpu.PrefetchScalarGridSpec(
            num_scalar_prefetch=1,
            grid=(seqs, pairs),
            in_specs=[spec(0), spec(1), spec(2)]
            + [pl.BlockSpec(memory_space=pl.ANY)] * len(ties),
            out_specs=[
                pl.BlockSpec((count, 1, local, LANES), lambda s, h, order: (0, s, 0, h)),
                pl.BlockSpec((1, 1, 8, length), lambda s, h, order: (s, h, 0, 0)),
            ],
        ),
        out_shape=[
            jax.ShapeDtypeStruct((count, seqs, local, width), BF16),
            jax.ShapeDtypeStruct((seqs, pairs, 8, length), F32),
        ],
        compiler_params=pltpu.CompilerParams(vmem_limit_bytes=VMEM_LIMIT),
        cost_estimate=pl.CostEstimate(
            flops=seqs * pairs * 16 * length * length * LANES // COST_SCALE,
            bytes_accessed=8 * seqs * length * width // COST_SCALE,
            transcendentals=0,
        ),
    )(order, joined, joined, joined, *ties)


def attention_backward(joined, mixed, grad_mixed, lse, order, ties=()):
    _, count, seqs, local, width = joined.shape
    length = count * local
    pairs = pl.cdiv(width, LANES)
    spec = lambda which: pl.BlockSpec(
        (1, count, 1, local, LANES), lambda s, h, order: (which, 0, s, 0, h)
    )
    rows = pl.BlockSpec((count, 1, local, LANES), lambda s, h, order: (0, s, 0, h))
    return pl.pallas_call(
        functools.partial(attention_backward_kernel, query_blocks(count), width),
        grid_spec=pltpu.PrefetchScalarGridSpec(
            num_scalar_prefetch=1,
            grid=(seqs, pairs),
            in_specs=[
                spec(0),
                spec(1),
                spec(2),
                rows,
                rows,
                pl.BlockSpec((1, 1, 8, length), lambda s, h, order: (s, h, 0, 0)),
            ]
            + [pl.BlockSpec(memory_space=pl.ANY)] * len(ties),
            out_specs=pl.BlockSpec(
                (3, count, 1, local, LANES), lambda s, h, order: (0, 0, s, 0, h)
            ),
            scratch_shapes=[pltpu.VMEM((length, LANES), F32), pltpu.VMEM((length, LANES), F32)],
        ),
        out_shape=jax.ShapeDtypeStruct(joined.shape, BF16),
        compiler_params=pltpu.CompilerParams(vmem_limit_bytes=VMEM_LIMIT),
        cost_estimate=pl.CostEstimate(
            flops=seqs * pairs * 20 * length * length * LANES // COST_SCALE,
            bytes_accessed=16 * seqs * length * width // COST_SCALE,
            transcendentals=0,
        ),
    )(order, joined, joined, joined, mixed, grad_mixed, lse, *ties)


def standardize(values):
    centred = values - jnp.mean(values, axis=-1, keepdims=True)
    inverse = lax.rsqrt(jnp.mean(centred * centred, axis=-1, keepdims=True) + EPSILON)
    return centred * inverse, inverse


def normalize_back(grad_out, standard, inverse, gain):
    scaled = grad_out * gain
    return inverse * (
        scaled
        - jnp.mean(scaled, axis=-1, keepdims=True)
        - standard * jnp.mean(scaled * standard, axis=-1, keepdims=True)
    )


def add_row(sums_ref, row, values):
    sums_ref[row : row + 1, :] += jnp.sum(values, axis=0, keepdims=True)


def clear_first(sums_ref):
    @pl.when(pl.program_id(0) == 0)
    def _():
        sums_ref[...] = jnp.zeros_like(sums_ref)


G_ONE, B_ONE, BIAS_Q, BIAS_V, BIAS_OUT, G_TWO, B_TWO, BIAS_PROJ = range(8)


def row(small_ref, index):
    return small_ref[index : index + 1, :]


def qkv_kernel(x_ref, w_ref, small_ref, joined_ref, low_ref):
    standard, _ = standardize(x_ref[...].astype(F32))
    low = (standard * row(small_ref, G_ONE) + row(small_ref, B_ONE)).astype(BF16)
    low_ref[...] = low
    for which, bias in enumerate((BIAS_Q, None, BIAS_V)):
        out = dot_nn(low, w_ref[which])
        if bias is not None:
            out = out + row(small_ref, bias)
        joined_ref[which] = out.astype(BF16)


def attended_kernel(x_ref, o_ref, w_ref, small_ref, *refs):
    middle_ref, low_ref = refs[-2:]
    middle = x_ref[...].astype(F32) + dot_nn(o_ref[...], w_ref[0]) + row(small_ref, BIAS_OUT)
    middle_ref[...] = middle
    standard, _ = standardize(middle)
    low_ref[...] = (standard * row(small_ref, G_TWO) + row(small_ref, B_TWO)).astype(BF16)


def hidden_kernel(low_ref, w_ref, bias_ref, *refs):
    act_ref, slope_ref = refs[-2:]
    low = low_ref[...]
    scale = 0.7978845608028654
    for which in range(w_ref.shape[0]):
        hidden = dot_nn(low, w_ref[which]) + bias_ref[which]
        square = hidden * hidden
        bent = jnp.tanh(scale * hidden * (1.0 + 0.044715 * square))
        half = 0.5 * (1.0 + bent)
        act_ref[which] = (hidden * half).astype(BF16)
        slope = half + 0.5 * hidden * (1.0 - bent * bent) * (
            scale * (1.0 + 3.0 * 0.044715 * square)
        )
        slope_ref[which] = slope.astype(BF16)


def output_kernel(middle_ref, act_ref, w_ref, small_ref, *refs):
    out_ref = refs[-1]
    total = middle_ref[...] + row(small_ref, BIAS_PROJ)
    for which in range(w_ref.shape[0]):
        total += dot_nn(act_ref[which], w_ref[which])
    out_ref[...] = total.astype(BF16)


def hidden_back_kernel(grad_ref, slope_ref, w_ref, *refs):
    out_ref, sums_ref = refs[-2:]
    clear_first(sums_ref)
    grad = grad_ref[...]
    for which in range(w_ref.shape[0]):
        back = dot_nt(grad, w_ref[which]) * slope_ref[which].astype(F32)
        low = back.astype(BF16)
        out_ref[which] = low
        add_row(sums_ref, which, low.astype(F32))


def middle_back_kernel(hidden_ref, grad_ref, middle_ref, w_ref, out_w_ref, small_ref, *refs):
    grad_middle_ref, low_ref, mixed_ref, sums_ref = refs[-4:]
    clear_first(sums_ref)
    grad_two = dot_nt(hidden_ref[0], w_ref[0])
    for which in range(1, w_ref.shape[0]):
        grad_two += dot_nt(hidden_ref[which], w_ref[which])
    standard, inverse = standardize(middle_ref[...])
    grad_out = grad_ref[...].astype(F32)
    grad_middle = grad_out + normalize_back(grad_two, standard, inverse, row(small_ref, G_TWO))
    low = grad_middle.astype(BF16)
    grad_middle_ref[...] = grad_middle
    low_ref[...] = low
    mixed_ref[...] = dot_nt(low, out_w_ref[0]).astype(BF16)
    add_row(sums_ref, G_TWO, grad_two * standard)
    add_row(sums_ref, B_TWO, grad_two)
    add_row(sums_ref, BIAS_OUT, low.astype(F32))
    add_row(sums_ref, BIAS_PROJ, grad_out)


def input_back_kernel(joined_ref, grad_middle_ref, x_ref, w_ref, small_ref, *refs):
    out_ref, sums_ref = refs[-2:]
    clear_first(sums_ref)
    grad_one = dot_nt(joined_ref[0], w_ref[0])
    for which in range(1, 3):
        grad_one += dot_nt(joined_ref[which], w_ref[which])
    standard, inverse = standardize(x_ref[...].astype(F32))
    back = normalize_back(grad_one, standard, inverse, row(small_ref, G_ONE))
    out_ref[...] = (grad_middle_ref[...] + back).astype(BF16)
    add_row(sums_ref, G_ONE, grad_one * standard)
    add_row(sums_ref, B_ONE, grad_one)
    add_row(sums_ref, BIAS_Q, joined_ref[0].astype(F32))
    add_row(sums_ref, BIAS_V, joined_ref[2].astype(F32))


def by_rows(kernel, by_row, fixed, outs, sums=None, ties=(), tile=256):
    rows, width = by_row[0].shape[-2:]
    tile = tile if rows % tile == 0 else rows
    whole = lambda shape, index: pl.BlockSpec(
        shape, lambda i: index, pipeline_mode=pl.Buffered(buffer_count=1)
    )
    tiled = lambda lead: pl.BlockSpec(
        tuple(lead) + (tile, width), lambda i: (0,) * len(lead) + (i, 0)
    )
    in_specs = [tiled(array.shape[:-2]) for array in by_row]
    operands = list(by_row)
    products = 0
    for entry in fixed:
        array, first, blocks = entry if isinstance(entry, tuple) else (entry, 0, entry.shape[0])
        shape = (blocks,) + array.shape[1:]
        in_specs.append(whole(shape, (first // blocks,) + (0,) * (array.ndim - 1)))
        operands.append(array)
        if array.dtype == BF16:
            products += blocks
    in_specs += [pl.BlockSpec(memory_space=pl.ANY)] * len(ties)
    operands += list(ties)
    out_specs = [tiled(lead) for lead, _ in outs]
    out_shape = [jax.ShapeDtypeStruct(tuple(lead) + (rows, width), kind) for lead, kind in outs]
    if sums:
        out_specs.append(pl.BlockSpec((sums, width), lambda i: (0, 0)))
        out_shape.append(jax.ShapeDtypeStruct((sums, width), F32))
    moved = sum(array.size * array.dtype.itemsize for array in operands)
    moved += sum(leaf.size * leaf.dtype.itemsize for leaf in out_shape)
    return pl.pallas_call(
        kernel,
        grid=(rows // tile,),
        in_specs=in_specs,
        out_specs=out_specs,
        out_shape=out_shape,
        compiler_params=pltpu.CompilerParams(vmem_limit_bytes=VMEM_LIMIT),
        cost_estimate=pl.CostEstimate(
            flops=3 * rows * width * width * products // COST_SCALE,
            bytes_accessed=moved // COST_SCALE,
            transcendentals=0,
        ),
    )(*operands)


def row_major(values):
    return with_layout_constraint(values, Layout(major_to_minor=tuple(range(values.ndim))))


def swap(values, axis, offset):
    count = lax.axis_size(axis)
    return lax.ppermute(values, axis, [(index, index ^ offset) for index in range(count)])


def after(values, *earlier):
    return lax.optimization_barrier((values, *earlier))


def held(values, *earlier):
    wrong = jnp.zeros((), jnp.bool_)
    for array in earlier:
        entry = array[(0,) * array.ndim]
        wrong = wrong | (entry != entry)
    return jnp.where(wrong, jnp.zeros_like(values), values)


def pick(bit, on_zero, on_one):
    return jnp.where(bit == 0, on_zero, on_one)


def to_sequences(values, count, *earlier):
    seqs, local, width = values.shape
    own = lax.axis_index("ctx")
    parts = values.swapaxes(1, 2).reshape(count, seqs // count, width, local)
    pieces = []
    for offset in range(count):
        piece = lax.dynamic_index_in_dim(parts, own ^ offset, keepdims=False)
        if earlier:
            piece = held(piece, *earlier)
        pieces.append(row_major(swap(row_major(piece), "ctx", offset)) if offset else piece)
    return row_major(row_major(jnp.stack(pieces)).swapaxes(2, 3))


def to_blocks(values, kind, *earlier):
    count, share, local, width = values.shape
    own = lax.axis_index("ctx")
    values = values.swapaxes(2, 3)
    if earlier:
        values = held(values, *earlier)
    values = row_major(values)
    out = row_major(jnp.zeros((count, share, width, local), kind))
    for offset in range(count):
        piece = row_major(values[offset])
        if offset:
            piece = row_major(swap(piece, "ctx", offset))
        out = lax.dynamic_update_index_in_dim(out, piece.astype(kind), own ^ offset, 0)
    return row_major(out).reshape(count * share, width, local).swapaxes(1, 2)


class Windows:
    def __init__(self, owned_rows):
        tiles = owned_rows // 16
        self.start = tiles // 2 * 16
        self.size = owned_rows - self.start
        ctx = lax.axis_index("ctx")
        self.core = ctx % 2
        self.y = ctx // 2
        self.x = lax.axis_index("replica")

    def rows(self, values):
        return pick(
            self.core, values[..., : self.size, :], values[..., self.start :, :]
        )

    def other_rows(self, values):
        return pick(
            self.core, values[..., self.start :, :], values[..., : self.size, :]
        )

    def block(self, blocks):
        return pick(
            self.x,
            pick(self.y, blocks[0], blocks[1]),
            pick(self.y, blocks[2], blocks[3]),
        )


def assemble_kernel(groups, start, size, transposed, here_ref, *refs):
    arrays, out_ref = refs[:-1], refs[-1]
    x, y, core = here_ref[0], here_ref[1], here_ref[2]
    for turn in range(2):
        row = pl.multiple_of((core ^ turn) * start, 16)
        for (places, first), ref in zip(groups, arrays[turn * len(groups) :]):
            for i, (dx, dy) in enumerate(places):
                block = 2 * (x ^ dx) + (y ^ dy)
                for s in range(ref.shape[1]):
                    place = (first + s, block) if transposed else (block, first + s)
                    out_ref[place + (pl.ds(row, size), slice(None))] = ref[
                        i, s, :size, :
                    ].astype(out_ref.dtype)


def assemble(win, groups, own, other, owned_rows, shards, transposed, kind):
    width = own[0].shape[-1]
    here = jnp.stack([win.x, win.y, win.core]).astype(jnp.int32)
    shape = (shards, 4, owned_rows, width) if transposed else (4, shards, owned_rows, width)
    return pl.pallas_call(
        functools.partial(assemble_kernel, groups, win.start, win.size, transposed),
        in_specs=[pl.BlockSpec(memory_space=pltpu.SMEM)]
        + [pl.BlockSpec(memory_space=pltpu.VMEM)] * (2 * len(groups)),
        out_specs=pl.BlockSpec(memory_space=pltpu.VMEM),
        out_shape=jax.ShapeDtypeStruct(shape, kind),
        compiler_params=pltpu.CompilerParams(vmem_limit_bytes=VMEM_LIMIT),
        cost_estimate=pl.CostEstimate(
            flops=0, bytes_accessed=16 * shards * owned_rows * width, transcendentals=0
        ),
    )(here, *own, *other)


def spread_chips(mine, hold=()):
    shards = mine.shape[0]
    if shards == 1:
        first = jnp.stack([mine, swap(mine, "replica", 1)])
        return [first, swap(first, "ctx", 2)]
    split = shards // 2
    low, high = mine[:split], mine[split:]
    low_there, high_there = after(swap(low, "replica", 1), swap(high, "ctx", 2))
    first = held(jnp.stack([low, low_there]), *hold)
    second = held(jnp.stack([high, high_there]), *hold)
    return [first, second, swap(first, "ctx", 2), swap(second, "replica", 1)]


def chip_groups(shards):
    if shards == 1:
        return ((((0, 0), (1, 0)), 0), (((0, 1), (1, 1)), 0))
    return (
        (((0, 0), (1, 0)), 0),
        (((0, 0), (0, 1)), shards // 2),
        (((0, 1), (1, 1)), 0),
        (((1, 0), (1, 1)), shards // 2),
    )


def spread_cores(own):
    return [swap(array, "ctx", 1) for array in own]


def place(win, own, other, owned_rows, shards, transposed=False, kind=BF16):
    return assemble(win, chip_groups(shards), own, other, owned_rows, shards, transposed, kind)


def add_pair(kept, received):
    return (kept.astype(F32) + received.astype(F32)).astype(BF16)


def corner(values):
    return values[(0,) * (values.ndim - 2)][:16, :LANES]


def reduce_first(win, grads, transposed):
    shards = grads.shape[0 if transposed else 1]
    split = shards // 2

    def part(values, blocks, which):
        return values[which, blocks] if transposed else values[blocks, which]

    lower, upper = slice(None, split), slice(split, None)
    entry = lambda values, i: values[:, i] if transposed else values[i]
    received = swap(win.other_rows(grads), "ctx", 1)
    both = add_pair(win.rows(grads), received)
    by_x = [part(both, slice(2 * i, 2 * i + 2), lower) for i in range(2)]
    by_y = [part(both, slice(i, None, 2), upper) for i in range(2)]
    x_sent = row_major(pick(win.x, by_x[1], by_x[0]))
    y_sent = row_major(pick(win.y, by_y[1], by_y[0]))
    x_received, y_received = after(
        row_major(swap(x_sent, "replica", 1)), row_major(swap(y_sent, "ctx", 2))
    )
    low = row_major(add_pair(pick(win.x, *by_x), x_received))
    high = row_major(add_pair(pick(win.y, *by_y), y_received))
    low, high = [entry(low, i) for i in range(2)], [entry(high, i) for i in range(2)]
    return (low, high), [corner(x_sent), corner(y_sent)]


def reduce_second(win, halves, *earlier):
    low, high = halves
    low_sent, high_sent = pick(win.y, low[1], low[0]), pick(win.x, high[1], high[0])
    if earlier:
        low_sent, high_sent = held(low_sent, *earlier), held(high_sent, *earlier)
    low_received, high_received = after(
        swap(low_sent, "ctx", 2), swap(high_sent, "replica", 1)
    )
    low_sum = add_pair(pick(win.y, *low), low_received)
    high_sum = add_pair(pick(win.x, *high), high_received)
    sums = jnp.concatenate([low_sum, high_sum], axis=0)
    return sums, [corner(low_sent)], [corner(sums)]


def reduce_vectors(values):
    values = add_pair(values, swap(values, "ctx", 1))
    values = add_pair(values, swap(values, "replica", 1))
    values = add_pair(values, swap(values, "ctx", 2))
    step = 1
    while step < lax.axis_size("shard"):
        values = add_pair(values, swap(values, "shard", step))
        step *= 2
    return values


def per_device(
    tokens,
    cotangent,
    block_order,
    ln1_gain,
    ln1_bias,
    qkv_weight,
    q_bias,
    v_bias,
    out_weight,
    out_bias,
    ln2_gain,
    ln2_bias,
    fc_weight,
    fc_bias,
    proj_weight,
    proj_bias,
):
    seq_count, local_len, width = tokens.shape
    owned_rows = ln1_gain.shape[0]
    shards = width // owned_rows
    wide = fc_weight.shape[1] // width
    count = lax.axis_size("ctx")
    rows = seq_count * local_len
    pairwise = lax.axis_size("replica") == 2 and count == 4 and shards == 4
    win = Windows(owned_rows)

    vectors = jnp.concatenate(
        [ln1_gain, ln1_bias, q_bias, v_bias, out_bias, ln2_gain, ln2_bias, proj_bias, fc_bias]
    )
    vector_rows = vectors.shape[0] // width
    vector_tile = jnp.pad(vectors.reshape(vector_rows, width), ((0, -vector_rows % 16), (0, 0)))
    column = lambda values, i: values[:, i * width : (i + 1) * width]
    blocks_a = [column(qkv_weight, i) for i in range(3)] + [out_weight]
    blocks_b = [column(fc_weight, i) for i in range(wide)]
    blocks_c = [proj_weight[i * owned_rows : (i + 1) * owned_rows] for i in range(wide)]

    def gather_z(values):
        return lax.all_gather(values, "shard", axis=0, tiled=False)

    low_inputs = to_sequences(tokens, count).reshape(rows, width)

    if pairwise:
        mine = [win.rows(win.block(blocks)) for blocks in (blocks_a, blocks_b, blocks_c)]
        part_a = gather_z(mine[0])
        mine_b, part_a = after(jnp.concatenate([mine[1], vector_tile], axis=0), part_a)
        part_b = gather_z(mine_b)
        mine_c, part_b = after(mine[2], part_b)
        part_c = gather_z(mine_c)
        part_a, low_inputs = after(part_a, low_inputs)
        own_a = spread_chips(part_a)
        other_a = spread_cores(own_a)
        full_a = place(win, own_a, other_a, owned_rows, shards)
        vector_part = part_b[:, win.size : win.size + vector_rows]
        own_b = spread_chips(held(part_b[:, : win.size], own_a[2]), hold=[full_a])
    else:
        vector_part = gather_z(vector_tile)[:, :vector_rows]
        full_a, full_b, full_c = [
            gather_z(jnp.stack(blocks)) for blocks in (blocks_a, blocks_b, blocks_c)
        ]
        full_a, full_b = full_a.transpose(1, 0, 2, 3), full_b.transpose(1, 0, 2, 3)
    w_a = full_a.reshape(4, width, width)
    vector_part = vector_part.reshape(shards, vector_rows * width).astype(F32)
    small = vector_part[:, : 8 * owned_rows].reshape(shards, 8, owned_rows)
    small = small.transpose(1, 0, 2).reshape(8, width)
    bias_fc = vector_part[:, 8 * owned_rows :].reshape(wide, 1, width)

    share = seq_count // count
    blocked = (count, share, local_len, width)
    index = jnp.arange(count, dtype=jnp.int32)
    held_by = jnp.sum(jnp.where(block_order[None, :] == index[:, None], index[None, :], 0), axis=1)
    order = (held_by ^ lax.axis_index("ctx")).astype(jnp.int32)

    joined, low_one = by_rows(
        qkv_kernel, [low_inputs], [(w_a, 0, 3), small], [((3,), BF16), ((), BF16)]
    )
    joined = joined.reshape((3,) + blocked)
    if pairwise:
        other_b = spread_cores(own_b)
        full_b = place(win, own_b, other_b, owned_rows, shards)
        own_c = spread_chips(held(part_c, joined), hold=[full_b])
        steps = [corner(own_c[0][1]), corner(own_c[1][1]), corner(own_c[2]), corner(own_c[3])]
    else:
        steps = [corner(joined[0, 0])] * 4
    mixed, lse = attention_forward(joined, order, ties=steps[:2])
    attended = mixed.reshape(rows, width)
    middle, low_two = by_rows(
        attended_kernel,
        [low_inputs, attended],
        [(w_a, 3, 1), small],
        [((), F32), ((), BF16)],
    )
    w_fc = full_b.reshape(wide, width, width)
    low_act, slope = by_rows(
        hidden_kernel,
        [low_two],
        [w_fc, bias_fc],
        [((wide,), BF16), ((wide,), BF16)],
        ties=steps[2:],
    )
    if pairwise:
        full_c = place(win, own_c, spread_cores(own_c), owned_rows, shards, transposed=True)
    w_proj = full_c.reshape(wide, width, width)
    low_grad_out = to_sequences(cotangent, count, joined).reshape(rows, width)

    def finish_units(sums, *earlier):
        sums = lax.psum_scatter(sums, "shard", scatter_dimension=0, tiled=False)
        own = spread_chips(held(sums[None], *earlier))
        return place(win, own, spread_cores(own), owned_rows, 1, kind=F32)[:, 0]

    def reduce_whole(grads, transposed=False):
        if transposed:
            grads = grads.transpose(1, 0, 2, 3)
        full = lax.psum_scatter(grads, "shard", scatter_dimension=1, tiled=False)
        return lax.psum(full, ("replica", "ctx")).astype(F32)

    def start_units(grads, transposed=False):
        if not pairwise:
            return grads, ((), (), ())
        halves, first = reduce_first(win, grads, transposed)
        sums, second, last = reduce_second(win, halves)
        return sums, (first, second, last)

    def by_shard(grads):
        return grads.astype(BF16).reshape(4, shards, owned_rows, width)

    grad_proj = jnp.einsum("ctx,td->cxd", low_act, low_grad_out, preferred_element_type=F32)
    grad_proj = grad_proj.astype(BF16)
    partial_proj, proj_marks = start_units(by_shard(grad_proj), transposed=True)
    (outputs,) = by_rows(
        output_kernel,
        [middle, low_act],
        [w_proj, small],
        [((), BF16)],
        ties=[corner(grad_proj)],
    )
    grad_hidden, sums_hidden = by_rows(
        hidden_back_kernel,
        [low_grad_out, slope],
        [w_proj],
        [((wide,), BF16)],
        sums=8,
        ties=[corner(outputs), *proj_marks[0]],
    )
    grad_fc = jnp.einsum("td,ctx->cdx", low_two, grad_hidden, preferred_element_type=F32)
    grad_fc = grad_fc.astype(BF16)
    partial_fc, fc_marks = start_units(by_shard(grad_fc))
    grad_middle, low_grad_middle, grad_mixed, sums_middle = by_rows(
        middle_back_kernel,
        [grad_hidden, low_grad_out, middle],
        [w_fc, (w_a, 3, 1), small],
        [((), F32), ((), BF16), ((), BF16)],
        sums=8,
        ties=[corner(grad_fc), *proj_marks[1]],
    )
    layer_out = to_blocks(
        outputs.reshape(blocked), BF16, *fc_marks[0][:1]
    )
    grad_out_weight = dot_tn(attended, low_grad_middle).astype(BF16)
    grad_joined = attention_backward(
        joined,
        mixed,
        grad_mixed.reshape(blocked),
        lse,
        order,
        ties=[corner(grad_out_weight), *proj_marks[2], *fc_marks[0]],
    ).reshape(3, rows, width)
    grad_qkv = jnp.einsum("td,ctx->cdx", low_one, grad_joined, preferred_element_type=F32)
    grad_qkv = grad_qkv.astype(BF16)
    grads_a = jnp.concatenate([grad_qkv, grad_out_weight[None]], axis=0)
    partial_a, mark = by_shard(grads_a), ()
    if pairwise:
        halves, mark = reduce_first(win, partial_a, False)
    grad_inputs, sums_input = by_rows(
        input_back_kernel,
        [grad_joined, grad_middle, low_inputs],
        [(w_a, 0, 3), small],
        [((), BF16)],
        sums=8,
        ties=[corner(grad_qkv), *mark, *fc_marks[2]],
    )
    if pairwise:
        partial_a, _, _ = reduce_second(win, halves, grad_inputs)
    earlier = (partial_a,) if pairwise else ()
    input_grad = to_blocks(grad_inputs.reshape(blocked), F32, *earlier)

    small_grads = sums_middle + sums_input
    grad_fc_bias = sums_hidden[:wide]
    vector_grads = jnp.concatenate(
        [
            small_grads.reshape(8, shards, owned_rows)
            .transpose(1, 0, 2)
            .reshape(shards, 8 * owned_rows),
            grad_fc_bias.reshape(shards, owned_rows * wide),
        ],
        axis=1,
    ).astype(BF16)
    vector_grads = jnp.pad(
        vector_grads.reshape(shards, vector_rows, width),
        ((0, 0), (0, -vector_rows % 16), (0, 0)),
    )
    if pairwise:
        owned_proj = finish_units(partial_proj, grad_joined)
        owned_a = finish_units(partial_a)
        owned_fc = finish_units(partial_fc, partial_a)
        owned_vectors = lax.dynamic_index_in_dim(
            reduce_vectors(held(vector_grads, partial_a)),
            lax.axis_index("shard"),
            keepdims=False,
        )
    else:
        owned_proj = reduce_whole(partial_proj, transposed=True)
        owned_a, owned_fc = reduce_whole(partial_a), reduce_whole(partial_fc)
        owned_vectors = lax.psum_scatter(
            vector_grads, "shard", scatter_dimension=0, tiled=False
        )
        owned_vectors = lax.psum(owned_vectors, ("replica", "ctx"))
    owned_vectors = owned_vectors[:vector_rows].reshape(-1).astype(F32)
    vec = [owned_vectors[i * owned_rows : (i + 1) * owned_rows] for i in range(8)]
    qkv_grad = jnp.concatenate([owned_a[i] for i in range(3)], axis=1)
    fc_grad = jnp.concatenate([owned_fc[i] for i in range(wide)], axis=1)
    return (
        layer_out,
        input_grad,
        vec[0],
        vec[1],
        qkv_grad,
        vec[2],
        vec[3],
        owned_a[3],
        vec[4],
        vec[5],
        vec[6],
        fc_grad,
        owned_vectors[8 * owned_rows :],
        owned_proj.reshape(wide * owned_rows, width),
        vec[7],
    )


def solution(mesh):
    vector, matrix = P("shard"), P("shard", None)
    rows = P(("shard", "replica"), "ctx", None)
    weights = (
        vector,
        vector,
        matrix,
        vector,
        vector,
        matrix,
        vector,
        vector,
        vector,
        matrix,
        vector,
        matrix,
        vector,
    )
    return jax.shard_map(
        per_device,
        mesh=mesh,
        in_specs=(rows, rows, P()) + weights,
        out_specs=(rows, rows) + weights,
        check_vma=False,
    )
```

```python
import functools

import jax
import jax.numpy as jnp
from jax import lax
from jax.experimental import pallas as pl
from jax.experimental.layout import Layout, with_layout_constraint
from jax.experimental.pallas import tpu as pltpu
from jax.sharding import PartitionSpec as P

HEAD_DIM = 64
EPSILON = 1e-05
LANES = 128
VMEM_LIMIT = 56 * 1024 * 1024
COST_SCALE = 8

BF16 = jnp.bfloat16
F32 = jnp.float32


def dot_nn(left, right):
    return lax.dot_general(left, right, (((1,), (0,)), ((), ())), preferred_element_type=F32)


def dot_nt(left, right):
    return lax.dot_general(left, right, (((1,), (1,)), ((), ())), preferred_element_type=F32)


def dot_tn(left, right):
    return lax.dot_general(left, right, (((0,), (0,)), ((), ())), preferred_element_type=F32)


def head_lanes(shape, which):
    lane = lax.broadcasted_iota(jnp.int32, shape, 1)
    return (lane < HEAD_DIM) if which == 0 else (lane >= HEAD_DIM)


def only_valid(values, width):
    if width % LANES == 0:
        return values
    lane = lax.broadcasted_iota(jnp.int32, values.shape, 1) + pl.program_id(1) * LANES
    return jnp.where(lane < width, values, jnp.zeros_like(values))


def sorted_rows(ref, lead, order_ref, first, last):
    return jnp.concatenate([ref[lead + (order_ref[i], 0)] for i in range(first, last)], axis=0)


def store_rows(ref, lead, order_ref, first, rows):
    local = ref.shape[-2]
    for i in range(rows.shape[0] // local):
        ref[lead + (order_ref[first + i], 0)] = rows[i * local : (i + 1) * local]


def causal(rows, columns):
    key_at = lax.broadcasted_iota(jnp.int32, (rows, columns), 0)
    query_at = lax.broadcasted_iota(jnp.int32, (rows, columns), 1)
    return key_at <= query_at


def attention_forward_kernel(blocks, width, order_ref, q_ref, k_ref, v_ref, *refs):
    o_ref, lse_ref = refs[-2:]
    count, local = k_ref.shape[1], k_ref.shape[3]
    tile = blocks * local
    keys = only_valid(sorted_rows(k_ref, (0,), order_ref, 0, count), width)
    values_t = sorted_rows(v_ref, (0,), order_ref, 0, count).astype(F32).T.astype(BF16)
    diagonal = causal(tile, tile)
    for first in range(0, count, blocks):
        start, stop = first * local, (first + blocks) * local
        queries = sorted_rows(q_ref, (0,), order_ref, first, first + blocks)
        queries = queries * jnp.asarray(HEAD_DIM**-0.5, BF16)
        pieces = []
        for which in range(2):
            masked_q = jnp.where(head_lanes(queries.shape, which), queries, jnp.zeros_like(queries))
            scores = dot_nt(keys[:stop], masked_q)
            tiles = []
            if start > 0:
                tiles.append(scores[:start])
            tiles.append(jnp.where(diagonal, scores[start:], -1e30))
            top = functools.reduce(
                jnp.maximum, [jnp.max(block, axis=0, keepdims=True) for block in tiles]
            )
            weights = [jnp.exp(block - top) for block in tiles]
            total = sum(jnp.sum(weight, axis=0, keepdims=True) for weight in weights)
            low = jnp.concatenate([weight.astype(BF16) for weight in weights], axis=0)
            rows = values_t[which * HEAD_DIM : (which + 1) * HEAD_DIM, :stop]
            pieces.append(dot_nn(rows, low) * (1.0 / total))
            lse_ref[0, 0, which : which + 1, start:stop] = top + jnp.log(total)
        mixed_t = jnp.concatenate(pieces, axis=0)
        store_rows(o_ref, (), order_ref, first, mixed_t.T.astype(BF16))


def attention_backward_kernel(
    blocks,
    width,
    order_ref,
    q_ref,
    k_ref,
    v_ref,
    o_ref,
    do_ref,
    lse_ref,
    *refs,
):
    out_ref, dk_acc, dv_acc = refs[-3:]
    count, local = k_ref.shape[1], k_ref.shape[3]
    tile = blocks * local
    keys = only_valid(sorted_rows(k_ref, (0,), order_ref, 0, count), width)
    values = only_valid(sorted_rows(v_ref, (0,), order_ref, 0, count), width)
    keys_t = keys.astype(F32).T.astype(BF16)
    diagonal = causal(tile, tile)
    for first in range(0, count, blocks):
        start, stop = first * local, (first + blocks) * local
        queries = sorted_rows(q_ref, (0,), order_ref, first, first + blocks)
        queries = queries * jnp.asarray(HEAD_DIM**-0.5, BF16)
        grads = sorted_rows(do_ref, (), order_ref, first, first + blocks)
        mixed = sorted_rows(o_ref, (), order_ref, first, first + blocks)
        product_t = (grads.astype(F32) * mixed.astype(F32)).T
        key_lanes = head_lanes((stop, LANES), 0)
        dq_parts, dk_parts, dv_parts = [], [], []
        for which in range(2):
            mine = head_lanes(queries.shape, which)
            masked_q = jnp.where(mine, queries, jnp.zeros_like(queries))
            masked_g = jnp.where(mine, grads, jnp.zeros_like(grads))
            delta = jnp.sum(
                product_t[which * HEAD_DIM : (which + 1) * HEAD_DIM], axis=0, keepdims=True
            )
            lse = lse_ref[0, 0, which : which + 1, start:stop]
            scores = dot_nt(keys[:stop], masked_q)
            grad_weights = dot_nt(values[:stop], masked_g)
            weights = jnp.exp(scores - lse)
            if start > 0:
                weights = jnp.concatenate(
                    [weights[:start], jnp.where(diagonal, weights[start:], 0.0)], axis=0
                )
            else:
                weights = jnp.where(diagonal, weights, 0.0)
            low_scores = (weights * (grad_weights - delta)).astype(BF16)
            dv_parts.append(dot_nn(weights.astype(BF16), grads))
            dk_parts.append(dot_nn(low_scores, queries))
            dq_parts.append(
                dot_nn(keys_t[which * HEAD_DIM : (which + 1) * HEAD_DIM, :stop], low_scores)
            )
        dq_t = jnp.concatenate(dq_parts, axis=0) * (HEAD_DIM**-0.5)
        store_rows(out_ref, (0,), order_ref, first, dq_t.T.astype(BF16))
        dk = jnp.where(key_lanes, dk_parts[0], dk_parts[1])
        dv = jnp.where(key_lanes, dv_parts[0], dv_parts[1])
        if start > 0:
            dk_acc[:start] += dk[:start]
            dv_acc[:start] += dv[:start]
        dk_acc[start:stop] = dk[start:]
        dv_acc[start:stop] = dv[start:]
    store_rows(out_ref, (1,), order_ref, 0, dk_acc[...].astype(BF16))
    store_rows(out_ref, (2,), order_ref, 0, dv_acc[...].astype(BF16))


def query_blocks(count):
    return 2 if count % 2 == 0 else 1


def attention_forward(joined, order, ties=()):
    _, count, seqs, local, width = joined.shape
    length = count * local
    pairs = pl.cdiv(width, LANES)
    spec = lambda which: pl.BlockSpec(
        (1, count, 1, local, LANES), lambda s, h, order: (which, 0, s, 0, h)
    )
    return pl.pallas_call(
        functools.partial(attention_forward_kernel, query_blocks(count), width),
        grid_spec=pltpu.PrefetchScalarGridSpec(
            num_scalar_prefetch=1,
            grid=(seqs, pairs),
            in_specs=[spec(0), spec(1), spec(2)]
            + [pl.BlockSpec(memory_space=pl.ANY)] * len(ties),
            out_specs=[
                pl.BlockSpec((count, 1, local, LANES), lambda s, h, order: (0, s, 0, h)),
                pl.BlockSpec((1, 1, 8, length), lambda s, h, order: (s, h, 0, 0)),
            ],
        ),
        out_shape=[
            jax.ShapeDtypeStruct((count, seqs, local, width), BF16),
            jax.ShapeDtypeStruct((seqs, pairs, 8, length), F32),
        ],
        compiler_params=pltpu.CompilerParams(vmem_limit_bytes=VMEM_LIMIT),
        cost_estimate=pl.CostEstimate(
            flops=seqs * pairs * 16 * length * length * LANES // COST_SCALE,
            bytes_accessed=8 * seqs * length * width // COST_SCALE,
            transcendentals=0,
        ),
    )(order, joined, joined, joined, *ties)


def attention_backward(joined, mixed, grad_mixed, lse, order, ties=()):
    _, count, seqs, local, width = joined.shape
    length = count * local
    pairs = pl.cdiv(width, LANES)
    spec = lambda which: pl.BlockSpec(
        (1, count, 1, local, LANES), lambda s, h, order: (which, 0, s, 0, h)
    )
    rows = pl.BlockSpec((count, 1, local, LANES), lambda s, h, order: (0, s, 0, h))
    return pl.pallas_call(
        functools.partial(attention_backward_kernel, query_blocks(count), width),
        grid_spec=pltpu.PrefetchScalarGridSpec(
            num_scalar_prefetch=1,
            grid=(seqs, pairs),
            in_specs=[
                spec(0),
                spec(1),
                spec(2),
                rows,
                rows,
                pl.BlockSpec((1, 1, 8, length), lambda s, h, order: (s, h, 0, 0)),
            ]
            + [pl.BlockSpec(memory_space=pl.ANY)] * len(ties),
            out_specs=pl.BlockSpec(
                (3, count, 1, local, LANES), lambda s, h, order: (0, 0, s, 0, h)
            ),
            scratch_shapes=[pltpu.VMEM((length, LANES), F32), pltpu.VMEM((length, LANES), F32)],
        ),
        out_shape=jax.ShapeDtypeStruct(joined.shape, BF16),
        compiler_params=pltpu.CompilerParams(vmem_limit_bytes=VMEM_LIMIT),
        cost_estimate=pl.CostEstimate(
            flops=seqs * pairs * 20 * length * length * LANES // COST_SCALE,
            bytes_accessed=16 * seqs * length * width // COST_SCALE,
            transcendentals=0,
        ),
    )(order, joined, joined, joined, mixed, grad_mixed, lse, *ties)


def standardize(values):
    centred = values - jnp.mean(values, axis=-1, keepdims=True)
    inverse = lax.rsqrt(jnp.mean(centred * centred, axis=-1, keepdims=True) + EPSILON)
    return centred * inverse, inverse


def normalize_back(grad_out, standard, inverse, gain):
    scaled = grad_out * gain
    return inverse * (
        scaled
        - jnp.mean(scaled, axis=-1, keepdims=True)
        - standard * jnp.mean(scaled * standard, axis=-1, keepdims=True)
    )


def add_row(sums_ref, row, values):
    sums_ref[row : row + 1, :] += jnp.sum(values, axis=0, keepdims=True)


def clear_first(sums_ref):
    @pl.when(pl.program_id(0) == 0)
    def _():
        sums_ref[...] = jnp.zeros_like(sums_ref)


G_ONE, B_ONE, BIAS_Q, BIAS_V, BIAS_OUT, G_TWO, B_TWO, BIAS_PROJ = range(8)


def row(small_ref, index):
    return small_ref[index : index + 1, :]


def qkv_kernel(x_ref, w_ref, small_ref, *refs):
    joined_ref, low_ref = refs[-2:]
    standard, _ = standardize(x_ref[...].astype(F32))
    low = (standard * row(small_ref, G_ONE) + row(small_ref, B_ONE)).astype(BF16)
    low_ref[...] = low
    for which, bias in enumerate((BIAS_Q, None, BIAS_V)):
        out = dot_nn(low, w_ref[which])
        if bias is not None:
            out = out + row(small_ref, bias)
        joined_ref[which] = out.astype(BF16)


def attended_kernel(x_ref, o_ref, w_ref, small_ref, *refs):
    middle_ref, low_ref = refs[-2:]
    middle = x_ref[...].astype(F32) + dot_nn(o_ref[...], w_ref[0]) + row(small_ref, BIAS_OUT)
    middle_ref[...] = middle
    standard, _ = standardize(middle)
    low_ref[...] = (standard * row(small_ref, G_TWO) + row(small_ref, B_TWO)).astype(BF16)


def hidden_kernel(low_ref, w_ref, bias_ref, *refs):
    act_ref, slope_ref = refs[-2:]
    low = low_ref[...]
    scale = 0.7978845608028654
    for which in range(w_ref.shape[0]):
        hidden = dot_nn(low, w_ref[which]) + bias_ref[which]
        square = hidden * hidden
        bent = jnp.tanh(scale * hidden * (1.0 + 0.044715 * square))
        half = 0.5 * (1.0 + bent)
        act_ref[which] = (hidden * half).astype(BF16)
        slope = half + 0.5 * hidden * (1.0 - bent * bent) * (
            scale * (1.0 + 3.0 * 0.044715 * square)
        )
        slope_ref[which] = slope.astype(BF16)


def output_kernel(middle_ref, act_ref, w_ref, small_ref, *refs):
    out_ref = refs[-1]
    total = middle_ref[...] + row(small_ref, BIAS_PROJ)
    for which in range(w_ref.shape[0]):
        total += dot_nn(act_ref[which], w_ref[which])
    out_ref[...] = total.astype(BF16)


def hidden_back_kernel(grad_ref, slope_ref, w_ref, *refs):
    out_ref, sums_ref = refs[-2:]
    clear_first(sums_ref)
    grad = grad_ref[...]
    for which in range(w_ref.shape[0]):
        back = dot_nt(grad, w_ref[which]) * slope_ref[which].astype(F32)
        low = back.astype(BF16)
        out_ref[which] = low
        add_row(sums_ref, which, low.astype(F32))


def middle_back_kernel(hidden_ref, grad_ref, middle_ref, w_ref, out_w_ref, small_ref, *refs):
    grad_middle_ref, low_ref, mixed_ref, sums_ref = refs[-4:]
    clear_first(sums_ref)
    grad_two = dot_nt(hidden_ref[0], w_ref[0])
    for which in range(1, w_ref.shape[0]):
        grad_two += dot_nt(hidden_ref[which], w_ref[which])
    standard, inverse = standardize(middle_ref[...])
    grad_out = grad_ref[...].astype(F32)
    grad_middle = grad_out + normalize_back(grad_two, standard, inverse, row(small_ref, G_TWO))
    low = grad_middle.astype(BF16)
    grad_middle_ref[...] = grad_middle
    low_ref[...] = low
    mixed_ref[...] = dot_nt(low, out_w_ref[0]).astype(BF16)
    add_row(sums_ref, G_TWO, grad_two * standard)
    add_row(sums_ref, B_TWO, grad_two)
    add_row(sums_ref, BIAS_OUT, low.astype(F32))
    add_row(sums_ref, BIAS_PROJ, grad_out)


def input_back_kernel(joined_ref, grad_middle_ref, x_ref, w_ref, small_ref, *refs):
    out_ref, sums_ref = refs[-2:]
    clear_first(sums_ref)
    grad_one = dot_nt(joined_ref[0], w_ref[0])
    for which in range(1, 3):
        grad_one += dot_nt(joined_ref[which], w_ref[which])
    standard, inverse = standardize(x_ref[...].astype(F32))
    back = normalize_back(grad_one, standard, inverse, row(small_ref, G_ONE))
    out_ref[...] = (grad_middle_ref[...] + back).astype(BF16)
    add_row(sums_ref, G_ONE, grad_one * standard)
    add_row(sums_ref, B_ONE, grad_one)
    add_row(sums_ref, BIAS_Q, joined_ref[0].astype(F32))
    add_row(sums_ref, BIAS_V, joined_ref[2].astype(F32))


def by_rows(kernel, by_row, fixed, outs, sums=None, ties=(), tile=256):
    rows, width = by_row[0].shape[-2:]
    tile = tile if rows % tile == 0 else rows
    whole = lambda shape, index: pl.BlockSpec(
        shape, lambda i: index, pipeline_mode=pl.Buffered(buffer_count=1)
    )
    tiled = lambda lead: pl.BlockSpec(
        tuple(lead) + (tile, width), lambda i: (0,) * len(lead) + (i, 0)
    )
    in_specs = [tiled(array.shape[:-2]) for array in by_row]
    operands = list(by_row)
    products = 0
    for entry in fixed:
        array, first, blocks = entry if isinstance(entry, tuple) else (entry, 0, entry.shape[0])
        shape = (blocks,) + array.shape[1:]
        in_specs.append(whole(shape, (first // blocks,) + (0,) * (array.ndim - 1)))
        operands.append(array)
        if array.dtype == BF16:
            products += blocks
    in_specs += [pl.BlockSpec(memory_space=pl.ANY)] * len(ties)
    operands += list(ties)
    out_specs = [tiled(lead) for lead, _ in outs]
    out_shape = [jax.ShapeDtypeStruct(tuple(lead) + (rows, width), kind) for lead, kind in outs]
    if sums:
        out_specs.append(pl.BlockSpec((sums, width), lambda i: (0, 0)))
        out_shape.append(jax.ShapeDtypeStruct((sums, width), F32))
    moved = sum(array.size * array.dtype.itemsize for array in operands)
    moved += sum(leaf.size * leaf.dtype.itemsize for leaf in out_shape)
    return pl.pallas_call(
        kernel,
        grid=(rows // tile,),
        in_specs=in_specs,
        out_specs=out_specs,
        out_shape=out_shape,
        compiler_params=pltpu.CompilerParams(vmem_limit_bytes=VMEM_LIMIT),
        cost_estimate=pl.CostEstimate(
            flops=3 * rows * width * width * products // COST_SCALE,
            bytes_accessed=moved // COST_SCALE,
            transcendentals=0,
        ),
    )(*operands)


def row_major(values):
    return with_layout_constraint(values, Layout(major_to_minor=tuple(range(values.ndim))))


def swap(values, axis, offset):
    count = lax.axis_size(axis)
    return lax.ppermute(values, axis, [(index, index ^ offset) for index in range(count)])


def after(values, *earlier):
    return lax.optimization_barrier((values, *earlier))


def held(values, *earlier):
    if not earlier:
        return values
    wrong = jnp.zeros((), jnp.bool_)
    for array in earlier:
        entry = array[(0,) * array.ndim]
        wrong = wrong | (entry != entry)
    return jnp.where(wrong, jnp.zeros_like(values), values)


def pick(bit, on_zero, on_one):
    return jnp.where(bit == 0, on_zero, on_one)


def to_sequences(values, count, start=(), finish=()):
    seqs, local, width = values.shape
    own = lax.axis_index("ctx")
    parts = values.swapaxes(1, 2).reshape(count, seqs // count, width, local)
    mine = [lax.dynamic_index_in_dim(parts, own ^ i, keepdims=False) for i in range(count)]
    far = row_major(held(jnp.stack(mine[2:]), *start))
    far = row_major(swap(far, "ctx", 2))
    near = row_major(swap(row_major(jnp.stack([mine[1], far[1]])), "ctx", 1))
    whole = row_major(jnp.stack([mine[0], near[0], far[0], near[1]]))
    return row_major(held(whole, *finish).swapaxes(2, 3))


def to_blocks(values, kind, *start):
    count, share, local, width = values.shape
    own = lax.axis_index("ctx")
    values = row_major(held(values.swapaxes(2, 3), *start))
    far = row_major(swap(row_major(values[2:]), "ctx", 2))
    near = row_major(swap(row_major(jnp.stack([values[1], far[1]])), "ctx", 1))
    out = row_major(jnp.zeros((count, share, width, local), kind))
    for offset, piece in enumerate([values[0], near[0], far[0], near[1]]):
        out = lax.dynamic_update_index_in_dim(out, piece.astype(kind), own ^ offset, 0)
    out = row_major(out).reshape(count * share, width, local).swapaxes(1, 2)
    return out, near


class Windows:
    def __init__(self, owned_rows):
        tiles = owned_rows // 16
        self.start = tiles // 2 * 16
        self.size = owned_rows - self.start
        ctx = lax.axis_index("ctx")
        self.core = ctx % 2
        self.y = ctx // 2
        self.x = lax.axis_index("replica")

    def rows(self, values):
        return pick(
            self.core, values[..., : self.size, :], values[..., self.start :, :]
        )

    def other_rows(self, values):
        return pick(
            self.core, values[..., self.start :, :], values[..., : self.size, :]
        )

    def block(self, blocks):
        return pick(
            self.x,
            pick(self.y, blocks[0], blocks[1]),
            pick(self.y, blocks[2], blocks[3]),
        )


def assemble_kernel(groups, start, size, transposed, here_ref, *refs):
    arrays, out_ref = refs[:-1], refs[-1]
    x, y, core = here_ref[0], here_ref[1], here_ref[2]
    for turn in range(2):
        row = pl.multiple_of((core ^ turn) * start, 16)
        for (places, first), ref in zip(groups, arrays[turn * len(groups) :]):
            for i, (dx, dy) in enumerate(places):
                block = 2 * (x ^ dx) + (y ^ dy)
                for s in range(ref.shape[1]):
                    place = (first + s, block) if transposed else (block, first + s)
                    out_ref[place + (pl.ds(row, size), slice(None))] = ref[
                        i, s, :size, :
                    ].astype(out_ref.dtype)


def assemble(win, groups, own, other, owned_rows, shards, transposed, kind):
    width = own[0].shape[-1]
    here = jnp.stack([win.x, win.y, win.core]).astype(jnp.int32)
    shape = (shards, 4, owned_rows, width) if transposed else (4, shards, owned_rows, width)
    return pl.pallas_call(
        functools.partial(assemble_kernel, groups, win.start, win.size, transposed),
        in_specs=[pl.BlockSpec(memory_space=pltpu.SMEM)]
        + [pl.BlockSpec(memory_space=pltpu.VMEM)] * (2 * len(groups)),
        out_specs=pl.BlockSpec(memory_space=pltpu.VMEM),
        out_shape=jax.ShapeDtypeStruct(shape, kind),
        compiler_params=pltpu.CompilerParams(vmem_limit_bytes=VMEM_LIMIT),
        cost_estimate=pl.CostEstimate(
            flops=0, bytes_accessed=16 * shards * owned_rows * width, transcendentals=0
        ),
    )(here, *own, *other)


def spread_chips(mine):
    shards = mine.shape[0]
    if shards == 1:
        first = jnp.stack([mine, swap(mine, "replica", 1)])
        return [first, swap(first, "ctx", 2)]
    split = shards // 2
    low, high = mine[:split], mine[split:]
    low_there, high_there = after(swap(low, "replica", 1), swap(high, "ctx", 2))
    first = jnp.stack([low, low_there])
    second = jnp.stack([high, high_there])
    third, fourth = after(swap(first, "ctx", 2), swap(second, "replica", 1))
    return [first, second, third, fourth]


def chip_groups(shards):
    if shards == 1:
        return ((((0, 0), (1, 0)), 0), (((0, 1), (1, 1)), 0))
    return (
        (((0, 0), (1, 0)), 0),
        (((0, 0), (0, 1)), shards // 2),
        (((0, 1), (1, 1)), 0),
        (((1, 0), (1, 1)), shards // 2),
    )


def spread_cores(own):
    return [swap(array, "ctx", 1) for array in own]


def place(win, own, other, owned_rows, shards, transposed=False, kind=BF16):
    return assemble(win, chip_groups(shards), own, other, owned_rows, shards, transposed, kind)


def add_pair(kept, received):
    return (kept.astype(F32) + received.astype(F32)).astype(BF16)


def corner(values):
    return values[(0,) * (values.ndim - 2)][:16, :LANES]


def reduce_first(win, grads, transposed):
    shards = grads.shape[0 if transposed else 1]
    split = shards // 2

    def part(values, blocks, which):
        return values[which, blocks] if transposed else values[blocks, which]

    lower, upper = slice(None, split), slice(split, None)
    entry = lambda values, i: values[:, i] if transposed else values[i]
    received = swap(win.other_rows(grads), "ctx", 1)
    both = add_pair(win.rows(grads), received)
    by_x = [part(both, slice(2 * i, 2 * i + 2), lower) for i in range(2)]
    by_y = [part(both, slice(i, None, 2), upper) for i in range(2)]
    x_sent = row_major(pick(win.x, by_x[1], by_x[0]))
    y_sent = row_major(pick(win.y, by_y[1], by_y[0]))
    x_received, y_received = after(
        row_major(swap(x_sent, "replica", 1)), row_major(swap(y_sent, "ctx", 2))
    )
    low = row_major(add_pair(pick(win.x, *by_x), x_received))
    high = row_major(add_pair(pick(win.y, *by_y), y_received))
    low, high = [entry(low, i) for i in range(2)], [entry(high, i) for i in range(2)]
    return (low, high), [corner(x_sent), corner(y_sent)]


def reduce_second(win, halves, *earlier):
    low, high = halves
    low_sent, high_sent = pick(win.y, low[1], low[0]), pick(win.x, high[1], high[0])
    if earlier:
        low_sent, high_sent = held(low_sent, *earlier), held(high_sent, *earlier)
    low_received, high_received = after(
        swap(low_sent, "ctx", 2), swap(high_sent, "replica", 1)
    )
    low_sum = add_pair(pick(win.y, *low), low_received)
    high_sum = add_pair(pick(win.x, *high), high_received)
    sums = jnp.concatenate([low_sum, high_sum], axis=0)
    return sums, [corner(low_sent)], [corner(sums)]


def reduce_vectors(values):
    values = add_pair(values, swap(values, "replica", 1))
    values = add_pair(values, swap(values, "ctx", 2))
    step = 1
    while step < lax.axis_size("shard"):
        values = add_pair(values, swap(values, "shard", step))
        step *= 2
    return values


def per_device(
    tokens,
    cotangent,
    block_order,
    ln1_gain,
    ln1_bias,
    qkv_weight,
    q_bias,
    v_bias,
    out_weight,
    out_bias,
    ln2_gain,
    ln2_bias,
    fc_weight,
    fc_bias,
    proj_weight,
    proj_bias,
):
    seq_count, local_len, width = tokens.shape
    owned_rows = ln1_gain.shape[0]
    shards = width // owned_rows
    wide = fc_weight.shape[1] // width
    count = lax.axis_size("ctx")
    rows = seq_count * local_len
    pairwise = lax.axis_size("replica") == 2 and count == 4 and shards == 4
    win = Windows(owned_rows)

    vectors = jnp.concatenate(
        [ln1_gain, ln1_bias, q_bias, v_bias, out_bias, ln2_gain, ln2_bias, proj_bias, fc_bias]
    )
    vector_rows = vectors.shape[0] // width
    vector_tile = jnp.pad(vectors.reshape(vector_rows, width), ((0, -vector_rows % 16), (0, 0)))
    column = lambda values, i: values[:, i * width : (i + 1) * width]
    blocks_a = [column(qkv_weight, i) for i in range(3)] + [out_weight]
    blocks_b = [column(fc_weight, i) for i in range(wide)]
    blocks_c = [proj_weight[i * owned_rows : (i + 1) * owned_rows] for i in range(wide)]

    def gather_z(values):
        return lax.all_gather(values, "shard", axis=0, tiled=False)

    low_inputs = to_sequences(tokens, count).reshape(rows, width)

    if pairwise:
        mine = [win.rows(win.block(blocks)) for blocks in (blocks_a, blocks_b, blocks_c)]
        part_a = gather_z(mine[0])
        mine_b, part_a = after(jnp.concatenate([mine[1], vector_tile], axis=0), part_a)
        part_b = gather_z(mine_b)
        mine_c, part_b = after(mine[2], part_b)
        part_c = gather_z(mine_c)
        part_a, low_inputs = after(part_a, low_inputs)
        own_a = spread_chips(part_a)
        other_a = spread_cores(own_a)
        full_a = place(win, own_a, other_a, owned_rows, shards)
        vector_part = part_b[:, win.size : win.size + vector_rows]
        own_b = spread_chips(held(part_b[:, : win.size], own_a[2]))
    else:
        vector_part = gather_z(vector_tile)[:, :vector_rows]
        full_a, full_b, full_c = [
            gather_z(jnp.stack(blocks)) for blocks in (blocks_a, blocks_b, blocks_c)
        ]
        full_a, full_b = full_a.transpose(1, 0, 2, 3), full_b.transpose(1, 0, 2, 3)
    w_a = full_a.reshape(4, width, width)
    vector_part = vector_part.reshape(shards, vector_rows * width).astype(F32)
    small = vector_part[:, : 8 * owned_rows].reshape(shards, 8, owned_rows)
    small = small.transpose(1, 0, 2).reshape(8, width)
    bias_fc = vector_part[:, 8 * owned_rows :].reshape(wide, 1, width)

    share = seq_count // count
    blocked = (count, share, local_len, width)
    index = jnp.arange(count, dtype=jnp.int32)
    held_by = jnp.sum(jnp.where(block_order[None, :] == index[:, None], index[None, :], 0), axis=1)
    order = (held_by ^ lax.axis_index("ctx")).astype(jnp.int32)

    steps = [corner(own_b[0][1]), corner(own_b[1][1])] if pairwise else []
    joined, low_one = by_rows(
        qkv_kernel, [low_inputs], [(w_a, 0, 3), small], [((3,), BF16), ((), BF16)], ties=steps
    )
    joined = joined.reshape((3,) + blocked)
    if pairwise:
        other_b = spread_cores(own_b)
        full_b = place(win, own_b, other_b, owned_rows, shards)
        own_c = spread_chips(held(part_c, own_b[2], joined))
        steps = [corner(own_c[0][1]), corner(own_c[1][1]), corner(own_c[2]), corner(own_c[3])]
    else:
        steps = [corner(joined[0, 0])] * 4
    mixed, lse = attention_forward(joined, order, ties=steps[:2])
    attended = mixed.reshape(rows, width)
    middle, low_two = by_rows(
        attended_kernel,
        [low_inputs, attended],
        [(w_a, 3, 1), small],
        [((), F32), ((), BF16)],
    )
    w_fc = full_b.reshape(wide, width, width)
    low_act, slope = by_rows(
        hidden_kernel,
        [low_two],
        [w_fc, bias_fc],
        [((wide,), BF16), ((wide,), BF16)],
        ties=steps[2:],
    )
    if pairwise:
        full_c = place(win, own_c, spread_cores(own_c), owned_rows, shards, transposed=True)
    w_proj = full_c.reshape(wide, width, width)
    start, finish = ((own_c[2], mixed), (full_c,)) if pairwise else ((), ())
    low_grad_out = to_sequences(cotangent, count, start, finish).reshape(rows, width)

    def finish_units(groups, *earlier):
        sums = [
            lax.psum_scatter(group, "shard", scatter_dimension=0, tiled=False)
            for group in groups
        ]
        own = spread_chips(held(jnp.stack(sums), *earlier))
        return place(
            win, own, spread_cores(own), owned_rows, len(sums), transposed=True, kind=F32
        )

    def reduce_whole(grads, transposed=False):
        if transposed:
            grads = grads.transpose(1, 0, 2, 3)
        full = lax.psum_scatter(grads, "shard", scatter_dimension=1, tiled=False)
        return lax.psum(full, ("replica", "ctx")).astype(F32)

    def start_units(grads, transposed=False):
        if not pairwise:
            return grads, ((), (), ())
        halves, first = reduce_first(win, grads, transposed)
        sums, second, last = reduce_second(win, halves)
        return sums, (first, second, last)

    def by_shard(grads):
        return grads.astype(BF16).reshape(4, shards, owned_rows, width)

    grad_proj = jnp.einsum("ctx,td->cxd", low_act, low_grad_out, preferred_element_type=F32)
    grad_proj = grad_proj.astype(BF16)
    partial_proj, proj_marks = start_units(by_shard(grad_proj), transposed=True)
    (outputs,) = by_rows(
        output_kernel,
        [middle, low_act],
        [w_proj, small],
        [((), BF16)],
        ties=[corner(grad_proj)],
    )
    grad_hidden, sums_hidden = by_rows(
        hidden_back_kernel,
        [low_grad_out, slope],
        [w_proj],
        [((wide,), BF16)],
        sums=8,
        ties=[corner(outputs), *proj_marks[0]],
    )
    grad_fc = jnp.einsum("td,ctx->cdx", low_two, grad_hidden, preferred_element_type=F32)
    grad_fc = grad_fc.astype(BF16)
    partial_fc, fc_marks = start_units(by_shard(grad_fc))
    layer_out, returned = to_blocks(outputs.reshape(blocked), BF16, *proj_marks[1])
    grad_middle, low_grad_middle, grad_mixed, sums_middle = by_rows(
        middle_back_kernel,
        [grad_hidden, low_grad_out, middle],
        [w_fc, (w_a, 3, 1), small],
        [((), F32), ((), BF16), ((), BF16)],
        sums=8,
        ties=[corner(grad_fc), *proj_marks[1]],
    )
    grad_out_weight = dot_tn(attended, low_grad_middle).astype(BF16)
    grad_joined = attention_backward(
        joined,
        mixed,
        grad_mixed.reshape(blocked),
        lse,
        order,
        ties=[corner(grad_out_weight), corner(returned), *proj_marks[2], *fc_marks[0]],
    ).reshape(3, rows, width)
    grad_qkv = jnp.einsum("td,ctx->cdx", low_one, grad_joined, preferred_element_type=F32)
    grad_qkv = grad_qkv.astype(BF16)
    grads_a = jnp.concatenate([grad_qkv, grad_out_weight[None]], axis=0)
    partial_a, mark = by_shard(grads_a), ()
    if pairwise:
        halves, mark = reduce_first(win, partial_a, False)
    grad_inputs, sums_input = by_rows(
        input_back_kernel,
        [grad_joined, grad_middle, low_inputs],
        [(w_a, 0, 3), small],
        [((), BF16)],
        sums=8,
        ties=[corner(grad_qkv), *mark, *fc_marks[2]],
    )
    if pairwise:
        partial_a, _, _ = reduce_second(win, halves, grad_inputs)
    small_grads = sums_middle + sums_input
    grad_fc_bias = sums_hidden[:wide]
    vector_grads = jnp.concatenate(
        [
            small_grads.reshape(8, shards, owned_rows)
            .transpose(1, 0, 2)
            .reshape(shards, 8 * owned_rows),
            grad_fc_bias.reshape(shards, owned_rows * wide),
        ],
        axis=1,
    ).astype(BF16)
    vector_grads = jnp.pad(
        vector_grads.reshape(shards, vector_rows, width),
        ((0, 0), (0, -vector_rows % 16), (0, 0)),
    )
    blocked_grads = grad_inputs.reshape(blocked)
    if pairwise:
        vector_grads = held(vector_grads, partial_a)
        vector_grads = add_pair(vector_grads, swap(vector_grads, "ctx", 1))
        (owned_a,) = finish_units([partial_a])
        owned_proj, owned_fc = finish_units([partial_proj, partial_fc], vector_grads)
        input_grad, _ = to_blocks(blocked_grads, F32, vector_grads)
        owned_vectors = lax.dynamic_index_in_dim(
            reduce_vectors(vector_grads), lax.axis_index("shard"), keepdims=False
        )
    else:
        input_grad, _ = to_blocks(blocked_grads, F32)
        owned_proj = reduce_whole(partial_proj, transposed=True)
        owned_a, owned_fc = reduce_whole(partial_a), reduce_whole(partial_fc)
        owned_vectors = lax.psum_scatter(
            vector_grads, "shard", scatter_dimension=0, tiled=False
        )
        owned_vectors = lax.psum(owned_vectors, ("replica", "ctx"))
    owned_vectors = owned_vectors[:vector_rows].reshape(-1).astype(F32)
    vec = [owned_vectors[i * owned_rows : (i + 1) * owned_rows] for i in range(8)]
    qkv_grad = jnp.concatenate([owned_a[i] for i in range(3)], axis=1)
    fc_grad = jnp.concatenate([owned_fc[i] for i in range(wide)], axis=1)
    return (
        layer_out,
        input_grad,
        vec[0],
        vec[1],
        qkv_grad,
        vec[2],
        vec[3],
        owned_a[3],
        vec[4],
        vec[5],
        vec[6],
        fc_grad,
        owned_vectors[8 * owned_rows :],
        owned_proj.reshape(wide * owned_rows, width),
        vec[7],
    )


def solution(mesh):
    vector, matrix = P("shard"), P("shard", None)
    rows = P(("shard", "replica"), "ctx", None)
    weights = (
        vector,
        vector,
        matrix,
        vector,
        vector,
        matrix,
        vector,
        vector,
        vector,
        matrix,
        vector,
        matrix,
        vector,
    )
    return jax.shard_map(
        per_device,
        mesh=mesh,
        in_specs=(rows, rows, P()) + weights,
        out_specs=(rows, rows) + weights,
        check_vma=False,
    )
```

```python
import functools

import jax
import jax.numpy as jnp
from jax import lax
from jax.experimental import pallas as pl
from jax.experimental.layout import Layout, with_layout_constraint
from jax.experimental.pallas import tpu as pltpu
from jax.sharding import PartitionSpec as P

HEAD_DIM = 64
EPSILON = 1e-05
LANES = 128
VMEM_LIMIT = 56 * 1024 * 1024
COST_SCALE = 8

BF16 = jnp.bfloat16
F32 = jnp.float32


def dot_nn(left, right):
    return lax.dot_general(left, right, (((1,), (0,)), ((), ())), preferred_element_type=F32)


def dot_nt(left, right):
    return lax.dot_general(left, right, (((1,), (1,)), ((), ())), preferred_element_type=F32)


def dot_tn(left, right):
    return lax.dot_general(left, right, (((0,), (0,)), ((), ())), preferred_element_type=F32)


def head_lanes(shape, which):
    lane = lax.broadcasted_iota(jnp.int32, shape, 1)
    return (lane < HEAD_DIM) if which == 0 else (lane >= HEAD_DIM)


def only_valid(values, width):
    if width % LANES == 0:
        return values
    lane = lax.broadcasted_iota(jnp.int32, values.shape, 1) + pl.program_id(1) * LANES
    return jnp.where(lane < width, values, jnp.zeros_like(values))


def sorted_rows(ref, lead, order_ref, first, last):
    return jnp.concatenate([ref[lead + (order_ref[i], 0)] for i in range(first, last)], axis=0)


def store_rows(ref, lead, order_ref, first, rows):
    local = ref.shape[-2]
    for i in range(rows.shape[0] // local):
        ref[lead + (order_ref[first + i], 0)] = rows[i * local : (i + 1) * local]


def causal(rows, columns):
    key_at = lax.broadcasted_iota(jnp.int32, (rows, columns), 0)
    query_at = lax.broadcasted_iota(jnp.int32, (rows, columns), 1)
    return key_at <= query_at


def attention_forward_kernel(blocks, width, order_ref, q_ref, k_ref, v_ref, *refs):
    o_ref, lse_ref = refs[-2:]
    count, local = k_ref.shape[1], k_ref.shape[3]
    tile = blocks * local
    keys = only_valid(sorted_rows(k_ref, (0,), order_ref, 0, count), width)
    values_t = sorted_rows(v_ref, (0,), order_ref, 0, count).astype(F32).T.astype(BF16)
    diagonal = causal(tile, tile)
    for first in range(0, count, blocks):
        start, stop = first * local, (first + blocks) * local
        queries = sorted_rows(q_ref, (0,), order_ref, first, first + blocks)
        queries = queries * jnp.asarray(HEAD_DIM**-0.5, BF16)
        pieces = []
        for which in range(2):
            masked_q = jnp.where(head_lanes(queries.shape, which), queries, jnp.zeros_like(queries))
            scores = dot_nt(keys[:stop], masked_q)
            tiles = []
            if start > 0:
                tiles.append(scores[:start])
            tiles.append(jnp.where(diagonal, scores[start:], -1e30))
            top = functools.reduce(
                jnp.maximum, [jnp.max(block, axis=0, keepdims=True) for block in tiles]
            )
            weights = [jnp.exp(block - top) for block in tiles]
            total = sum(jnp.sum(weight, axis=0, keepdims=True) for weight in weights)
            low = jnp.concatenate([weight.astype(BF16) for weight in weights], axis=0)
            rows = values_t[which * HEAD_DIM : (which + 1) * HEAD_DIM, :stop]
            pieces.append(dot_nn(rows, low) * (1.0 / total))
            lse_ref[0, 0, which : which + 1, start:stop] = top + jnp.log(total)
        mixed_t = jnp.concatenate(pieces, axis=0)
        store_rows(o_ref, (), order_ref, first, mixed_t.T.astype(BF16))


def attention_backward_kernel(
    blocks,
    width,
    order_ref,
    q_ref,
    k_ref,
    v_ref,
    o_ref,
    do_ref,
    lse_ref,
    *refs,
):
    out_ref, dk_acc, dv_acc = refs[-3:]
    count, local = k_ref.shape[1], k_ref.shape[3]
    tile = blocks * local
    keys = only_valid(sorted_rows(k_ref, (0,), order_ref, 0, count), width)
    values = only_valid(sorted_rows(v_ref, (0,), order_ref, 0, count), width)
    keys_t = keys.astype(F32).T.astype(BF16)
    diagonal = causal(tile, tile)
    for first in range(0, count, blocks):
        start, stop = first * local, (first + blocks) * local
        queries = sorted_rows(q_ref, (0,), order_ref, first, first + blocks)
        queries = queries * jnp.asarray(HEAD_DIM**-0.5, BF16)
        grads = sorted_rows(do_ref, (), order_ref, first, first + blocks)
        mixed = sorted_rows(o_ref, (), order_ref, first, first + blocks)
        product_t = (grads.astype(F32) * mixed.astype(F32)).T
        key_lanes = head_lanes((stop, LANES), 0)
        dq_parts, dk_parts, dv_parts = [], [], []
        for which in range(2):
            mine = head_lanes(queries.shape, which)
            masked_q = jnp.where(mine, queries, jnp.zeros_like(queries))
            masked_g = jnp.where(mine, grads, jnp.zeros_like(grads))
            delta = jnp.sum(
                product_t[which * HEAD_DIM : (which + 1) * HEAD_DIM], axis=0, keepdims=True
            )
            lse = lse_ref[0, 0, which : which + 1, start:stop]
            scores = dot_nt(keys[:stop], masked_q)
            grad_weights = dot_nt(values[:stop], masked_g)
            weights = jnp.exp(scores - lse)
            if start > 0:
                weights = jnp.concatenate(
                    [weights[:start], jnp.where(diagonal, weights[start:], 0.0)], axis=0
                )
            else:
                weights = jnp.where(diagonal, weights, 0.0)
            low_scores = (weights * (grad_weights - delta)).astype(BF16)
            dv_parts.append(dot_nn(weights.astype(BF16), grads))
            dk_parts.append(dot_nn(low_scores, queries))
            dq_parts.append(
                dot_nn(keys_t[which * HEAD_DIM : (which + 1) * HEAD_DIM, :stop], low_scores)
            )
        dq_t = jnp.concatenate(dq_parts, axis=0) * (HEAD_DIM**-0.5)
        store_rows(out_ref, (0,), order_ref, first, dq_t.T.astype(BF16))
        dk = jnp.where(key_lanes, dk_parts[0], dk_parts[1])
        dv = jnp.where(key_lanes, dv_parts[0], dv_parts[1])
        if start > 0:
            dk_acc[:start] += dk[:start]
            dv_acc[:start] += dv[:start]
        dk_acc[start:stop] = dk[start:]
        dv_acc[start:stop] = dv[start:]
    store_rows(out_ref, (1,), order_ref, 0, dk_acc[...].astype(BF16))
    store_rows(out_ref, (2,), order_ref, 0, dv_acc[...].astype(BF16))


def query_blocks(count):
    return 2 if count % 2 == 0 else 1


def attention_forward(joined, order, ties=()):
    _, count, seqs, local, width = joined.shape
    length = count * local
    pairs = pl.cdiv(width, LANES)
    spec = lambda which: pl.BlockSpec(
        (1, count, 1, local, LANES), lambda s, h, order: (which, 0, s, 0, h)
    )
    return pl.pallas_call(
        functools.partial(attention_forward_kernel, query_blocks(count), width),
        grid_spec=pltpu.PrefetchScalarGridSpec(
            num_scalar_prefetch=1,
            grid=(seqs, pairs),
            in_specs=[spec(0), spec(1), spec(2)]
            + [pl.BlockSpec(memory_space=pl.ANY)] * len(ties),
            out_specs=[
                pl.BlockSpec((count, 1, local, LANES), lambda s, h, order: (0, s, 0, h)),
                pl.BlockSpec((1, 1, 8, length), lambda s, h, order: (s, h, 0, 0)),
            ],
        ),
        out_shape=[
            jax.ShapeDtypeStruct((count, seqs, local, width), BF16),
            jax.ShapeDtypeStruct((seqs, pairs, 8, length), F32),
        ],
        compiler_params=pltpu.CompilerParams(vmem_limit_bytes=VMEM_LIMIT),
        cost_estimate=pl.CostEstimate(
            flops=seqs * pairs * 16 * length * length * LANES // COST_SCALE,
            bytes_accessed=8 * seqs * length * width // COST_SCALE,
            transcendentals=0,
        ),
    )(order, joined, joined, joined, *ties)


def attention_backward(joined, mixed, grad_mixed, lse, order, ties=()):
    _, count, seqs, local, width = joined.shape
    length = count * local
    pairs = pl.cdiv(width, LANES)
    spec = lambda which: pl.BlockSpec(
        (1, count, 1, local, LANES), lambda s, h, order: (which, 0, s, 0, h)
    )
    rows = pl.BlockSpec((count, 1, local, LANES), lambda s, h, order: (0, s, 0, h))
    return pl.pallas_call(
        functools.partial(attention_backward_kernel, query_blocks(count), width),
        grid_spec=pltpu.PrefetchScalarGridSpec(
            num_scalar_prefetch=1,
            grid=(seqs, pairs),
            in_specs=[
                spec(0),
                spec(1),
                spec(2),
                rows,
                rows,
                pl.BlockSpec((1, 1, 8, length), lambda s, h, order: (s, h, 0, 0)),
            ]
            + [pl.BlockSpec(memory_space=pl.ANY)] * len(ties),
            out_specs=pl.BlockSpec(
                (3, count, 1, local, LANES), lambda s, h, order: (0, 0, s, 0, h)
            ),
            scratch_shapes=[pltpu.VMEM((length, LANES), F32), pltpu.VMEM((length, LANES), F32)],
        ),
        out_shape=jax.ShapeDtypeStruct(joined.shape, BF16),
        compiler_params=pltpu.CompilerParams(vmem_limit_bytes=VMEM_LIMIT),
        cost_estimate=pl.CostEstimate(
            flops=seqs * pairs * 20 * length * length * LANES // COST_SCALE,
            bytes_accessed=16 * seqs * length * width // COST_SCALE,
            transcendentals=0,
        ),
    )(order, joined, joined, joined, mixed, grad_mixed, lse, *ties)


def standardize(values):
    centred = values - jnp.mean(values, axis=-1, keepdims=True)
    inverse = lax.rsqrt(jnp.mean(centred * centred, axis=-1, keepdims=True) + EPSILON)
    return centred * inverse, inverse


def normalize_back(grad_out, standard, inverse, gain):
    scaled = grad_out * gain
    return inverse * (
        scaled
        - jnp.mean(scaled, axis=-1, keepdims=True)
        - standard * jnp.mean(scaled * standard, axis=-1, keepdims=True)
    )


def add_row(sums_ref, row, values):
    sums_ref[row : row + 1, :] += jnp.sum(values, axis=0, keepdims=True)


def clear_first(sums_ref):
    @pl.when(pl.program_id(0) == 0)
    def _():
        sums_ref[...] = jnp.zeros_like(sums_ref)


G_ONE, B_ONE, BIAS_Q, BIAS_V, BIAS_OUT, G_TWO, B_TWO, BIAS_PROJ = range(8)


def row(small_ref, index):
    return small_ref[index : index + 1, :]


def qkv_kernel(x_ref, w_ref, small_ref, *refs):
    joined_ref, low_ref = refs[-2:]
    standard, _ = standardize(x_ref[...].astype(F32))
    low = (standard * row(small_ref, G_ONE) + row(small_ref, B_ONE)).astype(BF16)
    low_ref[...] = low
    for which, bias in enumerate((BIAS_Q, None, BIAS_V)):
        out = dot_nn(low, w_ref[which])
        if bias is not None:
            out = out + row(small_ref, bias)
        joined_ref[which] = out.astype(BF16)


def attended_kernel(x_ref, o_ref, w_ref, small_ref, *refs):
    middle_ref, low_ref = refs[-2:]
    middle = x_ref[...].astype(F32) + dot_nn(o_ref[...], w_ref[0]) + row(small_ref, BIAS_OUT)
    middle_ref[...] = middle
    standard, _ = standardize(middle)
    low_ref[...] = (standard * row(small_ref, G_TWO) + row(small_ref, B_TWO)).astype(BF16)


def hidden_kernel(low_ref, w_ref, bias_ref, *refs):
    act_ref, slope_ref = refs[-2:]
    low = low_ref[...]
    scale = 0.7978845608028654
    for which in range(w_ref.shape[0]):
        hidden = dot_nn(low, w_ref[which]) + bias_ref[which]
        square = hidden * hidden
        bent = jnp.tanh(scale * hidden * (1.0 + 0.044715 * square))
        half = 0.5 * (1.0 + bent)
        act_ref[which] = (hidden * half).astype(BF16)
        slope = half + 0.5 * hidden * (1.0 - bent * bent) * (
            scale * (1.0 + 3.0 * 0.044715 * square)
        )
        slope_ref[which] = slope.astype(BF16)


def output_kernel(middle_ref, act_ref, w_ref, small_ref, *refs):
    out_ref = refs[-1]
    total = middle_ref[...] + row(small_ref, BIAS_PROJ)
    for which in range(w_ref.shape[0]):
        total += dot_nn(act_ref[which], w_ref[which])
    out_ref[...] = total.astype(BF16)


def hidden_back_kernel(grad_ref, slope_ref, w_ref, *refs):
    out_ref, sums_ref = refs[-2:]
    clear_first(sums_ref)
    grad = grad_ref[...]
    for which in range(w_ref.shape[0]):
        back = dot_nt(grad, w_ref[which]) * slope_ref[which].astype(F32)
        low = back.astype(BF16)
        out_ref[which] = low
        add_row(sums_ref, which, low.astype(F32))


def middle_back_kernel(hidden_ref, grad_ref, middle_ref, w_ref, out_w_ref, small_ref, *refs):
    grad_middle_ref, low_ref, mixed_ref, sums_ref = refs[-4:]
    clear_first(sums_ref)
    grad_two = dot_nt(hidden_ref[0], w_ref[0])
    for which in range(1, w_ref.shape[0]):
        grad_two += dot_nt(hidden_ref[which], w_ref[which])
    standard, inverse = standardize(middle_ref[...])
    grad_out = grad_ref[...].astype(F32)
    grad_middle = grad_out + normalize_back(grad_two, standard, inverse, row(small_ref, G_TWO))
    low = grad_middle.astype(BF16)
    grad_middle_ref[...] = grad_middle
    low_ref[...] = low
    mixed_ref[...] = dot_nt(low, out_w_ref[0]).astype(BF16)
    add_row(sums_ref, G_TWO, grad_two * standard)
    add_row(sums_ref, B_TWO, grad_two)
    add_row(sums_ref, BIAS_OUT, low.astype(F32))
    add_row(sums_ref, BIAS_PROJ, grad_out)


def input_back_kernel(joined_ref, grad_middle_ref, x_ref, w_ref, small_ref, *refs):
    out_ref, sums_ref = refs[-2:]
    clear_first(sums_ref)
    grad_one = dot_nt(joined_ref[0], w_ref[0])
    for which in range(1, 3):
        grad_one += dot_nt(joined_ref[which], w_ref[which])
    standard, inverse = standardize(x_ref[...].astype(F32))
    back = normalize_back(grad_one, standard, inverse, row(small_ref, G_ONE))
    out_ref[...] = (grad_middle_ref[...] + back).astype(BF16)
    add_row(sums_ref, G_ONE, grad_one * standard)
    add_row(sums_ref, B_ONE, grad_one)
    add_row(sums_ref, BIAS_Q, joined_ref[0].astype(F32))
    add_row(sums_ref, BIAS_V, joined_ref[2].astype(F32))


def by_rows(kernel, by_row, fixed, outs, sums=None, ties=(), tile=256):
    rows, width = by_row[0].shape[-2:]
    tile = tile if rows % tile == 0 else rows
    whole = lambda shape, index: pl.BlockSpec(
        shape, lambda i: index, pipeline_mode=pl.Buffered(buffer_count=1)
    )
    tiled = lambda lead: pl.BlockSpec(
        tuple(lead) + (tile, width), lambda i: (0,) * len(lead) + (i, 0)
    )
    in_specs = [tiled(array.shape[:-2]) for array in by_row]
    operands = list(by_row)
    products = 0
    for entry in fixed:
        array, first, blocks = entry if isinstance(entry, tuple) else (entry, 0, entry.shape[0])
        shape = (blocks,) + array.shape[1:]
        in_specs.append(whole(shape, (first // blocks,) + (0,) * (array.ndim - 1)))
        operands.append(array)
        if array.dtype == BF16:
            products += blocks
    in_specs += [pl.BlockSpec(memory_space=pl.ANY)] * len(ties)
    operands += list(ties)
    out_specs = [tiled(lead) for lead, _ in outs]
    out_shape = [jax.ShapeDtypeStruct(tuple(lead) + (rows, width), kind) for lead, kind in outs]
    if sums:
        out_specs.append(pl.BlockSpec((sums, width), lambda i: (0, 0)))
        out_shape.append(jax.ShapeDtypeStruct((sums, width), F32))
    moved = sum(array.size * array.dtype.itemsize for array in operands)
    moved += sum(leaf.size * leaf.dtype.itemsize for leaf in out_shape)
    return pl.pallas_call(
        kernel,
        grid=(rows // tile,),
        in_specs=in_specs,
        out_specs=out_specs,
        out_shape=out_shape,
        compiler_params=pltpu.CompilerParams(vmem_limit_bytes=VMEM_LIMIT),
        cost_estimate=pl.CostEstimate(
            flops=3 * rows * width * width * products // COST_SCALE,
            bytes_accessed=moved // COST_SCALE,
            transcendentals=0,
        ),
    )(*operands)


def row_major(values):
    return with_layout_constraint(values, Layout(major_to_minor=tuple(range(values.ndim))))


def swap(values, axis, offset):
    count = lax.axis_size(axis)
    return lax.ppermute(values, axis, [(index, index ^ offset) for index in range(count)])


def after(values, *earlier):
    return lax.optimization_barrier((values, *earlier))


def held(values, *earlier):
    if not earlier:
        return values
    wrong = jnp.zeros((), jnp.bool_)
    for array in earlier:
        entry = array[(0,) * array.ndim]
        wrong = wrong | (entry != entry)
    return jnp.where(wrong, jnp.zeros_like(values), values)


def pick(bit, on_zero, on_one):
    return jnp.where(bit == 0, on_zero, on_one)


def to_sequences(values, count, start=(), finish=()):
    seqs, local, width = values.shape
    own = lax.axis_index("ctx")
    parts = values.swapaxes(1, 2).reshape(count, seqs // count, width, local)
    mine = [lax.dynamic_index_in_dim(parts, own ^ i, keepdims=False) for i in range(count)]
    far = row_major(held(jnp.stack(mine[2:]), *start))
    far = row_major(swap(far, "ctx", 2))
    near = row_major(swap(row_major(jnp.stack([mine[1], far[1]])), "ctx", 1))
    whole = row_major(jnp.stack([mine[0], near[0], far[0], near[1]]))
    return row_major(held(whole, *finish).swapaxes(2, 3))


def to_blocks(values, kind, *start):
    count, share, local, width = values.shape
    own = lax.axis_index("ctx")
    values = row_major(held(values.swapaxes(2, 3), *start))
    far = row_major(swap(row_major(values[2:]), "ctx", 2))
    near = row_major(swap(row_major(jnp.stack([values[1], far[1]])), "ctx", 1))
    out = row_major(jnp.zeros((count, share, width, local), kind))
    for offset, piece in enumerate([values[0], near[0], far[0], near[1]]):
        out = lax.dynamic_update_index_in_dim(out, piece.astype(kind), own ^ offset, 0)
    out = row_major(out).reshape(count * share, width, local).swapaxes(1, 2)
    return out, near


class Windows:
    def __init__(self, owned_rows):
        tiles = owned_rows // 16
        self.start = tiles // 2 * 16
        self.size = owned_rows - self.start
        ctx = lax.axis_index("ctx")
        self.core = ctx % 2
        self.y = ctx // 2
        self.x = lax.axis_index("replica")

    def rows(self, values):
        return pick(
            self.core, values[..., : self.size, :], values[..., self.start :, :]
        )

    def other_rows(self, values):
        return pick(
            self.core, values[..., self.start :, :], values[..., : self.size, :]
        )

    def block(self, blocks):
        return pick(
            self.x,
            pick(self.y, blocks[0], blocks[1]),
            pick(self.y, blocks[2], blocks[3]),
        )


def assemble_kernel(groups, start, size, transposed, here_ref, *refs):
    arrays, out_ref = refs[:-1], refs[-1]
    x, y, core = here_ref[0], here_ref[1], here_ref[2]
    for turn in range(2):
        row = pl.multiple_of((core ^ turn) * start, 16)
        for (places, first), ref in zip(groups, arrays[turn * len(groups) :]):
            for i, (dx, dy) in enumerate(places):
                block = 2 * (x ^ dx) + (y ^ dy)
                for s in range(ref.shape[1]):
                    place = (first + s, block) if transposed else (block, first + s)
                    out_ref[place + (pl.ds(row, size), slice(None))] = ref[
                        i, s, :size, :
                    ].astype(out_ref.dtype)


def assemble(win, groups, own, other, owned_rows, shards, transposed, kind):
    width = own[0].shape[-1]
    here = jnp.stack([win.x, win.y, win.core]).astype(jnp.int32)
    shape = (shards, 4, owned_rows, width) if transposed else (4, shards, owned_rows, width)
    return pl.pallas_call(
        functools.partial(assemble_kernel, groups, win.start, win.size, transposed),
        in_specs=[pl.BlockSpec(memory_space=pltpu.SMEM)]
        + [pl.BlockSpec(memory_space=pltpu.VMEM)] * (2 * len(groups)),
        out_specs=pl.BlockSpec(memory_space=pltpu.VMEM),
        out_shape=jax.ShapeDtypeStruct(shape, kind),
        compiler_params=pltpu.CompilerParams(vmem_limit_bytes=VMEM_LIMIT),
        cost_estimate=pl.CostEstimate(
            flops=0, bytes_accessed=16 * shards * owned_rows * width, transcendentals=0
        ),
    )(here, *own, *other)


def spread_chips(mine):
    shards = mine.shape[0]
    if shards == 1:
        first = jnp.stack([mine, swap(mine, "replica", 1)])
        return [first, swap(first, "ctx", 2)]
    split = shards // 2
    low, high = mine[:split], mine[split:]
    low_there, high_there = after(swap(low, "replica", 1), swap(high, "ctx", 2))
    first = jnp.stack([low, low_there])
    second = jnp.stack([high, high_there])
    third, fourth = after(swap(first, "ctx", 2), swap(second, "replica", 1))
    return [first, second, third, fourth]


def chip_groups(shards):
    if shards == 1:
        return ((((0, 0), (1, 0)), 0), (((0, 1), (1, 1)), 0))
    return (
        (((0, 0), (1, 0)), 0),
        (((0, 0), (0, 1)), shards // 2),
        (((0, 1), (1, 1)), 0),
        (((1, 0), (1, 1)), shards // 2),
    )


def spread_cores(own):
    return [swap(array, "ctx", 1) for array in own]


def place(win, own, other, owned_rows, shards, transposed=False, kind=BF16):
    return assemble(win, chip_groups(shards), own, other, owned_rows, shards, transposed, kind)


def grads_kernel(groups, start, size, forms, here_ref, *refs):
    total = sum(len(form) for form in forms)
    arrays, outs = refs[:-total], refs[-total:]
    x, y, core = here_ref[0], here_ref[1], here_ref[2]

    def put(form, targets, block, row, values):
        width = values.shape[-1]
        if form == (0,):
            owned = targets[0].shape[0] // 4
            at = pl.multiple_of(block * owned + row, 16)
            targets[0][pl.ds(at, size), :] = values
            return
        first = 0
        for wide, ref in zip(form, targets):
            for i in range(wide):

                @pl.when(block == first + i)
                def _():
                    ref[pl.ds(row, size), i * width : (i + 1) * width] = values

            first += wide

    for turn in range(2):
        row = pl.multiple_of((core ^ turn) * start, 16)
        for (places, first), ref in zip(groups, arrays[turn * len(groups) :]):
            for i, (dx, dy) in enumerate(places):
                block = 2 * (x ^ dx) + (y ^ dy)
                for s in range(ref.shape[1]):
                    before = sum(len(form) for form in forms[: first + s])
                    targets = outs[before : before + len(forms[first + s])]
                    put(forms[first + s], targets, block, row, ref[i, s].astype(F32))


def place_grads(win, own, other, owned_rows, forms):
    width = own[0].shape[-1]
    here = jnp.stack([win.x, win.y, win.core]).astype(jnp.int32)
    shapes = [
        (owned_rows, wide * width) if wide else (4 * owned_rows, width)
        for form in forms
        for wide in form
    ]
    groups = chip_groups(len(forms))
    return pl.pallas_call(
        functools.partial(grads_kernel, groups, win.start, win.size, forms),
        in_specs=[pl.BlockSpec(memory_space=pltpu.SMEM)]
        + [pl.BlockSpec(memory_space=pltpu.VMEM)] * (2 * len(groups)),
        out_specs=[pl.BlockSpec(memory_space=pltpu.VMEM)] * len(shapes),
        out_shape=[jax.ShapeDtypeStruct(shape, F32) for shape in shapes],
        compiler_params=pltpu.CompilerParams(vmem_limit_bytes=VMEM_LIMIT),
        cost_estimate=pl.CostEstimate(
            flops=0, bytes_accessed=4 * owned_rows * width * len(forms), transcendentals=0
        ),
    )(here, *own, *other)


def add_pair(kept, received):
    return (kept.astype(F32) + received.astype(F32)).astype(BF16)


def corner(values):
    return values[(0,) * (values.ndim - 2)][:16, :LANES]


def reduce_first(win, grads, transposed):
    shards = grads.shape[0 if transposed else 1]
    split = shards // 2

    def part(values, blocks, which):
        return values[which, blocks] if transposed else values[blocks, which]

    lower, upper = slice(None, split), slice(split, None)
    entry = lambda values, i: values[:, i] if transposed else values[i]
    received = swap(win.other_rows(grads), "ctx", 1)
    both = add_pair(win.rows(grads), received)
    by_x = [part(both, slice(2 * i, 2 * i + 2), lower) for i in range(2)]
    by_y = [part(both, slice(i, None, 2), upper) for i in range(2)]
    x_sent = row_major(pick(win.x, by_x[1], by_x[0]))
    y_sent = row_major(pick(win.y, by_y[1], by_y[0]))
    x_received, y_received = after(
        row_major(swap(x_sent, "replica", 1)), row_major(swap(y_sent, "ctx", 2))
    )
    low = row_major(add_pair(pick(win.x, *by_x), x_received))
    high = row_major(add_pair(pick(win.y, *by_y), y_received))
    low, high = [entry(low, i) for i in range(2)], [entry(high, i) for i in range(2)]
    return (low, high), [corner(x_sent), corner(y_sent)]


def reduce_second(win, halves, *earlier):
    low, high = halves
    low_sent, high_sent = pick(win.y, low[1], low[0]), pick(win.x, high[1], high[0])
    if earlier:
        low_sent, high_sent = held(low_sent, *earlier), held(high_sent, *earlier)
    low_received, high_received = after(
        swap(low_sent, "ctx", 2), swap(high_sent, "replica", 1)
    )
    low_sum = add_pair(pick(win.y, *low), low_received)
    high_sum = add_pair(pick(win.x, *high), high_received)
    sums = jnp.concatenate([low_sum, high_sum], axis=0)
    return sums, [corner(low_sent)], [corner(sums)]


def reduce_vectors(values):
    values = add_pair(values, swap(values, "ctx", 1))
    values = add_pair(values, swap(values, "replica", 1))
    step = 1
    while step < lax.axis_size("shard"):
        values = add_pair(values, swap(values, "shard", step))
        step *= 2
    return values


def per_device(
    tokens,
    cotangent,
    block_order,
    ln1_gain,
    ln1_bias,
    qkv_weight,
    q_bias,
    v_bias,
    out_weight,
    out_bias,
    ln2_gain,
    ln2_bias,
    fc_weight,
    fc_bias,
    proj_weight,
    proj_bias,
):
    seq_count, local_len, width = tokens.shape
    owned_rows = ln1_gain.shape[0]
    shards = width // owned_rows
    wide = fc_weight.shape[1] // width
    count = lax.axis_size("ctx")
    rows = seq_count * local_len
    pairwise = lax.axis_size("replica") == 2 and count == 4 and shards == 4
    win = Windows(owned_rows)

    vectors = jnp.concatenate(
        [ln1_gain, ln1_bias, q_bias, v_bias, out_bias, ln2_gain, ln2_bias, proj_bias, fc_bias]
    )
    vector_rows = vectors.shape[0] // width
    vector_tile = jnp.pad(vectors.reshape(vector_rows, width), ((0, -vector_rows % 16), (0, 0)))
    column = lambda values, i: values[:, i * width : (i + 1) * width]
    blocks_a = [column(qkv_weight, i) for i in range(3)] + [out_weight]
    blocks_b = [column(fc_weight, i) for i in range(wide)]
    blocks_c = [proj_weight[i * owned_rows : (i + 1) * owned_rows] for i in range(wide)]

    def gather_z(values):
        return lax.all_gather(values, "shard", axis=0, tiled=False)

    low_inputs = to_sequences(tokens, count).reshape(rows, width)

    if pairwise:
        mine = [win.rows(win.block(blocks)) for blocks in (blocks_a, blocks_b, blocks_c)]
        part_a = gather_z(mine[0])
        mine_b, part_a = after(jnp.concatenate([mine[1], vector_tile], axis=0), part_a)
        part_b = gather_z(mine_b)
        mine_c, part_b = after(mine[2], part_b)
        part_c = gather_z(mine_c)
        part_a, low_inputs = after(part_a, low_inputs)
        own_a = spread_chips(part_a)
        other_a = spread_cores(own_a)
        full_a = place(win, own_a, other_a, owned_rows, shards)
        vector_part = part_b[:, win.size : win.size + vector_rows]
        own_b = spread_chips(held(part_b[:, : win.size], own_a[2]))
    else:
        vector_part = gather_z(vector_tile)[:, :vector_rows]
        full_a, full_b, full_c = [
            gather_z(jnp.stack(blocks)) for blocks in (blocks_a, blocks_b, blocks_c)
        ]
        full_a, full_b = full_a.transpose(1, 0, 2, 3), full_b.transpose(1, 0, 2, 3)
    w_a = full_a.reshape(4, width, width)
    vector_part = vector_part.reshape(shards, vector_rows * width).astype(F32)
    small = vector_part[:, : 8 * owned_rows].reshape(shards, 8, owned_rows)
    small = small.transpose(1, 0, 2).reshape(8, width)
    bias_fc = vector_part[:, 8 * owned_rows :].reshape(wide, 1, width)

    share = seq_count // count
    blocked = (count, share, local_len, width)
    index = jnp.arange(count, dtype=jnp.int32)
    held_by = jnp.sum(jnp.where(block_order[None, :] == index[:, None], index[None, :], 0), axis=1)
    order = (held_by ^ lax.axis_index("ctx")).astype(jnp.int32)

    steps = [corner(own_b[0][1]), corner(own_b[1][1])] if pairwise else []
    joined, low_one = by_rows(
        qkv_kernel, [low_inputs], [(w_a, 0, 3), small], [((3,), BF16), ((), BF16)], ties=steps
    )
    joined = joined.reshape((3,) + blocked)
    if pairwise:
        other_b = spread_cores(own_b)
        full_b = place(win, own_b, other_b, owned_rows, shards)
        own_c = spread_chips(held(part_c, own_b[2], joined))
        steps = [corner(own_c[0][1]), corner(own_c[1][1]), corner(own_c[2]), corner(own_c[3])]
    else:
        steps = [corner(joined[0, 0])] * 4
    mixed, lse = attention_forward(joined, order, ties=steps[:2])
    attended = mixed.reshape(rows, width)
    middle, low_two = by_rows(
        attended_kernel,
        [low_inputs, attended],
        [(w_a, 3, 1), small],
        [((), F32), ((), BF16)],
    )
    w_fc = full_b.reshape(wide, width, width)
    low_act, slope = by_rows(
        hidden_kernel,
        [low_two],
        [w_fc, bias_fc],
        [((wide,), BF16), ((wide,), BF16)],
        ties=steps[2:],
    )
    if pairwise:
        full_c = place(win, own_c, spread_cores(own_c), owned_rows, shards, transposed=True)
    w_proj = full_c.reshape(wide, width, width)
    start, finish = ((own_c[2], mixed), (full_c,)) if pairwise else ((), ())
    low_grad_out = to_sequences(cotangent, count, start, finish).reshape(rows, width)

    def finish_units(groups, forms, *earlier):
        sums = [
            lax.psum_scatter(group, "shard", scatter_dimension=0, tiled=False)
            for group in groups
        ]
        own = spread_chips(held(jnp.stack(sums), *earlier))
        return own, place_grads(win, own, spread_cores(own), owned_rows, forms)

    def reduce_whole(grads, transposed=False):
        if transposed:
            grads = grads.transpose(1, 0, 2, 3)
        full = lax.psum_scatter(grads, "shard", scatter_dimension=1, tiled=False)
        return lax.psum(full, ("replica", "ctx")).astype(F32)

    def start_units(grads, transposed=False):
        if not pairwise:
            return grads, ((), (), ())
        halves, first = reduce_first(win, grads, transposed)
        sums, second, last = reduce_second(win, halves)
        return sums, (first, second, last)

    def by_shard(grads):
        return grads.astype(BF16).reshape(4, shards, owned_rows, width)

    grad_proj = jnp.einsum("ctx,td->cxd", low_act, low_grad_out, preferred_element_type=F32)
    grad_proj = grad_proj.astype(BF16)
    partial_proj, proj_marks = start_units(by_shard(grad_proj), transposed=True)
    (outputs,) = by_rows(
        output_kernel,
        [middle, low_act],
        [w_proj, small],
        [((), BF16)],
        ties=[corner(grad_proj)],
    )
    grad_hidden, sums_hidden = by_rows(
        hidden_back_kernel,
        [low_grad_out, slope],
        [w_proj],
        [((wide,), BF16)],
        sums=8,
        ties=[corner(outputs), *proj_marks[0]],
    )
    grad_fc = jnp.einsum("td,ctx->cdx", low_two, grad_hidden, preferred_element_type=F32)
    grad_fc = grad_fc.astype(BF16)
    partial_fc, fc_marks = start_units(by_shard(grad_fc))
    layer_out, returned = to_blocks(outputs.reshape(blocked), BF16, *proj_marks[1])
    grad_middle, low_grad_middle, grad_mixed, sums_middle = by_rows(
        middle_back_kernel,
        [grad_hidden, low_grad_out, middle],
        [w_fc, (w_a, 3, 1), small],
        [((), F32), ((), BF16), ((), BF16)],
        sums=8,
        ties=[corner(grad_fc), *proj_marks[1]],
    )
    grad_out_weight = dot_tn(attended, low_grad_middle).astype(BF16)
    grad_joined = attention_backward(
        joined,
        mixed,
        grad_mixed.reshape(blocked),
        lse,
        order,
        ties=[corner(grad_out_weight), corner(returned), *proj_marks[2], *fc_marks[0]],
    ).reshape(3, rows, width)
    grad_qkv = jnp.einsum("td,ctx->cdx", low_one, grad_joined, preferred_element_type=F32)
    grad_qkv = grad_qkv.astype(BF16)
    grads_a = jnp.concatenate([grad_qkv, grad_out_weight[None]], axis=0)
    partial_a, mark = by_shard(grads_a), ()
    if pairwise:
        halves, mark = reduce_first(win, partial_a, False)
    grad_inputs, sums_input = by_rows(
        input_back_kernel,
        [grad_joined, grad_middle, low_inputs],
        [(w_a, 0, 3), small],
        [((), BF16)],
        sums=8,
        ties=[corner(grad_qkv), *mark, *fc_marks[2]],
    )
    if pairwise:
        partial_a, _, _ = reduce_second(win, halves, grad_inputs)
    small_grads = sums_middle + sums_input
    grad_fc_bias = sums_hidden[:wide]
    vector_grads = jnp.concatenate(
        [
            small_grads.reshape(8, shards, owned_rows)
            .transpose(1, 0, 2)
            .reshape(shards, 8 * owned_rows),
            grad_fc_bias.reshape(shards, owned_rows * wide),
        ],
        axis=1,
    ).astype(BF16)
    vector_grads = jnp.pad(
        vector_grads.reshape(shards, vector_rows, width),
        ((0, 0), (0, -vector_rows % 16), (0, 0)),
    )
    blocked_grads = grad_inputs.reshape(blocked)
    if pairwise:
        vector_grads = held(vector_grads, partial_a)
        vector_grads = add_pair(vector_grads, swap(vector_grads, "ctx", 2))
        _, (qkv_grad, out_grad) = finish_units([partial_a], ((3, 1),))
        own, (proj_grad, fc_grad) = finish_units(
            [partial_proj, partial_fc], ((0,), (wide,)), vector_grads
        )
        input_grad, _ = to_blocks(blocked_grads, F32, own[0][1], own[1][1])
        owned_vectors = lax.dynamic_index_in_dim(
            reduce_vectors(vector_grads), lax.axis_index("shard"), keepdims=False
        )
    else:
        input_grad, _ = to_blocks(blocked_grads, F32)
        owned_proj = reduce_whole(partial_proj, transposed=True)
        owned_a, owned_fc = reduce_whole(partial_a), reduce_whole(partial_fc)
        owned_vectors = lax.psum_scatter(
            vector_grads, "shard", scatter_dimension=0, tiled=False
        )
        owned_vectors = lax.psum(owned_vectors, ("replica", "ctx"))
        side_by_side = lambda blocks: jnp.concatenate(list(blocks), axis=1)
        qkv_grad, out_grad = side_by_side(owned_a[:3]), owned_a[3]
        fc_grad = side_by_side(owned_fc)
        proj_grad = owned_proj.reshape(wide * owned_rows, width)
    owned_vectors = owned_vectors[:vector_rows].reshape(-1).astype(F32)
    vec = [owned_vectors[i * owned_rows : (i + 1) * owned_rows] for i in range(8)]
    return (
        layer_out,
        input_grad,
        vec[0],
        vec[1],
        qkv_grad,
        vec[2],
        vec[3],
        out_grad,
        vec[4],
        vec[5],
        vec[6],
        fc_grad,
        owned_vectors[8 * owned_rows :],
        proj_grad,
        vec[7],
    )


def solution(mesh):
    vector, matrix = P("shard"), P("shard", None)
    rows = P(("shard", "replica"), "ctx", None)
    weights = (
        vector,
        vector,
        matrix,
        vector,
        vector,
        matrix,
        vector,
        vector,
        vector,
        matrix,
        vector,
        matrix,
        vector,
    )
    return jax.shard_map(
        per_device,
        mesh=mesh,
        in_specs=(rows, rows, P()) + weights,
        out_specs=(rows, rows) + weights,
        check_vma=False,
    )
```

```python
import functools

import jax
import jax.numpy as jnp
from jax import lax
from jax.experimental import pallas as pl
from jax.experimental.layout import Layout, with_layout_constraint
from jax.experimental.pallas import tpu as pltpu
from jax.sharding import PartitionSpec as P

HEAD_DIM = 64
EPSILON = 1e-05
LANES = 128
VMEM_LIMIT = 56 * 1024 * 1024
COST_SCALE = 8

BF16 = jnp.bfloat16
F32 = jnp.float32


def dot_nn(left, right):
    return lax.dot_general(left, right, (((1,), (0,)), ((), ())), preferred_element_type=F32)


def dot_nt(left, right):
    return lax.dot_general(left, right, (((1,), (1,)), ((), ())), preferred_element_type=F32)


def dot_tn(left, right):
    return lax.dot_general(left, right, (((0,), (0,)), ((), ())), preferred_element_type=F32)


def head_lanes(shape, which):
    lane = lax.broadcasted_iota(jnp.int32, shape, 1)
    return (lane < HEAD_DIM) if which == 0 else (lane >= HEAD_DIM)


def only_valid(values, width):
    if width % LANES == 0:
        return values
    lane = lax.broadcasted_iota(jnp.int32, values.shape, 1) + pl.program_id(1) * LANES
    return jnp.where(lane < width, values, jnp.zeros_like(values))


def sorted_rows(ref, lead, order_ref, first, last):
    return jnp.concatenate([ref[lead + (order_ref[i], 0)] for i in range(first, last)], axis=0)


def store_rows(ref, lead, order_ref, first, rows):
    local = ref.shape[-2]
    for i in range(rows.shape[0] // local):
        ref[lead + (order_ref[first + i], 0)] = rows[i * local : (i + 1) * local]


def causal(rows, columns):
    key_at = lax.broadcasted_iota(jnp.int32, (rows, columns), 0)
    query_at = lax.broadcasted_iota(jnp.int32, (rows, columns), 1)
    return key_at <= query_at


def attention_forward_kernel(blocks, width, order_ref, q_ref, k_ref, v_ref, *refs):
    o_ref, lse_ref = refs[-2:]
    count, local = k_ref.shape[1], k_ref.shape[3]
    tile = blocks * local
    keys = only_valid(sorted_rows(k_ref, (0,), order_ref, 0, count), width)
    values_t = sorted_rows(v_ref, (0,), order_ref, 0, count).astype(F32).T.astype(BF16)
    diagonal = causal(tile, tile)
    for first in range(0, count, blocks):
        start, stop = first * local, (first + blocks) * local
        queries = sorted_rows(q_ref, (0,), order_ref, first, first + blocks)
        queries = queries * jnp.asarray(HEAD_DIM**-0.5, BF16)
        pieces = []
        for which in range(2):
            masked_q = jnp.where(head_lanes(queries.shape, which), queries, jnp.zeros_like(queries))
            scores = dot_nt(keys[:stop], masked_q)
            tiles = []
            if start > 0:
                tiles.append(scores[:start])
            tiles.append(jnp.where(diagonal, scores[start:], -1e30))
            top = functools.reduce(
                jnp.maximum, [jnp.max(block, axis=0, keepdims=True) for block in tiles]
            )
            weights = [jnp.exp(block - top) for block in tiles]
            total = sum(jnp.sum(weight, axis=0, keepdims=True) for weight in weights)
            low = jnp.concatenate([weight.astype(BF16) for weight in weights], axis=0)
            rows = values_t[which * HEAD_DIM : (which + 1) * HEAD_DIM, :stop]
            pieces.append(dot_nn(rows, low) * (1.0 / total))
            lse_ref[0, 0, which : which + 1, start:stop] = top + jnp.log(total)
        mixed_t = jnp.concatenate(pieces, axis=0)
        store_rows(o_ref, (), order_ref, first, mixed_t.T.astype(BF16))


def attention_backward_kernel(
    blocks,
    width,
    order_ref,
    q_ref,
    k_ref,
    v_ref,
    o_ref,
    do_ref,
    lse_ref,
    *refs,
):
    out_ref, dk_acc, dv_acc = refs[-3:]
    count, local = k_ref.shape[1], k_ref.shape[3]
    tile = blocks * local
    keys = only_valid(sorted_rows(k_ref, (0,), order_ref, 0, count), width)
    values = only_valid(sorted_rows(v_ref, (0,), order_ref, 0, count), width)
    keys_t = keys.astype(F32).T.astype(BF16)
    diagonal = causal(tile, tile)
    for first in range(0, count, blocks):
        start, stop = first * local, (first + blocks) * local
        queries = sorted_rows(q_ref, (0,), order_ref, first, first + blocks)
        queries = queries * jnp.asarray(HEAD_DIM**-0.5, BF16)
        grads = sorted_rows(do_ref, (), order_ref, first, first + blocks)
        mixed = sorted_rows(o_ref, (), order_ref, first, first + blocks)
        product_t = (grads.astype(F32) * mixed.astype(F32)).T
        key_lanes = head_lanes((stop, LANES), 0)
        dq_parts, dk_parts, dv_parts = [], [], []
        for which in range(2):
            mine = head_lanes(queries.shape, which)
            masked_q = jnp.where(mine, queries, jnp.zeros_like(queries))
            masked_g = jnp.where(mine, grads, jnp.zeros_like(grads))
            delta = jnp.sum(
                product_t[which * HEAD_DIM : (which + 1) * HEAD_DIM], axis=0, keepdims=True
            )
            lse = lse_ref[0, 0, which : which + 1, start:stop]
            scores = dot_nt(keys[:stop], masked_q)
            grad_weights = dot_nt(values[:stop], masked_g)
            weights = jnp.exp(scores - lse)
            if start > 0:
                weights = jnp.concatenate(
                    [weights[:start], jnp.where(diagonal, weights[start:], 0.0)], axis=0
                )
            else:
                weights = jnp.where(diagonal, weights, 0.0)
            low_scores = (weights * (grad_weights - delta)).astype(BF16)
            dv_parts.append(dot_nn(weights.astype(BF16), grads))
            dk_parts.append(dot_nn(low_scores, queries))
            dq_parts.append(
                dot_nn(keys_t[which * HEAD_DIM : (which + 1) * HEAD_DIM, :stop], low_scores)
            )
        dq_t = jnp.concatenate(dq_parts, axis=0) * (HEAD_DIM**-0.5)
        store_rows(out_ref, (0,), order_ref, first, dq_t.T.astype(BF16))
        dk = jnp.where(key_lanes, dk_parts[0], dk_parts[1])
        dv = jnp.where(key_lanes, dv_parts[0], dv_parts[1])
        if start > 0:
            dk_acc[:start] += dk[:start]
            dv_acc[:start] += dv[:start]
        dk_acc[start:stop] = dk[start:]
        dv_acc[start:stop] = dv[start:]
    store_rows(out_ref, (1,), order_ref, 0, dk_acc[...].astype(BF16))
    store_rows(out_ref, (2,), order_ref, 0, dv_acc[...].astype(BF16))


def query_blocks(count):
    return 2 if count % 2 == 0 else 1


def attention_forward(joined, order, first, last, into=(), ties=()):
    _, count, seqs, local, width = joined.shape
    length = count * local
    pairs = pl.cdiv(width, LANES)
    spec = lambda which: pl.BlockSpec(
        (1, count, 1, local, LANES), lambda s, h, order: (which, 0, s + first, 0, h)
    )
    extra = list(into) + list(ties)
    return pl.pallas_call(
        functools.partial(attention_forward_kernel, query_blocks(count), width),
        grid_spec=pltpu.PrefetchScalarGridSpec(
            num_scalar_prefetch=1,
            grid=(last - first, pairs),
            in_specs=[spec(0), spec(1), spec(2)]
            + [pl.BlockSpec(memory_space=pl.ANY)] * len(extra),
            out_specs=[
                pl.BlockSpec((count, 1, local, LANES), lambda s, h, order: (0, s + first, 0, h)),
                pl.BlockSpec((1, 1, 8, length), lambda s, h, order: (s + first, h, 0, 0)),
            ],
        ),
        out_shape=[
            jax.ShapeDtypeStruct((count, seqs, local, width), BF16),
            jax.ShapeDtypeStruct((seqs, pairs, 8, length), F32),
        ],
        input_output_aliases={4 + i: i for i in range(len(into))},
        compiler_params=pltpu.CompilerParams(vmem_limit_bytes=VMEM_LIMIT),
        cost_estimate=pl.CostEstimate(
            flops=(last - first) * pairs * 16 * length * length * LANES // COST_SCALE,
            bytes_accessed=8 * (last - first) * length * width // COST_SCALE,
            transcendentals=0,
        ),
    )(order, joined, joined, joined, *extra)


def attention_backward(joined, mixed, grad_mixed, lse, order, ties=()):
    _, count, seqs, local, width = joined.shape
    length = count * local
    pairs = pl.cdiv(width, LANES)
    spec = lambda which: pl.BlockSpec(
        (1, count, 1, local, LANES), lambda s, h, order: (which, 0, s, 0, h)
    )
    rows = pl.BlockSpec((count, 1, local, LANES), lambda s, h, order: (0, s, 0, h))
    return pl.pallas_call(
        functools.partial(attention_backward_kernel, query_blocks(count), width),
        grid_spec=pltpu.PrefetchScalarGridSpec(
            num_scalar_prefetch=1,
            grid=(seqs, pairs),
            in_specs=[
                spec(0),
                spec(1),
                spec(2),
                rows,
                rows,
                pl.BlockSpec((1, 1, 8, length), lambda s, h, order: (s, h, 0, 0)),
            ]
            + [pl.BlockSpec(memory_space=pl.ANY)] * len(ties),
            out_specs=pl.BlockSpec(
                (3, count, 1, local, LANES), lambda s, h, order: (0, 0, s, 0, h)
            ),
            scratch_shapes=[pltpu.VMEM((length, LANES), F32), pltpu.VMEM((length, LANES), F32)],
        ),
        out_shape=jax.ShapeDtypeStruct(joined.shape, BF16),
        compiler_params=pltpu.CompilerParams(vmem_limit_bytes=VMEM_LIMIT),
        cost_estimate=pl.CostEstimate(
            flops=seqs * pairs * 20 * length * length * LANES // COST_SCALE,
            bytes_accessed=16 * seqs * length * width // COST_SCALE,
            transcendentals=0,
        ),
    )(order, joined, joined, joined, mixed, grad_mixed, lse, *ties)


def standardize(values):
    centred = values - jnp.mean(values, axis=-1, keepdims=True)
    inverse = lax.rsqrt(jnp.mean(centred * centred, axis=-1, keepdims=True) + EPSILON)
    return centred * inverse, inverse


def normalize_back(grad_out, standard, inverse, gain):
    scaled = grad_out * gain
    return inverse * (
        scaled
        - jnp.mean(scaled, axis=-1, keepdims=True)
        - standard * jnp.mean(scaled * standard, axis=-1, keepdims=True)
    )


def add_row(sums_ref, row, values):
    sums_ref[row : row + 1, :] += jnp.sum(values, axis=0, keepdims=True)


def clear_first(sums_ref):
    @pl.when(pl.program_id(0) == 0)
    def _():
        sums_ref[...] = jnp.zeros_like(sums_ref)


G_ONE, B_ONE, BIAS_Q, BIAS_V, BIAS_OUT, G_TWO, B_TWO, BIAS_PROJ = range(8)


def row(small_ref, index):
    return small_ref[index : index + 1, :]


def qkv_kernel(x_ref, w_ref, small_ref, *refs):
    joined_ref, low_ref = refs[-2:]
    standard, _ = standardize(x_ref[...].astype(F32))
    low = (standard * row(small_ref, G_ONE) + row(small_ref, B_ONE)).astype(BF16)
    low_ref[...] = low
    for which, bias in enumerate((BIAS_Q, None, BIAS_V)):
        out = dot_nn(low, w_ref[which])
        if bias is not None:
            out = out + row(small_ref, bias)
        joined_ref[which] = out.astype(BF16)


def attended_kernel(x_ref, o_ref, w_ref, small_ref, *refs):
    middle_ref, low_ref = refs[-2:]
    middle = x_ref[...].astype(F32) + dot_nn(o_ref[...], w_ref[0]) + row(small_ref, BIAS_OUT)
    middle_ref[...] = middle
    standard, _ = standardize(middle)
    low_ref[...] = (standard * row(small_ref, G_TWO) + row(small_ref, B_TWO)).astype(BF16)


def hidden_kernel(low_ref, w_ref, bias_ref, *refs):
    act_ref, slope_ref = refs[-2:]
    low = low_ref[...]
    scale = 0.7978845608028654
    for which in range(w_ref.shape[0]):
        hidden = dot_nn(low, w_ref[which]) + bias_ref[which]
        square = hidden * hidden
        bent = jnp.tanh(scale * hidden * (1.0 + 0.044715 * square))
        half = 0.5 * (1.0 + bent)
        act_ref[which] = (hidden * half).astype(BF16)
        slope = half + 0.5 * hidden * (1.0 - bent * bent) * (
            scale * (1.0 + 3.0 * 0.044715 * square)
        )
        slope_ref[which] = slope.astype(BF16)


def output_kernel(middle_ref, act_ref, w_ref, small_ref, *refs):
    out_ref = refs[-1]
    total = middle_ref[...] + row(small_ref, BIAS_PROJ)
    for which in range(w_ref.shape[0]):
        total += dot_nn(act_ref[which], w_ref[which])
    out_ref[...] = total.astype(BF16)


def hidden_back_kernel(grad_ref, slope_ref, w_ref, *refs):
    out_ref, sums_ref = refs[-2:]
    clear_first(sums_ref)
    grad = grad_ref[...]
    for which in range(w_ref.shape[0]):
        back = dot_nt(grad, w_ref[which]) * slope_ref[which].astype(F32)
        low = back.astype(BF16)
        out_ref[which] = low
        add_row(sums_ref, which, low.astype(F32))


def middle_back_kernel(hidden_ref, grad_ref, middle_ref, w_ref, out_w_ref, small_ref, *refs):
    grad_middle_ref, low_ref, mixed_ref, sums_ref = refs[-4:]
    clear_first(sums_ref)
    grad_two = dot_nt(hidden_ref[0], w_ref[0])
    for which in range(1, w_ref.shape[0]):
        grad_two += dot_nt(hidden_ref[which], w_ref[which])
    standard, inverse = standardize(middle_ref[...])
    grad_out = grad_ref[...].astype(F32)
    grad_middle = grad_out + normalize_back(grad_two, standard, inverse, row(small_ref, G_TWO))
    low = grad_middle.astype(BF16)
    grad_middle_ref[...] = grad_middle
    low_ref[...] = low
    mixed_ref[...] = dot_nt(low, out_w_ref[0]).astype(BF16)
    add_row(sums_ref, G_TWO, grad_two * standard)
    add_row(sums_ref, B_TWO, grad_two)
    add_row(sums_ref, BIAS_OUT, low.astype(F32))
    add_row(sums_ref, BIAS_PROJ, grad_out)


def input_back_kernel(joined_ref, grad_middle_ref, x_ref, w_ref, small_ref, *refs):
    out_ref, sums_ref = refs[-2:]
    clear_first(sums_ref)
    grad_one = dot_nt(joined_ref[0], w_ref[0])
    for which in range(1, 3):
        grad_one += dot_nt(joined_ref[which], w_ref[which])
    standard, inverse = standardize(x_ref[...].astype(F32))
    back = normalize_back(grad_one, standard, inverse, row(small_ref, G_ONE))
    out_ref[...] = (grad_middle_ref[...] + back).astype(BF16)
    add_row(sums_ref, G_ONE, grad_one * standard)
    add_row(sums_ref, B_ONE, grad_one)
    add_row(sums_ref, BIAS_Q, joined_ref[0].astype(F32))
    add_row(sums_ref, BIAS_V, joined_ref[2].astype(F32))


def by_rows(kernel, by_row, fixed, outs, sums=None, ties=(), tile=256):
    rows, width = by_row[0].shape[-2:]
    tile = tile if rows % tile == 0 else rows
    whole = lambda shape, index: pl.BlockSpec(
        shape, lambda i: index, pipeline_mode=pl.Buffered(buffer_count=1)
    )
    tiled = lambda lead: pl.BlockSpec(
        tuple(lead) + (tile, width), lambda i: (0,) * len(lead) + (i, 0)
    )
    in_specs = [tiled(array.shape[:-2]) for array in by_row]
    operands = list(by_row)
    products = 0
    for entry in fixed:
        array, first, blocks = entry if isinstance(entry, tuple) else (entry, 0, entry.shape[0])
        shape = (blocks,) + array.shape[1:]
        in_specs.append(whole(shape, (first // blocks,) + (0,) * (array.ndim - 1)))
        operands.append(array)
        if array.dtype == BF16:
            products += blocks
    in_specs += [pl.BlockSpec(memory_space=pl.ANY)] * len(ties)
    operands += list(ties)
    out_specs = [tiled(lead) for lead, _ in outs]
    out_shape = [jax.ShapeDtypeStruct(tuple(lead) + (rows, width), kind) for lead, kind in outs]
    if sums:
        out_specs.append(pl.BlockSpec((sums, width), lambda i: (0, 0)))
        out_shape.append(jax.ShapeDtypeStruct((sums, width), F32))
    moved = sum(array.size * array.dtype.itemsize for array in operands)
    moved += sum(leaf.size * leaf.dtype.itemsize for leaf in out_shape)
    return pl.pallas_call(
        kernel,
        grid=(rows // tile,),
        in_specs=in_specs,
        out_specs=out_specs,
        out_shape=out_shape,
        compiler_params=pltpu.CompilerParams(vmem_limit_bytes=VMEM_LIMIT),
        cost_estimate=pl.CostEstimate(
            flops=3 * rows * width * width * products // COST_SCALE,
            bytes_accessed=moved // COST_SCALE,
            transcendentals=0,
        ),
    )(*operands)


def row_major(values):
    return with_layout_constraint(values, Layout(major_to_minor=tuple(range(values.ndim))))


def swap(values, axis, offset):
    count = lax.axis_size(axis)
    return lax.ppermute(values, axis, [(index, index ^ offset) for index in range(count)])


def after(values, *earlier):
    return lax.optimization_barrier((values, *earlier))


def held(values, *earlier):
    if not earlier:
        return values
    wrong = jnp.zeros((), jnp.bool_)
    for array in earlier:
        entry = array[(0,) * array.ndim]
        wrong = wrong | (entry != entry)
    return jnp.where(wrong, jnp.zeros_like(values), values)


def pick(bit, on_zero, on_one):
    return jnp.where(bit == 0, on_zero, on_one)


def to_sequences(values, count, start=(), then=(), finish=()):
    seqs, local, width = values.shape
    own = lax.axis_index("ctx")
    parts = values.swapaxes(1, 2).reshape(count, seqs // count, width, local)
    mine = [lax.dynamic_index_in_dim(parts, own ^ i, keepdims=False) for i in range(count)]
    far = row_major(held(jnp.stack(mine[2:]), *start))
    far = row_major(swap(far, "ctx", 2))
    near = row_major(held(jnp.stack([mine[1], far[1]]), *then))
    near = row_major(swap(near, "ctx", 1))
    whole = row_major(jnp.stack([mine[0], near[0], far[0], near[1]]))
    return row_major(held(whole, *finish).swapaxes(2, 3))


def to_blocks(values, kind, *start):
    count, share, local, width = values.shape
    own = lax.axis_index("ctx")
    values = row_major(held(values.swapaxes(2, 3), *start))
    far = row_major(swap(row_major(values[2:]), "ctx", 2))
    near = row_major(swap(row_major(jnp.stack([values[1], far[1]])), "ctx", 1))
    out = row_major(jnp.zeros((count, share, width, local), kind))
    for offset, piece in enumerate([values[0], near[0], far[0], near[1]]):
        out = lax.dynamic_update_index_in_dim(out, piece.astype(kind), own ^ offset, 0)
    out = row_major(out).reshape(count * share, width, local).swapaxes(1, 2)
    return out, near


class Windows:
    def __init__(self, owned_rows):
        tiles = owned_rows // 16
        self.start = tiles // 2 * 16
        self.size = owned_rows - self.start
        ctx = lax.axis_index("ctx")
        self.core = ctx % 2
        self.y = ctx // 2
        self.x = lax.axis_index("replica")

    def rows(self, values):
        return pick(
            self.core, values[..., : self.size, :], values[..., self.start :, :]
        )

    def other_rows(self, values):
        return pick(
            self.core, values[..., self.start :, :], values[..., : self.size, :]
        )

    def block(self, blocks):
        return pick(
            self.x,
            pick(self.y, blocks[0], blocks[1]),
            pick(self.y, blocks[2], blocks[3]),
        )


def assemble_kernel(groups, start, size, transposed, here_ref, *refs):
    arrays, out_ref = refs[:-1], refs[-1]
    x, y, core = here_ref[0], here_ref[1], here_ref[2]
    for turn in range(2):
        row = pl.multiple_of((core ^ turn) * start, 16)
        for (places, first), ref in zip(groups, arrays[turn * len(groups) :]):
            for i, (dx, dy) in enumerate(places):
                block = 2 * (x ^ dx) + (y ^ dy)
                for s in range(ref.shape[1]):
                    place = (first + s, block) if transposed else (block, first + s)
                    out_ref[place + (pl.ds(row, size), slice(None))] = ref[
                        i, s, :size, :
                    ].astype(out_ref.dtype)


def assemble(win, groups, own, other, owned_rows, shards, transposed, kind):
    width = own[0].shape[-1]
    here = jnp.stack([win.x, win.y, win.core]).astype(jnp.int32)
    shape = (shards, 4, owned_rows, width) if transposed else (4, shards, owned_rows, width)
    return pl.pallas_call(
        functools.partial(assemble_kernel, groups, win.start, win.size, transposed),
        in_specs=[pl.BlockSpec(memory_space=pltpu.SMEM)]
        + [pl.BlockSpec(memory_space=pltpu.VMEM)] * (2 * len(groups)),
        out_specs=pl.BlockSpec(memory_space=pltpu.VMEM),
        out_shape=jax.ShapeDtypeStruct(shape, kind),
        compiler_params=pltpu.CompilerParams(vmem_limit_bytes=VMEM_LIMIT),
        cost_estimate=pl.CostEstimate(
            flops=0, bytes_accessed=16 * shards * owned_rows * width, transcendentals=0
        ),
    )(here, *own, *other)


def spread_chips(mine, hold=()):
    shards = mine.shape[0]
    if shards == 1:
        first = jnp.stack([mine, swap(mine, "replica", 1)])
        return [first, swap(first, "ctx", 2)]
    split = shards // 2
    low, high = mine[:split], mine[split:]
    low_there, high_there = after(swap(low, "replica", 1), swap(high, "ctx", 2))
    first = held(jnp.stack([low, low_there]), *hold)
    second = held(jnp.stack([high, high_there]), *hold)
    third, fourth = after(swap(first, "ctx", 2), swap(second, "replica", 1))
    return [first, second, third, fourth]


def chip_groups(shards):
    if shards == 1:
        return ((((0, 0), (1, 0)), 0), (((0, 1), (1, 1)), 0))
    return (
        (((0, 0), (1, 0)), 0),
        (((0, 0), (0, 1)), shards // 2),
        (((0, 1), (1, 1)), 0),
        (((1, 0), (1, 1)), shards // 2),
    )


def spread_cores(own):
    return [swap(array, "ctx", 1) for array in own]


def place(win, own, other, owned_rows, shards, transposed=False, kind=BF16):
    return assemble(win, chip_groups(shards), own, other, owned_rows, shards, transposed, kind)


def grads_kernel(groups, start, size, forms, here_ref, *refs):
    total = sum(len(form) for form in forms)
    arrays, outs = refs[:-total], refs[-total:]
    x, y, core = here_ref[0], here_ref[1], here_ref[2]

    def put(form, targets, block, row, values):
        width = values.shape[-1]
        if form == (0,):
            owned = targets[0].shape[0] // 4
            at = pl.multiple_of(block * owned + row, 16)
            targets[0][pl.ds(at, size), :] = values
            return
        first = 0
        for wide, ref in zip(form, targets):
            for i in range(wide):

                @pl.when(block == first + i)
                def _():
                    ref[pl.ds(row, size), i * width : (i + 1) * width] = values

            first += wide

    for turn in range(2):
        row = pl.multiple_of((core ^ turn) * start, 16)
        for (places, first), ref in zip(groups, arrays[turn * len(groups) :]):
            for i, (dx, dy) in enumerate(places):
                block = 2 * (x ^ dx) + (y ^ dy)
                for s in range(ref.shape[1]):
                    before = sum(len(form) for form in forms[: first + s])
                    targets = outs[before : before + len(forms[first + s])]
                    put(forms[first + s], targets, block, row, ref[i, s].astype(F32))


def place_grads(win, own, other, owned_rows, forms):
    width = own[0].shape[-1]
    here = jnp.stack([win.x, win.y, win.core]).astype(jnp.int32)
    shapes = [
        (owned_rows, wide * width) if wide else (4 * owned_rows, width)
        for form in forms
        for wide in form
    ]
    groups = chip_groups(len(forms))
    return pl.pallas_call(
        functools.partial(grads_kernel, groups, win.start, win.size, forms),
        in_specs=[pl.BlockSpec(memory_space=pltpu.SMEM)]
        + [pl.BlockSpec(memory_space=pltpu.VMEM)] * (2 * len(groups)),
        out_specs=[pl.BlockSpec(memory_space=pltpu.VMEM)] * len(shapes),
        out_shape=[jax.ShapeDtypeStruct(shape, F32) for shape in shapes],
        compiler_params=pltpu.CompilerParams(vmem_limit_bytes=VMEM_LIMIT),
        cost_estimate=pl.CostEstimate(
            flops=0, bytes_accessed=4 * owned_rows * width * len(forms), transcendentals=0
        ),
    )(here, *own, *other)


def add_pair(kept, received):
    return (kept.astype(F32) + received.astype(F32)).astype(BF16)


def corner(values):
    return values[(0,) * (values.ndim - 2)][:16, :LANES]


def reduce_first(win, grads, transposed):
    shards = grads.shape[0 if transposed else 1]
    split = shards // 2

    def part(values, blocks, which):
        return values[which, blocks] if transposed else values[blocks, which]

    lower, upper = slice(None, split), slice(split, None)
    entry = lambda values, i: values[:, i] if transposed else values[i]
    received = swap(win.other_rows(grads), "ctx", 1)
    both = add_pair(win.rows(grads), received)
    by_x = [part(both, slice(2 * i, 2 * i + 2), lower) for i in range(2)]
    by_y = [part(both, slice(i, None, 2), upper) for i in range(2)]
    x_sent = row_major(pick(win.x, by_x[1], by_x[0]))
    y_sent = row_major(pick(win.y, by_y[1], by_y[0]))
    x_received, y_received = after(
        row_major(swap(x_sent, "replica", 1)), row_major(swap(y_sent, "ctx", 2))
    )
    low = row_major(add_pair(pick(win.x, *by_x), x_received))
    high = row_major(add_pair(pick(win.y, *by_y), y_received))
    low, high = [entry(low, i) for i in range(2)], [entry(high, i) for i in range(2)]
    return (low, high), [corner(x_sent), corner(y_sent)]


def reduce_second(win, halves, *earlier):
    low, high = halves
    low_sent, high_sent = pick(win.y, low[1], low[0]), pick(win.x, high[1], high[0])
    if earlier:
        low_sent, high_sent = held(low_sent, *earlier), held(high_sent, *earlier)
    low_received, high_received = after(
        swap(low_sent, "ctx", 2), swap(high_sent, "replica", 1)
    )
    low_sum = add_pair(pick(win.y, *low), low_received)
    high_sum = add_pair(pick(win.x, *high), high_received)
    sums = jnp.concatenate([low_sum, high_sum], axis=0)
    return sums, [corner(low_sent)], [corner(sums)]


def reduce_vectors(values):
    values = add_pair(values, swap(values, "ctx", 1))
    values = add_pair(values, swap(values, "replica", 1))
    step = 1
    while step < lax.axis_size("shard"):
        values = add_pair(values, swap(values, "shard", step))
        step *= 2
    return values


def per_device(
    tokens,
    cotangent,
    block_order,
    ln1_gain,
    ln1_bias,
    qkv_weight,
    q_bias,
    v_bias,
    out_weight,
    out_bias,
    ln2_gain,
    ln2_bias,
    fc_weight,
    fc_bias,
    proj_weight,
    proj_bias,
):
    seq_count, local_len, width = tokens.shape
    owned_rows = ln1_gain.shape[0]
    shards = width // owned_rows
    wide = fc_weight.shape[1] // width
    count = lax.axis_size("ctx")
    rows = seq_count * local_len
    pairwise = lax.axis_size("replica") == 2 and count == 4 and shards == 4
    win = Windows(owned_rows)

    vectors = jnp.concatenate(
        [ln1_gain, ln1_bias, q_bias, v_bias, out_bias, ln2_gain, ln2_bias, proj_bias, fc_bias]
    )
    vector_rows = vectors.shape[0] // width
    vector_tile = jnp.pad(vectors.reshape(vector_rows, width), ((0, -vector_rows % 16), (0, 0)))
    column = lambda values, i: values[:, i * width : (i + 1) * width]
    blocks_a = [column(qkv_weight, i) for i in range(3)] + [out_weight]
    blocks_b = [column(fc_weight, i) for i in range(wide)]
    blocks_c = [proj_weight[i * owned_rows : (i + 1) * owned_rows] for i in range(wide)]

    def gather_z(values):
        return lax.all_gather(values, "shard", axis=0, tiled=False)

    low_inputs = to_sequences(tokens, count).reshape(rows, width)

    if pairwise:
        mine = [win.rows(win.block(blocks)) for blocks in (blocks_a, blocks_b, blocks_c)]
        part_a = gather_z(mine[0])
        mine_b, part_a = after(jnp.concatenate([mine[1], vector_tile], axis=0), part_a)
        part_b = gather_z(mine_b)
        mine_c, part_b = after(mine[2], part_b)
        part_c = gather_z(mine_c)
        part_a, low_inputs = after(part_a, low_inputs)
        own_a = spread_chips(part_a)
        other_a = spread_cores(own_a)
        full_a = place(win, own_a, other_a, owned_rows, shards)
        vector_part = part_b[:, win.size : win.size + vector_rows]
        own_b = spread_chips(held(part_b[:, : win.size], own_a[2]))
    else:
        vector_part = gather_z(vector_tile)[:, :vector_rows]
        full_a, full_b, full_c = [
            gather_z(jnp.stack(blocks)) for blocks in (blocks_a, blocks_b, blocks_c)
        ]
        full_a, full_b = full_a.transpose(1, 0, 2, 3), full_b.transpose(1, 0, 2, 3)
    w_a = full_a.reshape(4, width, width)
    vector_part = vector_part.reshape(shards, vector_rows * width).astype(F32)
    small = vector_part[:, : 8 * owned_rows].reshape(shards, 8, owned_rows)
    small = small.transpose(1, 0, 2).reshape(8, width)
    bias_fc = vector_part[:, 8 * owned_rows :].reshape(wide, 1, width)

    share = seq_count // count
    blocked = (count, share, local_len, width)
    index = jnp.arange(count, dtype=jnp.int32)
    held_by = jnp.sum(jnp.where(block_order[None, :] == index[:, None], index[None, :], 0), axis=1)
    order = (held_by ^ lax.axis_index("ctx")).astype(jnp.int32)

    steps = [corner(own_b[0][1]), corner(own_b[1][1])] if pairwise else []
    joined, low_one = by_rows(
        qkv_kernel, [low_inputs], [(w_a, 0, 3), small], [((3,), BF16), ((), BF16)], ties=steps
    )
    joined = joined.reshape((3,) + blocked)
    middle_seq = share // 2
    begun = attention_forward(joined, order, 0, middle_seq)
    if pairwise:
        other_b = spread_cores(own_b)
        full_b = place(win, own_b, other_b, owned_rows, shards)
        own_c = spread_chips(held(part_c, own_b[2], joined), hold=[begun[0]])
        steps = [corner(own_c[0][1]), corner(own_c[1][1]), corner(own_c[2]), corner(own_c[3])]
    else:
        steps = [corner(joined[0, 0])] * 4
    mixed, lse = attention_forward(joined, order, middle_seq, share, begun, steps[:2])
    attended = mixed.reshape(rows, width)
    middle, low_two = by_rows(
        attended_kernel,
        [low_inputs, attended],
        [(w_a, 3, 1), small],
        [((), F32), ((), BF16)],
    )
    w_fc = full_b.reshape(wide, width, width)
    low_act, slope = by_rows(
        hidden_kernel,
        [low_two],
        [w_fc, bias_fc],
        [((wide,), BF16), ((wide,), BF16)],
        ties=steps[2:],
    )
    if pairwise:
        full_c = place(win, own_c, spread_cores(own_c), owned_rows, shards, transposed=True)
    w_proj = full_c.reshape(wide, width, width)
    holds = ((own_c[2], low_two), (low_act,), (full_c,)) if pairwise else ((), (), ())
    low_grad_out = to_sequences(cotangent, count, *holds).reshape(rows, width)

    def finish_units(groups, forms, *earlier):
        sums = [
            lax.psum_scatter(group, "shard", scatter_dimension=0, tiled=False)
            for group in groups
        ]
        own = spread_chips(held(jnp.stack(sums), *earlier))
        return place_grads(win, own, spread_cores(own), owned_rows, forms)

    def reduce_whole(grads, transposed=False):
        if transposed:
            grads = grads.transpose(1, 0, 2, 3)
        full = lax.psum_scatter(grads, "shard", scatter_dimension=1, tiled=False)
        return lax.psum(full, ("replica", "ctx")).astype(F32)

    def start_units(grads, transposed=False):
        if not pairwise:
            return grads, ((), (), ())
        halves, first = reduce_first(win, grads, transposed)
        sums, second, last = reduce_second(win, halves)
        return sums, (first, second, last)

    def by_shard(grads):
        return grads.astype(BF16).reshape(4, shards, owned_rows, width)

    grad_proj = jnp.einsum("ctx,td->cxd", low_act, low_grad_out, preferred_element_type=F32)
    grad_proj = grad_proj.astype(BF16)
    partial_proj, proj_marks = start_units(by_shard(grad_proj), transposed=True)
    (outputs,) = by_rows(
        output_kernel,
        [middle, low_act],
        [w_proj, small],
        [((), BF16)],
        ties=[corner(grad_proj)],
    )
    grad_hidden, sums_hidden = by_rows(
        hidden_back_kernel,
        [low_grad_out, slope],
        [w_proj],
        [((wide,), BF16)],
        sums=8,
        ties=[corner(outputs), *proj_marks[0]],
    )
    grad_fc = jnp.einsum("td,ctx->cdx", low_two, grad_hidden, preferred_element_type=F32)
    grad_fc = grad_fc.astype(BF16)
    partial_fc, fc_marks = start_units(by_shard(grad_fc))
    layer_out, returned = to_blocks(outputs.reshape(blocked), BF16, *proj_marks[1])
    grad_middle, low_grad_middle, grad_mixed, sums_middle = by_rows(
        middle_back_kernel,
        [grad_hidden, low_grad_out, middle],
        [w_fc, (w_a, 3, 1), small],
        [((), F32), ((), BF16), ((), BF16)],
        sums=8,
        ties=[corner(grad_fc), *proj_marks[1]],
    )
    grad_out_weight = dot_tn(attended, low_grad_middle).astype(BF16)
    grad_joined = attention_backward(
        joined,
        mixed,
        grad_mixed.reshape(blocked),
        lse,
        order,
        ties=[corner(grad_out_weight), corner(returned), *proj_marks[2], *fc_marks[0]],
    ).reshape(3, rows, width)
    grad_qkv = jnp.einsum("td,ctx->cdx", low_one, grad_joined, preferred_element_type=F32)
    grad_qkv = grad_qkv.astype(BF16)
    grads_a = jnp.concatenate([grad_qkv, grad_out_weight[None]], axis=0)
    partial_a, mark = by_shard(grads_a), ()
    if pairwise:
        halves, mark = reduce_first(win, partial_a, False)
    grad_inputs, sums_input = by_rows(
        input_back_kernel,
        [grad_joined, grad_middle, low_inputs],
        [(w_a, 0, 3), small],
        [((), BF16)],
        sums=8,
        ties=[*mark, *fc_marks[2]],
    )
    if pairwise:
        partial_a, _, _ = reduce_second(win, halves, grad_inputs)
    small_grads = sums_middle + sums_input
    grad_fc_bias = sums_hidden[:wide]
    vector_grads = jnp.concatenate(
        [
            small_grads.reshape(8, shards, owned_rows)
            .transpose(1, 0, 2)
            .reshape(shards, 8 * owned_rows),
            grad_fc_bias.reshape(shards, owned_rows * wide),
        ],
        axis=1,
    ).astype(BF16)
    vector_grads = jnp.pad(
        vector_grads.reshape(shards, vector_rows, width),
        ((0, 0), (0, -vector_rows % 16), (0, 0)),
    )
    blocked_grads = grad_inputs.reshape(blocked)
    if pairwise:
        vector_grads = held(vector_grads, partial_a)
        vector_grads = add_pair(vector_grads, swap(vector_grads, "ctx", 2))
        qkv_grad, out_grad = finish_units([partial_a], ((3, 1),))
        proj_grad, fc_grad = finish_units(
            [partial_proj, partial_fc], ((0,), (wide,)), vector_grads
        )
        input_grad, _ = to_blocks(blocked_grads, F32, vector_grads)
        owned_vectors = lax.dynamic_index_in_dim(
            reduce_vectors(vector_grads), lax.axis_index("shard"), keepdims=False
        )
    else:
        input_grad, _ = to_blocks(blocked_grads, F32)
        owned_proj = reduce_whole(partial_proj, transposed=True)
        owned_a, owned_fc = reduce_whole(partial_a), reduce_whole(partial_fc)
        owned_vectors = lax.psum_scatter(
            vector_grads, "shard", scatter_dimension=0, tiled=False
        )
        owned_vectors = lax.psum(owned_vectors, ("replica", "ctx"))
        side_by_side = lambda blocks: jnp.concatenate(list(blocks), axis=1)
        qkv_grad, out_grad = side_by_side(owned_a[:3]), owned_a[3]
        fc_grad = side_by_side(owned_fc)
        proj_grad = owned_proj.reshape(wide * owned_rows, width)
    owned_vectors = owned_vectors[:vector_rows].reshape(-1).astype(F32)
    vec = [owned_vectors[i * owned_rows : (i + 1) * owned_rows] for i in range(8)]
    return (
        layer_out,
        input_grad,
        vec[0],
        vec[1],
        qkv_grad,
        vec[2],
        vec[3],
        out_grad,
        vec[4],
        vec[5],
        vec[6],
        fc_grad,
        owned_vectors[8 * owned_rows :],
        proj_grad,
        vec[7],
    )


def solution(mesh):
    vector, matrix = P("shard"), P("shard", None)
    rows = P(("shard", "replica"), "ctx", None)
    weights = (
        vector,
        vector,
        matrix,
        vector,
        vector,
        matrix,
        vector,
        vector,
        vector,
        matrix,
        vector,
        matrix,
        vector,
    )
    return jax.shard_map(
        per_device,
        mesh=mesh,
        in_specs=(rows, rows, P()) + weights,
        out_specs=(rows, rows) + weights,
        check_vma=False,
    )
```
